128 devices in a mesh: shard: 8 (over x_hi, z), rep: 16 (over x_lo, y, core).
Axes of the slice: x: 4 (x_hi: 2, x_lo: 2; x = x_hi * 2 + x_lo), y: 4, z: 4, core: 2. Of those that a mesh axis runs over, the one named last changes fastest.
Arguments:
- inputs: bfloat16 [16, 1024, 2048], P('rep', 'shard'), may hold values from -6 to 6
- cotangent: bfloat16 [16, 1024, 2048], P('rep', 'shard'), may hold values from -6 to 6
- ln1_gain: bfloat16 [2048], P('shard'), may hold values from 0.25 to 1.75
- ln1_bias: bfloat16 [2048], P('shard'), may hold values from -1.75 to 1.75
- qkv_weight: bfloat16 [2048, 6144], P('shard'), may hold values from -0.125 to 0.125
- qkv_bias: bfloat16 [6144], P('shard'), may hold values from -1.75 to 1.75
- out_weight: bfloat16 [2048, 2048], P('shard'), may hold values from -3 to 3
- ln2_gain: bfloat16 [2048], P('shard'), may hold values from 0.25 to 1.75
- ln2_bias: bfloat16 [2048], P('shard'), may hold values from -1.75 to 1.75
- gate_weight: bfloat16 [2048, 5632], P('shard'), may hold values from -0.125 to 0.125
- up_weight: bfloat16 [2048, 5632], P('shard'), may hold values from -0.125 to 0.125
- down_weight: bfloat16 [5632, 2048], P('shard'), may hold values from -0.078125 to 0.078125
Outputs:
- activations: bfloat16 [16, 1024, 2048], P('rep', 'shard')
- input_grad: float32 [16, 1024, 2048], P('rep', 'shard')
- ln1_gain_grad: float32 [2048], P('shard')
- ln1_bias_grad: float32 [2048], P('shard')
- qkv_weight_grad: float32 [2048, 6144], P('shard')
- qkv_bias_grad: float32 [6144], P('shard')
- out_weight_grad: float32 [2048, 2048], P('shard')
- ln2_gain_grad: float32 [2048], P('shard')
- ln2_bias_grad: float32 [2048], P('shard')
- gate_weight_grad: float32 [2048, 5632], P('shard')
- up_weight_grad: float32 [2048, 5632], P('shard')
- down_weight_grad: float32 [5632, 2048], P('shard')
The draws below stay inside these ranges and needn't reach their ends.
All inputs are finite; a program needn't handle non-finite values.
Results may differ from the reference program's by a relative error of at most 0.025.
Values may be sent and summed in bfloat16 or wider, within the bound.
A program may use at most 384 MiB of HBM per device.

```python
import jax
import jax.numpy as jnp
from jax import lax

D = 2048
HEADS = 32
HEAD_DIM = 64
FF = 5632
ROT = 16
SEQ = 1024
SEQS = 16


def shard_levels(stream_key, extent, cuts, low, high):
    def one(dim, shards_of):
        draws = jax.random.uniform(jax.random.fold_in(jax.random.fold_in(stream_key, 6), dim), (shards_of,), jnp.float32, low / len(cuts), high / len(cuts))
        return jnp.repeat(jnp.exp(draws), extent[dim] // shards_of).reshape((-1,) + (1,) * (len(extent) - dim - 1))

    factor_of = one(*cuts[0])
    for cut in cuts[1:]:
        factor_of = factor_of * one(*cut)
    return factor_of


def bell_draw(rng, extent, deviation, most, split=(), kind=jnp.bfloat16):
    factor_of = shard_levels(rng, extent, split, -0.22, 0.18) if split else 1.0
    values = jax.random.normal(rng, extent, jnp.float32) * deviation * factor_of
    return jnp.minimum(jnp.maximum(values, -most), most).astype(kind)


def setup_inputs(seed: int = 0) -> dict:
    streams_of = jax.random.split(jax.random.key(seed), 13)
    inputs = bell_draw(streams_of[0], (SEQS, SEQ, D), 1.0, 6.0, ((0, 16), (1, 8)))
    cotangent = bell_draw(streams_of[1], (SEQS, SEQ, D), 1.0, 6.0, ((0, 16), (1, 8)))
    ln1_gain = jnp.clip(1.0 + 0.15 * jax.random.normal(streams_of[2], (D,), jnp.float32), 0.25, 1.75).astype(jnp.bfloat16)
    ln1_bias = bell_draw(streams_of[3], (D,), 0.3, 1.75, ((0, 8),))
    qkv_weight = bell_draw(streams_of[4], (D, 3 * D), D ** -0.5, 0.125, ((0, 8),))
    qkv_bias = bell_draw(streams_of[5], (3 * D,), 0.3, 1.75, ((0, 8),))
    out_weight = bell_draw(streams_of[6], (D, D), (2 * D // SEQ) ** -0.5, 3.0, ((0, 8),))
    ln2_gain = jnp.clip(1.0 + 0.15 * jax.random.normal(streams_of[7], (D,), jnp.float32), 0.25, 1.75).astype(jnp.bfloat16)
    ln2_bias = bell_draw(streams_of[8], (D,), 0.3, 1.75, ((0, 8),))
    gate_weight = bell_draw(streams_of[9], (D, FF), D ** -0.5, 0.125, ((0, 8),))
    up_weight = bell_draw(streams_of[10], (D, FF), D ** -0.5, 0.125, ((0, 8),))
    down_weight = bell_draw(streams_of[11], (FF, D), FF ** -0.5, 0.078125, ((0, 8),))
    return dict(inputs=inputs, cotangent=cotangent, ln1_gain=ln1_gain, ln1_bias=ln1_bias, qkv_weight=qkv_weight, qkv_bias=qkv_bias, out_weight=out_weight, ln2_gain=ln2_gain, ln2_bias=ln2_bias, gate_weight=gate_weight, up_weight=up_weight, down_weight=down_weight)


EPS = 1e-05
BASE = 10000.0

@jax.custom_vjp
def low(v):
    return lax.optimization_barrier(v.astype(jnp.bfloat16)).astype(jnp.float32)

@jax.custom_vjp
def low_back(v):
    return v

def low_keep(v):
    return (low(v), None)

def low_pass(kept, grad):
    return (grad,)

def back_keep(v):
    return (v, None)

def back_low(kept, grad):
    return (low(grad),)
low.defvjp(low_keep, low_pass)
low_back.defvjp(back_keep, back_low)

def matmul(left, right):
    return jnp.dot(left, right, precision=lax.Precision.HIGHEST)

def normalize(values, gain, shift):
    center = values - lax.optimization_barrier(jnp.mean(values, -1, keepdims=True))
    inverse = lax.rsqrt(lax.optimization_barrier(jnp.mean(center * center, -1, keepdims=True)) + EPS)
    return center * inverse * gain + shift

def turn(values, cosine, sine):
    half = ROT // 2
    part = values[..., :ROT]
    swapped = jnp.concatenate([-part[..., half:], part[..., :half]], -1)
    return jnp.concatenate([part * cosine + swapped * sine, values[..., ROT:]], -1)

def layer(resid_in, params):
    gain_one, shift_one, w_qkv, bias_qkv, w_out, gain_two, shift_two, w_gate, w_up, w_down = params
    positions = jnp.arange(SEQ).astype(jnp.float32)
    freqs = BASE ** (-jnp.arange(0, ROT, 2).astype(jnp.float32) / ROT)
    angles = positions[:, None] * freqs[None, :]
    angles = jnp.concatenate([angles, angles], -1)[:, None, :]
    cosine = jnp.cos(angles)
    sine = jnp.sin(angles)
    input_one = low(normalize(resid_in, gain_one, shift_one))
    projected = low_back(matmul(input_one, w_qkv) + bias_qkv)
    query = low(turn(projected[:, :D].reshape(SEQ, HEADS, HEAD_DIM), cosine, sine))
    key_all = low(turn(projected[:, D:2 * D].reshape(SEQ, HEADS, HEAD_DIM), cosine, sine))
    value_all = low(projected[:, 2 * D:].reshape(SEQ, HEADS, HEAD_DIM))
    scores = low_back(jnp.einsum('qhd,khd->hqk', query, key_all, precision=lax.Precision.HIGHEST) * HEAD_DIM ** (-0.5))
    allowed = jnp.arange(SEQ)[None, :] <= jnp.arange(SEQ)[:, None]
    scores = jnp.where(allowed, scores, -1e+30)
    top = lax.optimization_barrier(jnp.max(scores, -1, keepdims=True))
    expo = jnp.where(allowed, jnp.exp(scores - top), 0.0)
    probs = low(expo / lax.optimization_barrier(jnp.sum(expo, -1, keepdims=True)))
    mixed = jnp.einsum('hqk,khd->qhd', probs, value_all, precision=lax.Precision.HIGHEST)
    attended = low(low_back(mixed.reshape(SEQ, D)))
    resid_mid = resid_in + low_back(matmul(attended, w_out))
    input_two = low(normalize(resid_mid, gain_two, shift_two))
    gate_pre = low_back(matmul(input_two, w_gate))
    up_pre = low_back(matmul(input_two, w_up))
    hidden = low(jax.nn.silu(gate_pre) * up_pre)
    return resid_mid + low_back(matmul(hidden, w_down))

def reference(inputs, cotangent, ln1_gain, ln1_bias, qkv_weight, qkv_bias, out_weight, ln2_gain, ln2_bias, gate_weight, up_weight, down_weight):
    params = tuple((w.astype(jnp.float32) for w in (ln1_gain, ln1_bias, qkv_weight, qkv_bias, out_weight, ln2_gain, ln2_bias, gate_weight, up_weight, down_weight)))

    def one_seq(carry, pair):
        seq_in, seq_cot = pair
        result, pull = jax.vjp(layer, seq_in.astype(jnp.float32), params)
        grad_in, grad_params = pull(seq_cot.astype(jnp.float32))
        carry = tuple((c + g for c, g in zip(carry, grad_params)))
        return (carry, (result.astype(jnp.bfloat16), grad_in))
    zeros = tuple((jnp.zeros_like(p) for p in params))
    sums, outputs = lax.scan(one_seq, zeros, (inputs, cotangent))
    activations, input_grad = outputs
    return (activations, input_grad, sums[0], sums[1], sums[2], sums[3], sums[4], sums[5], sums[6], sums[7], sums[8], sums[9])
```

```python
import functools

import jax
import jax.numpy as jnp
import numpy as np
from jax import lax
from jax.experimental import pallas as pl
from jax.experimental.pallas import tpu as pltpu
from jax.sharding import PartitionSpec as P

HEADS = 32
HEAD_DIM = 64
ROT = 16
WIDTH = 2048
GROUP = 8
REPS = 16
ROWS = 128
TOTAL = GROUP * ROWS
LOCAL = WIDTH // GROUP
LOCAL_HEADS = HEADS // GROUP
FF = 5632
LOCAL_FF = FF // GROUP
HID = 768
SLAB = LOCAL // REPS
CHUNK = 256
CHUNKS = TOTAL // CHUNK
EPS = 1e-05
BASE = 10000.0
BF = jnp.bfloat16
F32 = jnp.float32
MESH = pl.DeviceIdType.MESH
VM = pl.BlockSpec(memory_space=pltpu.VMEM)
ANY = pl.BlockSpec(memory_space=pl.ANY)
DMA = pltpu.SemaphoreType.DMA


def dot(left, right):
    return jnp.dot(left, right, preferred_element_type=F32)


def dot_nt(left, right):
    return lax.dot_general(left, right, (((1,), (1,)), ((), ())), preferred_element_type=F32)


FAR, UP, DOWN = (1, 0, 0, 0, 0), (0, 1, 0, 0, 0), (0, -1, 0, 0, 0)
NEAR, NORTH, SOUTH, TWIN = (0, 0, 1, 0, 0), (0, 0, 0, 1, 0), (0, 0, 0, -1, 0), (0, 0, 0, 0, 1)
HERE = (0, 0, 0, 0, 0)
SIZES = (2, 4, 2, 4, 2)
PEERS = tuple((f, z, 0, 0, 0) for f in range(2) for z in range(4) if (f, z) != (0, 0))


def place():
    shard, rep = lax.axis_index("shard"), lax.axis_index("rep")
    return (shard // 4, lax.rem(shard, 4), rep // 8, lax.rem(rep // 2, 4), lax.rem(rep, 2))


def shift(where, offset):
    return tuple(
        lax.rem(a + (o + 2 * n) % n, n) if o % n else a for a, o, n in zip(where, offset, SIZES)
    )


def shard_at(where, offset=HERE):
    far, level = shift(where, offset)[:2]
    return far * 4 + level


def rep_at(where, offset=HERE):
    near, north, core = shift(where, offset)[2:]
    return near * 8 + north * 2 + core


def device(where, offset):
    return (shard_at(where, offset), rep_at(where, offset))


def less(a, b):
    return tuple((p - q) % n for p, q, n in zip(a, b, SIZES))


def negative(a):
    return tuple(-p for p in a)


def greet(where, offsets):
    barrier = pltpu.get_barrier_semaphore()
    for offset in offsets:
        pl.semaphore_signal(
            barrier, inc=1, device_id=device(where, negative(offset)), device_id_type=MESH
        )
    pl.semaphore_wait(barrier, len(offsets))


def remote(src, dst, sends, recvs, i, to):
    return pltpu.make_async_remote_copy(
        src_ref=src,
        dst_ref=dst,
        send_sem=sends.at[i],
        recv_sem=recvs.at[i],
        device_id=to,
        device_id_type=MESH,
    )


def token_moves():
    moves = []

    def add(owner, part, step, first, turn):
        moves.append((owner, part, step, first, turn))
        return len(moves) - 1

    near, far = (0, WIDTH // 2), (WIDTH // 2, WIDTH // 2)
    whole, top, low = (0, ROWS), (0, ROWS // 2), (ROWS // 2, ROWS // 2)
    up2 = (0, 2, 0, 0, 0)
    up = add(HERE, (whole, near), UP, None, 0)
    down = add(HERE, (whole, near), DOWN, None, 0)
    add(HERE, (whole, near), FAR, None, 0.2)
    a = add(DOWN, (top, near), UP, up, 1)
    b = add(UP, (low, near), DOWN, down, 1)
    add(DOWN, (whole, near), FAR, up, 1.1)
    add(UP, (whole, near), FAR, down, 1.1)
    add(up2, (top, near), FAR, a, 2)
    add(up2, (low, near), FAR, b, 2)
    over = add(HERE, (whole, far), FAR, None, 1)
    up = add(HERE, (whole, far), UP, None, 1.1)
    down = add(HERE, (whole, far), DOWN, None, 1.1)
    add(DOWN, (top, far), UP, up, 3)
    add(UP, (low, far), DOWN, down, 3)
    up = add(FAR, (whole, far), UP, over, 2.5)
    down = add(FAR, (whole, far), DOWN, over, 2.5)
    add(tuple(p + q for p, q in zip(FAR, DOWN)), (top, far), UP, up, 4)
    add(tuple(p + q for p, q in zip(FAR, UP)), (low, far), DOWN, down, 4)
    return tuple(moves)


MOVES = token_moves()
COUNT = len(MOVES)
TURNS = tuple(sorted(range(COUNT), key=lambda i: MOVES[i][4]))
FED = tuple(tuple(j for j in range(COUNT) if MOVES[j][3] == i) for i in range(COUNT))
NEIGHBOURS = (FAR, UP, DOWN)
LANDS = {}
for _i in range(COUNT):
    LANDS[_i] = _i
LANDINGS = COUNT


def token_part(ref, block, part):
    (row, rows), (col, cols) = part
    return ref.at[block, pl.ds(row, rows), pl.ds(col, cols)]


class Gather:
    def __init__(self, where, ref, sends, recvs):
        self.where, self.ref, self.sends, self.recvs = where, ref, sends, recvs
        self.got = set()

    def move(self, i, arriving=False):
        owner, part, step, _, _ = MOVES[i]
        block = shard_at(self.where, less(owner, step) if arriving else owner)
        ref = token_part(self.ref, block, part)
        return remote(ref, ref, self.sends, self.recvs, i, device(self.where, step))

    def take(self, i):
        if i not in self.got:
            self.got.add(i)
            self.move(i, True).wait_recv()

    def turn(self, i):
        if MOVES[i][3] is not None:
            self.take(MOVES[i][3])
        self.move(i).start()

    def finish(self):
        for i in TURNS:
            self.take(i)
        for i in TURNS:
            self.move(i).wait_send()

    def run(self):
        for i in TURNS:
            self.turn(i)
        self.finish()


class Scatter:
    def __init__(self, where, buf, land, sends, recvs):
        self.where, self.buf, self.land, self.sends, self.recvs = where, buf, land, sends, recvs
        self.got = set()

    def move(self, i, arriving=False):
        owner, part, step, _, _ = MOVES[i]
        block = shard_at(self.where, owner if arriving else less(owner, step))
        (row, rows), (col, cols) = part
        return remote(
            token_part(self.buf, block, part),
            self.land.at[LANDS[i], pl.ds(row, rows)],
            self.sends,
            self.recvs,
            i,
            device(self.where, negative(step)),
        )

    def take(self, i):
        if i in self.got:
            return
        self.got.add(i)
        owner, ((row, rows), (col, cols)), _, _, _ = MOVES[i]
        self.move(i, True).wait_recv()
        at = (shard_at(self.where, owner), pl.ds(row, rows), pl.ds(col, cols))
        total = self.buf[at].astype(F32) + self.land[LANDS[i], pl.ds(row, rows)].astype(F32)
        self.buf[at] = total.astype(BF)

    def turn(self, i):
        for j in FED[i]:
            self.take(j)
        self.move(i).start()

    def finish(self):
        for i in reversed(TURNS):
            self.take(i)
        for i in reversed(TURNS):
            self.move(i).wait_send()

    def run(self):
        for i in reversed(TURNS):
            self.turn(i)
        self.finish()


def slab_moves():
    moves = []

    def add(owner, part, step, first, turn):
        moves.append((owner, part, step, first, turn))
        return len(moves) - 1

    whole, half, rest = (0, GROUP), (0, GROUP // 2), (GROUP // 2, GROUP // 2)
    near = add(HERE, whole, NEAR, None, 0)
    for base, first, turn in ((HERE, None, 0), (NEAR, near, 1)):
        def at(*steps):
            return tuple(sum(p) for p in zip(base, *steps))

        up = add(base, whole, NORTH, first, turn)
        down = add(base, whole, SOUTH, first, turn)
        add(base, whole, TWIN, first, turn + 0.1)
        a = add(at(SOUTH), half, NORTH, up, turn + 2)
        b = add(at(NORTH), rest, SOUTH, down, turn + 2)
        add(at(SOUTH), whole, TWIN, up, turn + 2.1)
        add(at(NORTH), whole, TWIN, down, turn + 2.1)
        add(at(NORTH, NORTH), half, TWIN, a, turn + 4)
        add(at(NORTH, NORTH), rest, TWIN, b, turn + 4)
    return tuple(moves)


SLABS = slab_moves()
SLAB_COUNT = len(SLABS)
SLAB_TURNS = tuple(sorted(range(SLAB_COUNT), key=lambda i: SLABS[i][4]))
SLAB_FED = tuple(tuple(j for j in range(SLAB_COUNT) if SLABS[j][3] == i) for i in range(SLAB_COUNT))
SLAB_LANDS = {}
for _i in range(SLAB_COUNT):
    if SLABS[_i][1][0] == 0:
        SLAB_LANDS[_i] = len(set(SLAB_LANDS.values()))
    else:
        SLAB_LANDS[_i] = SLAB_LANDS[_i - 1] if SLABS[_i - 1][1][1] < GROUP else None
SLAB_LANDINGS = len(set(SLAB_LANDS.values()))
REP_NEIGHBOURS = (NEAR, NORTH, SOUTH, TWIN)


class Spread:
    def __init__(self, where, cuts, ref, own_sem, first_sends, first_recvs, sends, recvs):
        self.where, self.cuts, self.ref, self.own_sem = where, cuts, ref, own_sem
        self.first_sends, self.first_recvs = first_sends, first_recvs
        self.slabs = SlabGather(where, ref, sends, recvs)

    def first(self, n, offset, arriving=False):
        me, rep = shard_at(self.where), rep_at(self.where)
        owner = shard_at(self.where, negative(offset)) if arriving else me
        copies = []
        for j, (src, (col, cols)) in enumerate(self.cuts(shard_at(self.where, offset))):
            copies.append(
                remote(
                    src,
                    self.ref.at[owner, rep, :, pl.ds(col, cols)],
                    self.first_sends,
                    self.first_recvs,
                    (n, j),
                    device(self.where, offset),
                )
            )
        return copies

    def own(self):
        me, rep = shard_at(self.where), rep_at(self.where)
        return [
            pltpu.make_async_copy(
                src, self.ref.at[me, rep, :, pl.ds(col, cols)], self.own_sem.at[j]
            )
            for j, (src, (col, cols)) in enumerate(self.cuts(me))
        ]

    def begin(self):
        for n, offset in enumerate(PEERS):
            for copy in self.first(n, offset):
                copy.start()
        for copy in self.own():
            copy.start()

    def middle(self):
        for copy in self.own():
            copy.wait()
        for n, offset in enumerate(PEERS):
            for copy in self.first(n, offset, True):
                copy.wait_recv()

    def finish(self):
        self.slabs.finish()
        for n, offset in enumerate(PEERS):
            for copy in self.first(n, offset):
                copy.wait_send()

    def turn(self, i):
        self.slabs.turn(i)


class SlabGather:
    def __init__(self, where, ref, sends, recvs):
        self.where, self.ref, self.sends, self.recvs = where, ref, sends, recvs
        self.got = set()

    def move(self, i, arriving=False):
        owner, (first, count), step, _, _ = SLABS[i]
        rep = rep_at(self.where, less(owner, step) if arriving else owner)
        scale = self.ref.shape[0]
        ref = self.ref.at[pl.ds(first * scale // GROUP, count * scale // GROUP), rep]
        return remote(ref, ref, self.sends, self.recvs, i, device(self.where, step))

    def take(self, i):
        if i not in self.got:
            self.got.add(i)
            self.move(i, True).wait_recv()

    def turn(self, i):
        if SLABS[i][3] is not None:
            self.take(SLABS[i][3])
        self.move(i).start()

    def finish(self):
        for i in SLAB_TURNS:
            self.take(i)
        for i in SLAB_TURNS:
            self.move(i).wait_send()


class SlabScatter:
    def __init__(self, where, ref, land, sends, recvs):
        self.where, self.ref, self.land, self.sends, self.recvs = where, ref, land, sends, recvs
        self.got = set()

    def span(self, i):
        first, count = SLABS[i][1]
        scale = self.ref.shape[0]
        return pl.ds(first * scale // GROUP, count * scale // GROUP)

    def move(self, i, arriving=False):
        owner, _, step, _, _ = SLABS[i]
        rep = rep_at(self.where, owner if arriving else less(owner, step))
        return remote(
            self.ref.at[self.span(i), rep],
            self.land.at[SLAB_LANDS[i], self.span(i)],
            self.sends,
            self.recvs,
            i,
            device(self.where, negative(step)),
        )

    def take(self, i):
        if i in self.got:
            return
        self.got.add(i)
        self.move(i, True).wait_recv()
        first, count = SLABS[i][1]
        scale = self.ref.shape[0]
        rep = rep_at(self.where, SLABS[i][0])

        @pl.loop(first * scale // GROUP, (first + count) * scale // GROUP)
        def _(n):
            total = self.ref[n, rep].astype(F32) + self.land[SLAB_LANDS[i], n].astype(F32)
            self.ref[n, rep] = total.astype(BF)

    def turn(self, i):
        for j in SLAB_FED[i]:
            self.take(j)
        self.move(i).start()

    def finish(self):
        for i in reversed(SLAB_TURNS):
            self.take(i)
        for i in reversed(SLAB_TURNS):
            self.move(i).wait_send()


def spread_scratch(cuts):
    return [DMA((cuts,)), DMA((7, cuts)), DMA((7, cuts)), DMA((SLAB_COUNT,)), DMA((SLAB_COUNT,))]


def qkv_cuts(w_ref, rep):
    rows = pl.ds(pl.multiple_of(rep * SLAB, SLAB), SLAB)

    def cuts(shard):
        return [
            (
                w_ref.at[rows, pl.ds(pl.multiple_of(j * WIDTH + shard * LOCAL, LOCAL), LOCAL)],
                (j * LOCAL, LOCAL),
            )
            for j in range(3)
        ]

    return cuts


def hidden_start(shard):
    return (shard // 2) * (2 * LOCAL_FF) + lax.rem(shard, 2) * (5 * 128)


def gate_up_cuts(gate_ref, up_ref, rep):
    rows = pl.ds(pl.multiple_of(rep * SLAB, SLAB), SLAB)

    def cuts(shard):
        cols = pl.ds(pl.multiple_of(hidden_start(shard), 128), HID)
        return [(gate_ref.at[rows, cols], (0, HID)), (up_ref.at[rows, cols], (HID, HID))]

    return cuts


def normalize(values, gain, shift_):
    center = values - jnp.mean(values, -1, keepdims=True)
    inverse = lax.rsqrt(jnp.mean(center * center, -1, keepdims=True) + EPS)
    scaled = center * inverse
    return (scaled * gain + shift_, scaled, inverse)


def normalize_back(grad, gain, scaled, inverse):
    weighted = grad * gain
    return inverse * (
        weighted
        - jnp.mean(weighted, -1, keepdims=True)
        - scaled * jnp.mean(weighted * scaled, -1, keepdims=True)
    )


def small_row(small_ref, row):
    return jnp.concatenate([small_ref[s, row : row + 1, :] for s in range(GROUP)], axis=1)


def rotary_tables():
    positions = np.arange(TOTAL, dtype=np.float32)
    freqs = np.float32(BASE) ** (-np.arange(0, ROT, 2).astype(np.float32) / np.float32(ROT))
    angles = positions[:, None] * freqs[None, :].astype(np.float32)
    cosine, sine = np.cos(angles).astype(np.float32), np.sin(angles).astype(np.float32)
    half = ROT // 2
    one = np.ones((TOTAL, HEAD_DIM), np.float32)
    low, high = np.zeros((TOTAL, HEAD_DIM), np.float32), np.zeros((TOTAL, HEAD_DIM), np.float32)
    one[:, :half], one[:, half:ROT] = cosine, cosine
    low[:, :half] = -sine
    high[:, half:ROT] = sine
    return np.stack([np.concatenate([t, t], 1) for t in (one, low, high)])


def turned(values, table_ref, rows, sign):
    parts = []
    for side in range(2):
        part = values[:, side * 128 : (side + 1) * 128]
        swing = pltpu.roll(part, 128 - ROT // 2, 1) * table_ref[1, rows, :] + (
            pltpu.roll(part, ROT // 2, 1) * table_ref[2, rows, :]
        )
        straight = part * table_ref[0, rows, :]
        parts.append(straight + swing if sign > 0 else straight - swing)
    return jnp.concatenate(parts, axis=1)


def chunk_rows(i):
    return pl.ds(pl.multiple_of(i * CHUNK, CHUNK), CHUNK)


def token_chunk(ref, i):
    return ref[pl.ds(i * 2, 2)].reshape(CHUNK, WIDTH)


def bias_row(small_ref, shard, j):
    block = j * GROUP + shard
    return small_ref[block // 3, pl.ds(4 + lax.rem(block, 3), 1), :]


def project(shard, tokens_ref, w_ref, small_ref, table_ref, q_ref, k_ref, v_ref):
    @pl.loop(0, CHUNKS)
    def _(i):
        rows = chunk_rows(i)
        tokens = token_chunk(tokens_ref, i)
        for j, ref in enumerate((q_ref, k_ref, v_ref)):
            w = w_ref[:, :, :, j * LOCAL : (j + 1) * LOCAL].reshape(WIDTH, LOCAL)
            value = dot(tokens, w) + bias_row(small_ref, shard, j)
            if j < 2:
                value = turned(value, table_ref, rows, 1)
            if j == 0:
                value = value * HEAD_DIM ** (-0.5)
            ref[rows, :] = value.astype(BF)


def head_lanes(h):
    return lax.broadcasted_iota(jnp.int32, (CHUNK, LOCAL), 1) // HEAD_DIM == h


def allowed_keys(i):
    keys = CHUNK * (i + 1)
    return lax.broadcasted_iota(jnp.int32, (keys, CHUNK), 0) <= (
        lax.broadcasted_iota(jnp.int32, (keys, CHUNK), 1) + CHUNK * i
    )


def attend(q_ref, k_ref, v_ref, vt_ref, mixed_ref, att_ref, lse_ref):
    vt_ref[...] = v_ref[...].astype(F32).T.astype(BF)
    for i in range(CHUNKS):
        keys = CHUNK * (i + 1)
        cols = slice(CHUNK * i, keys)

        @pl.loop(0, LOCAL_HEADS)
        def _(h):
            query = jnp.where(head_lanes(h), q_ref[cols, :], jnp.zeros((), BF))
            scores = dot_nt(k_ref[:keys, :], query)
            scores = jnp.where(allowed_keys(i), scores, -1e30)
            top = jnp.max(scores, 0, keepdims=True)
            expo = jnp.exp(scores - top)
            denom = jnp.sum(expo, 0, keepdims=True)
            probs_low = (expo * (1.0 / denom)).astype(BF)
            lanes = pl.ds(pl.multiple_of(h * HEAD_DIM, HEAD_DIM), HEAD_DIM)
            mixed_ref[lanes, cols] = dot(vt_ref[lanes, :keys], probs_low)
            lse_ref[pl.ds(h, 1), cols] = top + jnp.log(denom)

        att_ref[cols, :] = mixed_ref[:, cols].T.astype(BF)


def attend_back(q_ref, k_ref, v_ref, da_ref, lse_ref, kt_ref, dqt_ref, dk_ref, dv_ref):
    kt_ref[...] = k_ref[...].astype(F32).T.astype(BF)
    dk_ref[...] = jnp.zeros_like(dk_ref)
    dv_ref[...] = jnp.zeros_like(dv_ref)
    for i in range(CHUNKS):
        keys = CHUNK * (i + 1)
        cols = slice(CHUNK * i, keys)

        @pl.loop(0, LOCAL_HEADS)
        def _(h):
            query = jnp.where(head_lanes(h), q_ref[cols, :], jnp.zeros((), BF))
            grad = jnp.where(head_lanes(h), da_ref[cols, :], jnp.zeros((), BF))
            scores = dot_nt(k_ref[:keys, :], query)
            probs = jnp.where(allowed_keys(i), jnp.exp(scores - lse_ref[pl.ds(h, 1), cols]), 0.0)
            grad_probs = dot_nt(v_ref[:keys, :], grad)
            total = jnp.sum(grad_probs * probs, 0, keepdims=True)
            grad_scores = (probs * (grad_probs - total)).astype(BF)
            dv_ref[:keys, :] += dot(probs.astype(BF), grad)
            dk_ref[:keys, :] += dot(grad_scores, query)
            lanes = pl.ds(pl.multiple_of(h * HEAD_DIM, HEAD_DIM), HEAD_DIM)
            dqt_ref[lanes, cols] = dot(kt_ref[lanes, :keys], grad_scores)


def times(left_ref, w_ref, out_ref):
    @pl.loop(0, CHUNKS)
    def _(i):
        left = left_ref[chunk_rows(i), :]
        for j in range(WIDTH // 512):
            cols = slice(j * 512, (j + 1) * 512)
            out_ref[pl.ds(i * 2, 2), :, cols] = (
                dot(left, w_ref[:, cols]).astype(BF).reshape(2, ROWS, 512)
            )


def times_back(left_ref, w_ref, out_ref):
    depth = left_ref.shape[1]

    @pl.loop(0, CHUNKS)
    def _(i):
        left = left_ref[chunk_rows(i), :]
        for j in range(GROUP):
            w = w_ref[j].reshape(LOCAL, depth)
            out_ref[pl.ds(i * 2, 2), :, j * LOCAL : (j + 1) * LOCAL] = (
                dot_nt(left, w).astype(BF).reshape(2, ROWS, LOCAL)
            )


def feed_forward(shard, tokens_ref, grads_ref, w_ref, down_ref, hid_ref, dgu_ref):
    odd = lax.rem(shard, 2)

    @pl.loop(0, CHUNKS)
    def _(i):
        rows = chunk_rows(i)
        tokens, grads = token_chunk(tokens_ref, i), token_chunk(grads_ref, i)
        for j in range(HID // CHUNK):
            cols = slice(j * CHUNK, (j + 1) * CHUNK)
            late = slice(HID + j * CHUNK, HID + (j + 1) * CHUNK)
            gate = dot(tokens, w_ref[:, :, :, cols].reshape(WIDTH, CHUNK))
            up = dot(tokens, w_ref[:, :, :, late].reshape(WIDTH, CHUNK))
            grad = dot_nt(grads, down_ref[cols, :])
            unit = lax.broadcasted_iota(jnp.int32, (CHUNK, CHUNK), 1) + (j * CHUNK - 64 * odd)
            mine = jnp.logical_and(unit >= 0, unit < LOCAL_FF)
            sigma = 1.0 / (1.0 + jnp.exp(-gate))
            silu = gate * sigma
            hid_ref[rows, cols] = jnp.where(mine, silu * up, 0.0).astype(BF)
            grad_gate = grad * up * (sigma * (1.0 + gate * (1.0 - sigma)))
            dgu_ref[rows, cols] = jnp.where(mine, grad_gate, 0.0).astype(BF)
            dgu_ref[rows, late] = jnp.where(mine, grad * silu, 0.0).astype(BF)


def outer(left_ref, right_ref, out_ref):
    depth = out_ref.shape[-1]
    tiles = left_ref.shape[-1] // LOCAL

    @pl.loop(0, tiles)
    def _(m):
        cols = pl.ds(pl.multiple_of(m * LOCAL, LOCAL), LOCAL)
        if len(left_ref.shape) == 3:
            left = left_ref[:, :, cols].reshape(TOTAL, LOCAL)
        else:
            left = left_ref[:, cols]
        left = left.astype(F32).T.astype(BF)
        for j in range(depth // 512 if depth % 512 == 0 else depth // 256):
            size = 512 if depth % 512 == 0 else 256
            part = slice(j * size, (j + 1) * size)
            if len(right_ref.shape) == 3:
                right = right_ref[:, :, part].reshape(TOTAL, size)
            else:
                right = right_ref[:, part]
            out_ref[cols, part] = dot(left, right).astype(BF)


def params(cid=None, mib=56):
    if cid is None:
        return pltpu.CompilerParams(vmem_limit_bytes=mib * 2**20)
    return pltpu.CompilerParams(
        collective_id=cid, has_side_effects=True, vmem_limit_bytes=mib * 2**20
    )


def start_kernel(x_ref, small_ref, qkv_ref, out_ref, all_small, w_ref, *sems):
    small_sends, small_recvs, sends, recvs = sems[:4]
    where = place()
    greet(where, PEERS + REP_NEIGHBOURS)
    me = shard_at(where)

    def small(n, offset, arriving=False):
        owner = shard_at(where, negative(offset)) if arriving else me
        return remote(
            small_ref, all_small.at[owner], small_sends, small_recvs, n, device(where, offset)
        )

    for n, offset in enumerate(PEERS):
        small(n, offset).start()
    all_small[me] = small_ref[...]
    spread = Spread(where, qkv_cuts(qkv_ref, rep_at(where)), w_ref, *sems[4:])
    spread.begin()
    for n, offset in enumerate(PEERS):
        small(n, offset, True).wait_recv()
    normed, _, _ = normalize(
        x_ref[...].astype(F32), small_row(all_small, 0), small_row(all_small, 1)
    )
    out_ref[me] = normed.astype(BF)
    gather = Gather(where, out_ref, sends, recvs)
    early = [i for i in TURNS if MOVES[i][3] is None]
    for i in early:
        gather.turn(i)
    spread.middle()
    queue = [("s", SLABS[i][4] - 1.5, i) for i in range(SLAB_COUNT)]
    queue += [("g", MOVES[i][4], i) for i in range(COUNT) if i not in early]
    for kind, _, i in sorted(queue, key=lambda e: e[1]):
        (spread if kind == "s" else gather).turn(i)
    gather.finish()
    spread.finish()
    for n, offset in enumerate(PEERS):
        small(n, offset).wait_send()


def start(x, small, qkv_weight):
    return pl.pallas_call(
        start_kernel,
        out_shape=(
            jax.ShapeDtypeStruct((GROUP, ROWS, WIDTH), BF),
            jax.ShapeDtypeStruct((GROUP, 8, LOCAL), F32),
            jax.ShapeDtypeStruct((GROUP, REPS, SLAB, 3 * LOCAL), BF),
        ),
        in_specs=[VM, VM, ANY],
        out_specs=(VM, VM, VM),
        scratch_shapes=[DMA((7,)), DMA((7,)), DMA((COUNT,)), DMA((COUNT,))] + spread_scratch(3),
        compiler_params=params(0),
        name="start",
    )(x, small, qkv_weight)


def attention_kernel(tokens_ref, w_ref, small_ref, table_ref, ow_ref, q_ref, k_ref, v_ref, att_ref, lse_ref, part_ref, vt_ref, mixed_ref):
    shard = lax.axis_index("shard")
    project(shard, tokens_ref, w_ref, small_ref, table_ref, q_ref, k_ref, v_ref)
    attend(q_ref, k_ref, v_ref, vt_ref, mixed_ref, att_ref, lse_ref)
    times(att_ref, ow_ref, part_ref)


def attention(tokens, w_qkv, small, table, out_weight):
    sds = jax.ShapeDtypeStruct
    return pl.pallas_call(
        attention_kernel,
        out_shape=(
            *[sds((TOTAL, LOCAL), BF)] * 4,
            sds((8, TOTAL), F32),
            sds((GROUP, ROWS, WIDTH), BF),
        ),
        in_specs=[VM] * 5,
        out_specs=(VM,) * 6,
        scratch_shapes=[pltpu.VMEM((LOCAL, TOTAL), BF), pltpu.VMEM((LOCAL, TOTAL), F32)],
        compiler_params=params(),
        name="attention",
    )(tokens, w_qkv, small, table, out_weight)


def middle_kernel(part_ref, x_ref, small_ref, gate_ref, up_ref, mid_ref, out_ref, w_ref, buf, land, *sems):
    back_sends, back_recvs, sends, recvs = sems[:4]
    where = place()
    greet(where, PEERS + REP_NEIGHBOURS)
    me = shard_at(where)
    spread = Spread(where, gate_up_cuts(gate_ref, up_ref, rep_at(where)), w_ref, *sems[4:])
    buf[...] = part_ref[...]
    scatter = Scatter(where, buf, land, back_sends, back_recvs)
    turns = [i for i in reversed(TURNS)]
    first = [i for i in turns if not FED[i]]
    for i in first:
        scatter.turn(i)
    spread.begin()
    rest = [i for i in turns if FED[i]]
    for i in rest[:4]:
        scatter.turn(i)
    spread.middle()
    early = [i for i in SLAB_TURNS if SLABS[i][3] is None]
    for i in early:
        spread.turn(i)
    for i in rest[4:]:
        scatter.turn(i)
    scatter.finish()
    mid = x_ref[...].astype(F32) + buf[me].astype(F32)
    mid_ref[...] = mid
    normed, _, _ = normalize(mid, small_row(small_ref, 2), small_row(small_ref, 3))
    out_ref[me] = normed.astype(BF)
    gather = Gather(where, out_ref, sends, recvs)
    starts = [i for i in TURNS if MOVES[i][3] is None]
    for i in starts:
        gather.turn(i)
    queue = [("s", SLABS[i][4] - 1, i) for i in range(SLAB_COUNT) if i not in early]
    queue += [("g", MOVES[i][4], i) for i in range(COUNT) if i not in starts]
    for kind, _, i in sorted(queue, key=lambda e: e[1]):
        (spread if kind == "s" else gather).turn(i)
    gather.finish()
    spread.finish()


def middle(part, x, small, gate_weight, up_weight):
    sds = jax.ShapeDtypeStruct
    return pl.pallas_call(
        middle_kernel,
        out_shape=(
            sds((ROWS, WIDTH), F32),
            sds((GROUP, ROWS, WIDTH), BF),
            sds((GROUP, REPS, SLAB, 2 * HID), BF),
        ),
        in_specs=[VM, VM, VM, ANY, ANY],
        out_specs=(VM, VM, VM),
        scratch_shapes=[
            pltpu.VMEM((GROUP, ROWS, WIDTH), BF),
            pltpu.VMEM((LANDINGS, ROWS, WIDTH // 2), BF),
            *[DMA((COUNT,))] * 4,
        ]
        + spread_scratch(2),
        compiler_params=params(1),
        name="middle",
    )(part, x, small, gate_weight, up_weight)


def mlp_kernel(tokens_ref, grads_ref, w_ref, down_ref, hid_ref, dgu_ref, part_ref, back_ref):
    shard = lax.axis_index("shard")
    feed_forward(shard, tokens_ref, grads_ref, w_ref, down_ref, hid_ref, dgu_ref)
    times(hid_ref, down_ref, part_ref)
    times_back(dgu_ref, w_ref, back_ref)


def mlp(tokens, grads, w_gu, down):
    sds = jax.ShapeDtypeStruct
    return pl.pallas_call(
        mlp_kernel,
        out_shape=(
            sds((TOTAL, HID), BF),
            sds((TOTAL, 2 * HID), BF),
            sds((GROUP, ROWS, WIDTH), BF),
            sds((GROUP, ROWS, WIDTH), BF),
        ),
        in_specs=[VM] * 4,
        out_specs=(VM,) * 4,
        compiler_params=params(),
        name="mlp",
    )(tokens, grads, w_gu, down)


def turnback_kernel(part_ref, mid_ref, gy_ref, small_ref, a2_ref, dgu_ref, hid_ref, grads_ref, dmid_ref, out_ref, sums_ref, ggu_ref, gdown_ref, buf, land, *sems):
    back_sends, back_recvs, sends, recvs = sems[:4]
    where = place()
    greet(where, NEIGHBOURS)
    me = shard_at(where)
    buf[...] = part_ref[...]
    scatter = Scatter(where, buf, land, back_sends, back_recvs)
    for i in reversed(TURNS):
        scatter.turn(i)
    scatter.finish()
    gain = small_row(small_ref, 2)
    _, scaled, inverse = normalize(mid_ref[...], gain, small_row(small_ref, 3))
    grad = buf[me].astype(F32)
    sums_ref[0:1, :] = jnp.sum(grad * scaled, 0, keepdims=True)
    sums_ref[1:2, :] = jnp.sum(grad, 0, keepdims=True)
    dmid = gy_ref[...].astype(F32) + normalize_back(grad, gain, scaled, inverse)
    dmid_ref[...] = dmid
    out_ref[me] = dmid.astype(BF)
    gather = Gather(where, out_ref, sends, recvs)
    starts = [i for i in TURNS if MOVES[i][3] is None]
    for i in starts:
        gather.turn(i)
    outer(hid_ref, grads_ref, gdown_ref)
    for i in TURNS:
        if i not in starts:
            gather.turn(i)
    outer(a2_ref, dgu_ref, ggu_ref)
    gather.finish()


def turnback(part, mid, gy, small, a2, dgu, hid, grads):
    sds = jax.ShapeDtypeStruct
    return pl.pallas_call(
        turnback_kernel,
        out_shape=(
            sds((ROWS, WIDTH), F32),
            sds((GROUP, ROWS, WIDTH), BF),
            sds((8, WIDTH), F32),
            sds((WIDTH, 2 * HID), BF),
            sds((HID, WIDTH), BF),
        ),
        in_specs=[VM] * 8,
        out_specs=(VM,) * 5,
        scratch_shapes=[
            pltpu.VMEM((GROUP, ROWS, WIDTH), BF),
            pltpu.VMEM((LANDINGS, ROWS, WIDTH // 2), BF),
            *[DMA((COUNT,))] * 4,
        ],
        compiler_params=params(2, 60),
        name="turnback",
    )(part, mid, gy, small, a2, dgu, hid, grads)


def attention_back_kernel(tokens_ref, ow_ref, q_ref, k_ref, v_ref, lse_ref, table_ref, w_ref, att_ref, dqkv_ref, part_ref, sums_ref, gout_ref, da_ref, kt_ref, dqt_ref, dk_ref, dv_ref):
    @pl.loop(0, CHUNKS)
    def _(i):
        da_ref[chunk_rows(i), :] = dot_nt(token_chunk(tokens_ref, i), ow_ref[...]).astype(BF)

    attend_back(q_ref, k_ref, v_ref, da_ref, lse_ref, kt_ref, dqt_ref, dk_ref, dv_ref)
    sums_ref[...] = jnp.zeros_like(sums_ref)
    for i in range(CHUNKS):
        rows = slice(i * CHUNK, (i + 1) * CHUNK)
        grad_q = dqt_ref[:, rows].T * HEAD_DIM ** (-0.5)
        for j, value in enumerate((grad_q, dk_ref[rows, :], dv_ref[rows, :])):
            if j < 2:
                value = turned(value, table_ref, rows, -1)
            low = value.astype(BF)
            cols = slice(j * LOCAL, (j + 1) * LOCAL)
            dqkv_ref[rows, cols] = low
            sums_ref[0:1, cols] += jnp.sum(low.astype(F32), 0, keepdims=True)
    times_back(dqkv_ref, w_ref, part_ref)
    outer(att_ref, tokens_ref, gout_ref)


def attention_back(tokens, out_weight, q, k, v, lse, table, w_qkv, att):
    sds = jax.ShapeDtypeStruct
    return pl.pallas_call(
        attention_back_kernel,
        out_shape=(
            sds((TOTAL, 3 * LOCAL), BF),
            sds((GROUP, ROWS, WIDTH), BF),
            sds((8, 3 * LOCAL), F32),
            sds((LOCAL, WIDTH), BF),
        ),
        in_specs=[VM] * 9,
        out_specs=(VM,) * 4,
        scratch_shapes=[
            pltpu.VMEM((TOTAL, LOCAL), BF),
            pltpu.VMEM((LOCAL, TOTAL), BF),
            pltpu.VMEM((LOCAL, TOTAL), F32),
            pltpu.VMEM((TOTAL, LOCAL), F32),
            pltpu.VMEM((TOTAL, LOCAL), F32),
        ],
        compiler_params=params(),
        name="attention_back",
    )(tokens, out_weight, q, k, v, lse, table, w_qkv, att)


def finish_kernel(part_ref, x_ref, dmid_ref, small_ref, a1_ref, dqkv_ref, down_ref, mid_ref, grad_ref, act_ref, sums_ref, gqkv_ref, buf, land, buf_down, land_down, *sems):
    where = place()
    greet(where, NEIGHBOURS)
    me = shard_at(where)
    buf[...] = part_ref[...]
    buf_down[...] = down_ref[...]
    scatter = Scatter(where, buf, land, sems[0], sems[1])
    first = [i for i in reversed(TURNS) if not FED[i]]
    for i in first:
        scatter.turn(i)
    outer(a1_ref, dqkv_ref, gqkv_ref)
    for i in reversed(TURNS):
        if i not in first:
            scatter.turn(i)
    scatter.finish()
    gain = small_row(small_ref, 0)
    _, scaled, inverse = normalize(x_ref[...].astype(F32), gain, small_row(small_ref, 1))
    grad = buf[me].astype(F32)
    sums_ref[0:1, :] = jnp.sum(grad * scaled, 0, keepdims=True)
    sums_ref[1:2, :] = jnp.sum(grad, 0, keepdims=True)
    grad_ref[...] = dmid_ref[...] + normalize_back(grad, gain, scaled, inverse)
    last = Scatter(where, buf_down, land_down, sems[2], sems[3])
    last.run()
    act_ref[...] = (mid_ref[...] + buf_down[me].astype(F32)).astype(BF)


def finish(part, x, dmid, small, a1, dqkv, down, mid):
    sds = jax.ShapeDtypeStruct
    return pl.pallas_call(
        finish_kernel,
        out_shape=(
            sds((ROWS, WIDTH), F32),
            sds((ROWS, WIDTH), BF),
            sds((8, WIDTH), F32),
            sds((WIDTH, 3 * LOCAL), BF),
        ),
        in_specs=[VM] * 8,
        out_specs=(VM,) * 4,
        scratch_shapes=[
            pltpu.VMEM((GROUP, ROWS, WIDTH), BF),
            pltpu.VMEM((LANDINGS, ROWS, WIDTH // 2), BF),
            pltpu.VMEM((GROUP, ROWS, WIDTH), BF),
            pltpu.VMEM((LANDINGS, ROWS, WIDTH // 2), BF),
            *[DMA((COUNT,))] * 4,
        ],
        compiler_params=params(3),
        name="finish",
    )(part, x, dmid, small, a1, dqkv, down, mid)


class Return:
    def __init__(self, where, ref, out, first_sends, first_recvs, sends, recvs):
        self.where, self.ref, self.out = where, ref, out
        self.first_sends, self.first_recvs = first_sends, first_recvs
        self.slabs = SlabGather(where, out, sends, recvs)

    def first(self, n, offset, arriving=False):
        me, rep = shard_at(self.where), rep_at(self.where)
        source = shard_at(self.where, negative(offset)) if arriving else me
        return remote(
            self.ref.at[shard_at(self.where, offset), rep],
            self.out.at[source, rep],
            self.first_sends,
            self.first_recvs,
            n,
            device(self.where, offset),
        )

    def begin(self):
        me, rep = shard_at(self.where), rep_at(self.where)
        for n, offset in enumerate(PEERS):
            self.first(n, offset).start()
        self.out[me, rep] = self.ref[me, rep]

    def middle(self):
        for n, offset in enumerate(PEERS):
            self.first(n, offset, True).wait_recv()

    def finish(self):
        self.slabs.finish()
        for n, offset in enumerate(PEERS):
            self.first(n, offset).wait_send()


class Vectors:
    ROUNDS = ((TWIN,), (NEAR,), (NORTH, SOUTH, (0, 0, 0, 2, 0)))

    def __init__(self, where, msg, land, mine, round_land, first_sends, first_recvs, sends, recvs):
        self.where, self.msg, self.land, self.mine, self.round_land = where, msg, land, mine, round_land
        self.first_sends, self.first_recvs = first_sends, first_recvs
        self.sends, self.recvs = sends, recvs

    def first(self, n, offset, arriving=False):
        me = shard_at(self.where)
        source = shard_at(self.where, negative(offset)) if arriving else me
        return remote(
            self.msg.at[shard_at(self.where, offset)],
            self.land.at[source],
            self.first_sends,
            self.first_recvs,
            n,
            device(self.where, offset),
        )

    def begin(self):
        me = shard_at(self.where)
        for n, offset in enumerate(PEERS):
            self.first(n, offset).start()
        self.land[me] = self.msg[me]

    def middle(self):
        me = shard_at(self.where)
        for n, offset in enumerate(PEERS):
            self.first(n, offset, True).wait_recv()
        total = self.land[0]
        for source in range(1, GROUP):
            total = total + self.land[source]
        self.mine[0] = total
        for p in range(3):
            block = 3 * me + p
            self.mine[0, 4 + p : 5 + p, :] = self.land[lax.rem(block, GROUP), pl.ds(4 + block // GROUP, 1), :]

    def hop(self, n, i, step):
        return remote(self.mine.at[n], self.round_land.at[i], self.sends, self.recvs, i, device(self.where, step))

    def round(self, n):
        base = sum(len(r) for r in self.ROUNDS[:n])
        for i, step in enumerate(self.ROUNDS[n]):
            self.hop(n, base + i, step).start()
        total = self.mine[n]
        for i, step in enumerate(self.ROUNDS[n]):
            self.hop(n, base + i, step).wait_recv()
            total = total + self.round_land[base + i]
        self.mine[n + 1] = total

    def finish(self):
        for n, offset in enumerate(PEERS):
            self.first(n, offset).wait_send()
        for n, steps in enumerate(self.ROUNDS):
            base = sum(len(r) for r in self.ROUNDS[:n])
            for i, step in enumerate(steps):
                self.hop(n, base + i, step).wait_send()


VECTOR_SCRATCH = [
    pltpu.VMEM((GROUP, 8, LOCAL), F32),
    pltpu.VMEM((GROUP, 8, LOCAL), F32),
    pltpu.VMEM((4, 8, LOCAL), F32),
    pltpu.VMEM((5, 8, LOCAL), F32),
    DMA((7,)),
    DMA((7,)),
    DMA((5,)),
    DMA((5,)),
]


class Writer:
    def __init__(self, stage, sem):
        self.stage, self.sem, self.count, self.flying = stage, sem, 0, []

    def put(self, value, dst):
        slot = self.count % 2
        if self.count >= 2:
            self.flying.pop(0).wait()
        rows, cols = value.shape
        src = self.stage.at[slot, pl.ds(0, rows), pl.ds(0, cols)]
        self.stage[slot, :rows, :cols] = value
        copy = pltpu.make_async_copy(src, dst, self.sem.at[slot])
        copy.start()
        self.flying.append(copy)
        self.count += 1

    def finish(self):
        for copy in self.flying:
            copy.wait()


def unpack_columns(block, out_ref, writer, base, width, starts):
    for s in range(GROUP):
        value = block(s)
        start = starts[s]
        if s % 2 == 0:
            seam = value[:, 640:] + block(s + 1)[:, :128]
            value = jnp.concatenate([value[:, :640], seam], axis=1)
        else:
            value, start = value[:, 128:], start + 128
        writer.put(value, out_ref.at[:, pl.ds(start, value.shape[1])])


def reduce_kernel(ggu_ref, grest_ref, gqkv_ref, one_ref, two_ref, bias_ref, gate_ref, up_ref, qkv_ref, rest_ref, vec_ref, *scratch):
    where = place()
    greet(where, PEERS + REP_NEIGHBOURS + ((0, 0, 0, 2, 0),))
    me, rep = shard_at(where), rep_at(where)
    refs = (ggu_ref, grest_ref, gqkv_ref)
    copies, lands, outs = scratch[0:3], scratch[3:6], scratch[6:9]
    sems = scratch[9:]
    scatters = [
        SlabScatter(where, copies[n], lands[n], sems[4 * n], sems[4 * n + 1]) for n in range(3)
    ]
    vectors = Vectors(where, *sems[16:24])
    stage, stage_sem = sems[24:26]
    for d in range(GROUP):
        cols = slice(d * LOCAL, (d + 1) * LOCAL)
        vectors.msg[d, 0:2, :] = one_ref[0:2, cols]
        vectors.msg[d, 2:4, :] = two_ref[0:2, cols]
        for j in range(3):
            vectors.msg[d, 4 + j : 5 + j, :] = bias_ref[0:1, j * LOCAL : (j + 1) * LOCAL]
    vectors.begin()
    for n in range(3):
        copies[n][...] = refs[n][...]
        for i in reversed(SLAB_TURNS):
            if not SLAB_FED[i]:
                scatters[n].turn(i)
    vectors.middle()
    for n in range(3):
        for i in reversed(SLAB_TURNS):
            if SLAB_FED[i]:
                scatters[n].turn(i)
        if n < 3:
            vectors.round(n)
    vec_ref[...] = vectors.mine[3]
    first = {0: sems[12:14], 2: sems[14:16]}
    gathers = []
    for n in range(3):
        scatters[n].finish()
        if n == 1:
            outs[n][:, rep] = copies[n][:, rep]
            gathers.append(SlabGather(where, outs[n], sems[4 * n + 2], sems[4 * n + 3]))
        else:
            back = Return(where, copies[n], outs[n], *first[n], sems[4 * n + 2], sems[4 * n + 3])
            back.begin()
            gathers.append(back)
    for n in range(3):
        if n != 1:
            gathers[n].middle()
        slabs = gathers[n] if n == 1 else gathers[n].slabs
        for i in SLAB_TURNS:
            slabs.turn(i)
    writer = Writer(stage, stage_sem)
    for n in range(3):
        gathers[n].finish()
        if n == 0:
            starts = [(s // 2) * 2 * LOCAL_FF + (s % 2) * 640 for s in range(GROUP)]
            for side, ref in enumerate((gate_ref, up_ref)):
                unpack_columns(
                    lambda s: outs[0][s, :, :, side * HID : (side + 1) * HID].reshape(LOCAL, HID).astype(F32),
                    ref, writer, 0, HID, starts,
                )
        elif n == 1:
            for j in range(4):
                for half in range(2):
                    cols = slice(half * 1024, (half + 1) * 1024)
                    writer.put(
                        outs[1][j, :, :, cols].reshape(LOCAL, 1024).astype(F32),
                        rest_ref.at[pl.ds(j * LOCAL, LOCAL), pl.ds(half * 1024, 1024)],
                    )
        else:
            for s in range(GROUP):
                for j in range(3):
                    writer.put(
                        outs[2][s, :, :, j * LOCAL : (j + 1) * LOCAL].reshape(LOCAL, LOCAL).astype(F32),
                        qkv_ref.at[:, pl.ds(j * WIDTH + s * LOCAL, LOCAL)],
                    )
    writer.finish()
    vectors.finish()


def reduce(g_gu, g_rest, g_qkv, sums_one, sums_two, sums_bias):
    sds = jax.ShapeDtypeStruct
    shapes = [(GROUP, REPS, SLAB, 2 * HID), (4, REPS, SLAB, WIDTH), (GROUP, REPS, SLAB, 3 * LOCAL)]
    return pl.pallas_call(
        reduce_kernel,
        out_shape=(
            sds((LOCAL, FF), F32),
            sds((LOCAL, FF), F32),
            sds((LOCAL, 3 * WIDTH), F32),
            sds((4 * LOCAL, WIDTH), F32),
            sds((8, LOCAL), F32),
        ),
        in_specs=[VM] * 6,
        out_specs=(ANY, ANY, ANY, ANY, VM),
        scratch_shapes=[pltpu.VMEM(s, BF) for s in shapes]
        + [pltpu.VMEM((SLAB_LANDINGS, s[0], SLAB, s[3]), BF) for s in shapes]
        + [pltpu.VMEM(s, BF) for s in shapes]
        + [DMA((SLAB_COUNT,))] * 12
        + [DMA((7,))] * 4
        + VECTOR_SCRATCH
        + [pltpu.VMEM((2, LOCAL, 1024), F32), DMA((2,))],
        compiler_params=params(4, 62),
        name="reduce",
    )(g_gu.reshape(shapes[0]), g_rest.reshape(shapes[1]), g_qkv.reshape(shapes[2]), sums_one, sums_two, sums_bias)


def shards(
    inputs,
    cotangent,
    ln1_gain,
    ln1_bias,
    qkv_weight,
    qkv_bias,
    out_weight,
    ln2_gain,
    ln2_bias,
    gate_weight,
    up_weight,
    down_weight,
):
    batch, length, width = inputs.shape
    me = lax.axis_index("shard")
    odd = lax.rem(me, 2)
    table = jnp.asarray(rotary_tables())
    x = inputs.reshape(length, width)
    gy = cotangent.reshape(length, width)
    rows = [ln1_gain, ln1_bias, ln2_gain, ln2_bias, qkv_bias, jnp.zeros((LOCAL,), BF)]
    small = jnp.concatenate(rows).astype(F32).reshape(8, LOCAL)
    grads = lax.all_gather(gy, "shard", axis=0)
    down = lax.dynamic_update_slice(jnp.zeros((HID, width), BF), down_weight, (64 * odd, 0))

    a1, all_small, w_qkv = start(x, small, qkv_weight)
    q, k, v, att, lse, part = attention(a1, w_qkv, all_small, table, out_weight)
    mid, a2, w_gu = middle(part, x, all_small, gate_weight, up_weight)
    hid, dgu, part_down, part_two = mlp(a2, grads, w_gu, down)
    dmid, dy1, sums_two, g_gu, g_down = turnback(part_two, mid, gy, all_small, a2, dgu, hid, grads)
    dqkv, part_one, sums_bias, g_out = attention_back(
        dy1, out_weight, q, k, v, lse, table, w_qkv, att
    )
    input_grad, activations, sums_one, g_qkv = finish(
        part_one, x, dmid, all_small, a1, dqkv, part_down, mid
    )

    g_rest = jnp.concatenate([g_out, g_down])
    g_gate, g_up, g_qkv, g_rest, vectors = reduce(g_gu, g_rest, g_qkv, sums_one, sums_two, sums_bias)
    g_down = lax.dynamic_slice(g_rest, (LOCAL + 64 * odd, 0), (LOCAL_FF, width))
    return (
        activations.reshape(batch, length, width),
        input_grad.reshape(batch, length, width),
        vectors[0],
        vectors[1],
        g_qkv,
        vectors[4:7].reshape(3 * LOCAL),
        g_rest[:LOCAL],
        vectors[2],
        vectors[3],
        g_gate,
        g_up,
        g_down,
    )


def solution(mesh):
    tokens, vector, matrix = P("rep", "shard", None), P("shard"), P("shard", None)
    return jax.shard_map(
        shards,
        mesh=mesh,
        in_specs=(tokens, tokens, vector, vector, matrix, vector, matrix, vector, vector, matrix, matrix, matrix),
        out_specs=(tokens, tokens, vector, vector, matrix, vector, matrix, vector, vector, matrix, matrix, matrix),
        check_vma=False,
    )
```

```python
import functools

import jax
import jax.numpy as jnp
import numpy as np
from jax import lax
from jax.experimental import pallas as pl
from jax.experimental.pallas import tpu as pltpu
from jax.sharding import PartitionSpec as P

HEADS = 32
HEAD_DIM = 64
ROT = 16
WIDTH = 2048
GROUP = 8
REPS = 16
ROWS = 128
TOTAL = GROUP * ROWS
LOCAL = WIDTH // GROUP
LOCAL_HEADS = HEADS // GROUP
FF = 5632
LOCAL_FF = FF // GROUP
HID = 768
SLAB = LOCAL // REPS
NEAR_COLS, FAR_COLS = 768, 1280
CHUNK = 256
CHUNKS = TOTAL // CHUNK
EPS = 1e-05
BASE = 10000.0
BF = jnp.bfloat16
F32 = jnp.float32
MESH = pl.DeviceIdType.MESH
VM = pl.BlockSpec(memory_space=pltpu.VMEM)
ANY = pl.BlockSpec(memory_space=pl.ANY)
DMA = pltpu.SemaphoreType.DMA


def dot(left, right):
    return jnp.dot(left, right, preferred_element_type=F32)


def dot_nt(left, right):
    return lax.dot_general(left, right, (((1,), (1,)), ((), ())), preferred_element_type=F32)


FAR, UP, DOWN = (1, 0, 0, 0, 0), (0, 1, 0, 0, 0), (0, -1, 0, 0, 0)
NEAR, NORTH, SOUTH, TWIN = (0, 0, 1, 0, 0), (0, 0, 0, 1, 0), (0, 0, 0, -1, 0), (0, 0, 0, 0, 1)
HERE = (0, 0, 0, 0, 0)
SIZES = (2, 4, 2, 4, 2)
PEERS = tuple((f, z, 0, 0, 0) for f in range(2) for z in range(4) if (f, z) != (0, 0))


def place():
    shard, rep = lax.axis_index("shard"), lax.axis_index("rep")
    return (shard // 4, lax.rem(shard, 4), rep // 8, lax.rem(rep // 2, 4), lax.rem(rep, 2))


def shift(where, offset):
    return tuple(
        lax.rem(a + (o + 2 * n) % n, n) if o % n else a for a, o, n in zip(where, offset, SIZES)
    )


def shard_at(where, offset=HERE):
    far, level = shift(where, offset)[:2]
    return far * 4 + level


def rep_at(where, offset=HERE):
    near, north, core = shift(where, offset)[2:]
    return near * 8 + north * 2 + core


def device(where, offset):
    return (shard_at(where, offset), rep_at(where, offset))


def less(a, b):
    return tuple((p - q) % n for p, q, n in zip(a, b, SIZES))


def negative(a):
    return tuple(-p for p in a)


def greet(where, offsets):
    barrier = pltpu.get_barrier_semaphore()
    for offset in offsets:
        pl.semaphore_signal(
            barrier, inc=1, device_id=device(where, negative(offset)), device_id_type=MESH
        )
    pl.semaphore_wait(barrier, len(offsets))


def remote(src, dst, sends, recvs, i, to):
    return pltpu.make_async_remote_copy(
        src_ref=src,
        dst_ref=dst,
        send_sem=sends.at[i],
        recv_sem=recvs.at[i],
        device_id=to,
        device_id_type=MESH,
    )


def token_moves():
    moves = []

    def add(owner, part, step, first, turn):
        moves.append((owner, part, step, first, turn))
        return len(moves) - 1

    near, far = (0, NEAR_COLS), (NEAR_COLS, FAR_COLS)
    whole, top, low = (0, ROWS), (0, ROWS // 2), (ROWS // 2, ROWS // 2)
    up2 = (0, 2, 0, 0, 0)
    up = add(HERE, (whole, near), UP, None, 0)
    down = add(HERE, (whole, near), DOWN, None, 0)
    add(HERE, (whole, near), FAR, None, 0.2)
    a = add(DOWN, (top, near), UP, up, 1)
    b = add(UP, (low, near), DOWN, down, 1)
    add(DOWN, (whole, near), FAR, up, 1.1)
    add(UP, (whole, near), FAR, down, 1.1)
    add(up2, (top, near), FAR, a, 2)
    add(up2, (low, near), FAR, b, 2)
    over = add(HERE, (whole, far), FAR, None, 0.1)
    up = add(HERE, (whole, far), UP, None, 1.1)
    down = add(HERE, (whole, far), DOWN, None, 1.1)
    add(DOWN, (top, far), UP, up, 3)
    add(UP, (low, far), DOWN, down, 3)
    up = add(FAR, (whole, far), UP, over, 2.5)
    down = add(FAR, (whole, far), DOWN, over, 2.5)
    add(tuple(p + q for p, q in zip(FAR, DOWN)), (top, far), UP, up, 4)
    add(tuple(p + q for p, q in zip(FAR, UP)), (low, far), DOWN, down, 4)
    return tuple(moves)


MOVES = token_moves()
COUNT = len(MOVES)
TURNS = tuple(sorted(range(COUNT), key=lambda i: MOVES[i][4]))
FED = tuple(tuple(j for j in range(COUNT) if MOVES[j][3] == i) for i in range(COUNT))
NEIGHBOURS = (FAR, UP, DOWN)
LANDS = {}
for _i in range(COUNT):
    pair = MOVES[_i][1][0][0] > 0
    LANDS[_i] = LANDS[_i - 1] if pair else len(set(LANDS.values()))
LANDINGS = len(set(LANDS.values()))


def token_part(ref, block, part):
    (row, rows), (col, cols) = part
    return ref.at[block, pl.ds(row, rows), pl.ds(col, cols)]


class Gather:
    def __init__(self, where, ref, sends, recvs, own=None):
        self.where, self.ref, self.sends, self.recvs, self.own = where, ref, sends, recvs, own
        self.got = set()

    def move(self, i, arriving=False):
        owner, part, step, _, _ = MOVES[i]
        block = shard_at(self.where, less(owner, step) if arriving else owner)
        ref = token_part(self.ref, block, part)
        src = ref
        if owner == HERE and self.own is not None and not arriving:
            src = token_part(self.own, 0, part)
        return remote(src, ref, self.sends, self.recvs, i, device(self.where, step))

    def take(self, i):
        if i not in self.got:
            self.got.add(i)
            self.move(i, True).wait_recv()

    def turn(self, i):
        if MOVES[i][3] is not None:
            self.take(MOVES[i][3])
        self.move(i).start()

    def take_all(self):
        for i in TURNS:
            self.take(i)

    def finish(self):
        for i in TURNS:
            self.take(i)
        for i in TURNS:
            self.move(i).wait_send()

    def run(self):
        for i in TURNS:
            self.turn(i)
        self.finish()


def agenda(mover, turns, start, unit, backwards=False):
    last = max(turns[i] for i in turns)
    return [
        (start + unit * ((last - t) if backwards else t), mover, i) for i, t in turns.items()
    ]


def slab_agenda(mover, start, unit):
    turns = mover.slabs.TURNS if hasattr(mover, "slabs") else mover.TURNS
    return [(start + unit * t, mover, i) for i, t in enumerate(turns)]


class Agenda:
    def __init__(self):
        self.items = []

    def add(self, items):
        self.items = sorted(self.items + items, key=lambda e: e[0])

    def until(self, time):
        while self.items and self.items[0][0] <= time:
            _, mover, i = self.items.pop(0)
            mover.turn(i)


TOKEN_TURNS = {i: MOVES[i][4] for i in range(COUNT)}


class Scatter:
    def __init__(self, where, buf, land, sends, recvs):
        self.where, self.buf, self.land, self.sends, self.recvs = where, buf, land, sends, recvs
        self.got = set()

    def move(self, i, arriving=False):
        owner, part, step, _, _ = MOVES[i]
        block = shard_at(self.where, owner if arriving else less(owner, step))
        (row, rows), (col, cols) = part
        return remote(
            token_part(self.buf, block, part),
            self.land.at[LANDS[i], pl.ds(row, rows), pl.ds(0, cols)],
            self.sends,
            self.recvs,
            i,
            device(self.where, negative(step)),
        )

    def take(self, i):
        if i in self.got:
            return
        self.got.add(i)
        owner, ((row, rows), (col, cols)), _, _, _ = MOVES[i]
        self.move(i, True).wait_recv()
        at = (shard_at(self.where, owner), pl.ds(row, rows), pl.ds(col, cols))
        total = self.buf[at].astype(F32) + self.land[LANDS[i], pl.ds(row, rows), pl.ds(0, cols)].astype(F32)
        self.buf[at] = total.astype(BF)

    def turn(self, i):
        for j in FED[i]:
            self.take(j)
        self.move(i).start()

    def take_all(self):
        for i in reversed(TURNS):
            self.take(i)

    def finish(self):
        for i in reversed(TURNS):
            self.take(i)
        for i in reversed(TURNS):
            self.move(i).wait_send()

    def run(self):
        for i in reversed(TURNS):
            self.turn(i)
        self.finish()


ALONG = ((0, 0, 0, 1, 0), (0, 0, 0, 3, 0), (0, 0, 0, 2, 0))
SLAB_HOPS = (NEAR,) + ALONG + ALONG + (TWIN,)
SLAB_COUNT = 10
REP_NEIGHBOURS = (NEAR, TWIN) + ALONG


def spot(where, offset=HERE):
    near, north = shift(where, offset)[2:4]
    return near * 4 + north


def both(a, b):
    return tuple(p + q for p, q in zip(a, b))


class Spread:
    def __init__(self, where, cuts, ref, own_sem, first_sends, first_recvs, sends, recvs):
        self.where, self.cuts, self.ref, self.own_sem = where, cuts, ref, own_sem
        self.first_sends, self.first_recvs = first_sends, first_recvs
        self.slabs = RingGather(where, ref, sends, recvs)

    def first(self, n, offset, arriving=False):
        me = shard_at(self.where)
        owner = shard_at(self.where, negative(offset)) if arriving else me
        copies = []
        for j, (src, (col, cols)) in enumerate(self.cuts(shard_at(self.where, offset))):
            copies.append(
                remote(
                    src,
                    self.ref.at[owner, spot(self.where), self.where[4], :, pl.ds(col, cols)],
                    self.first_sends,
                    self.first_recvs,
                    (n, j),
                    device(self.where, offset),
                )
            )
        return copies

    def own(self):
        me = shard_at(self.where)
        return [
            pltpu.make_async_copy(
                src,
                self.ref.at[me, spot(self.where), self.where[4], :, pl.ds(col, cols)],
                self.own_sem.at[j],
            )
            for j, (src, (col, cols)) in enumerate(self.cuts(me))
        ]

    def begin(self):
        for n, offset in enumerate(PEERS):
            for copy in self.first(n, offset):
                copy.start()
        for copy in self.own():
            copy.start()

    def middle(self):
        for copy in self.own():
            copy.wait()
        for n, offset in enumerate(PEERS):
            for copy in self.first(n, offset, True):
                copy.wait_recv()

    def finish(self, taken=False):
        self.slabs.finish(taken)
        for n, offset in enumerate(PEERS):
            for copy in self.first(n, offset):
                copy.wait_send()

    def turn(self, i):
        self.slabs.turn(i)


def slab_span(ref, first, count):
    size = ref.shape[0]
    start, stop = first * size // GROUP, (first + count) * size // GROUP
    return pl.ds(start, stop - start)


class SlabGather:
    TURNS = (0, 0.6, 4.2)

    def __init__(self, where, ref, sends, recvs):
        self.where, self.ref, self.sends, self.recvs = where, ref, sends, recvs
        self.done = 0

    def hop(self, i, arriving=False):
        step = SLAB_HOPS[i]
        core = self.where[4]
        if step == TWIN:
            part = self.ref.at[:, :, (1 - core) if arriving else core]
        else:
            base = NEAR if 4 <= i < 7 else HERE
            owner = both(base, negative(step)) if arriving else base
            part = self.ref.at[:, spot(self.where, owner), core]
        return remote(part, part, self.sends, self.recvs, i, device(self.where, step))

    def turn(self, stage):
        assert stage == self.done
        self.done += 1
        if stage == 0:
            for i in range(4):
                self.hop(i).start()
        elif stage == 1:
            self.hop(0, True).wait_recv()
            for i in range(4, 7):
                self.hop(i).start()
        else:
            for i in range(1, 7):
                self.hop(i, True).wait_recv()
            self.hop(7).start()

    def take_all(self):
        self.hop(7, True).wait_recv()

    def finish(self, taken=False):
        if not taken:
            self.take_all()
        for i in range(len(SLAB_HOPS)):
            self.hop(i).wait_send()


class RingGather:
    TURNS = (0, 0.6, 1.2, 2.3, 3.4)
    NORTH, SOUTH = ALONG[:2]
    HOPS = (
        (NEAR, HERE, 0),
        (NORTH, HERE, 0),
        (SOUTH, HERE, 0),
        (NORTH, NEAR, 0),
        (SOUTH, NEAR, 0),
        (NORTH, HERE, 1),
        (SOUTH, HERE, 1),
        (NORTH, NEAR, 1),
        (SOUTH, NEAR, 1),
        (TWIN, HERE, 2),
    )

    def __init__(self, where, ref, sends, recvs):
        self.where, self.ref, self.sends, self.recvs = where, ref, sends, recvs
        self.done = 0
        self.cut = ref.shape[0] - ref.shape[0] // 2

    def hop(self, i, arriving=False):
        (step, base, kind), core = self.HOPS[i], self.where[4]
        if kind == 2:
            part = self.ref.at[:, :, (1 - core) if arriving else core]
        else:
            owner = both(base, negative(step)) if kind else base
            if arriving:
                owner = both(owner, negative(step))
            blocks = slice(None)
            if kind:
                blocks = (
                    pl.ds(0, self.cut)
                    if step == self.NORTH
                    else pl.ds(self.cut, self.ref.shape[0] - self.cut)
                )
            part = self.ref.at[blocks, spot(self.where, owner), core]
        return remote(part, part, self.sends, self.recvs, i, device(self.where, step))

    def turn(self, stage):
        assert stage == self.done
        self.done += 1
        waits, starts = (
            ((), (0, 1, 2)),
            ((0,), (3, 4)),
            ((1, 2), (5, 6)),
            ((3, 4), (7, 8)),
            ((5, 6, 7, 8), (9,)),
        )[stage]
        for i in waits:
            self.hop(i, True).wait_recv()
        for i in starts:
            self.hop(i).start()

    def take_all(self):
        self.hop(9, True).wait_recv()

    def finish(self, taken=False):
        if not taken:
            self.take_all()
        for i in range(10):
            self.hop(i).wait_send()


class SlabScatter:
    TURNS = (0, 1.0, 5.5)

    def __init__(self, where, ref, twin, land, sends, recvs):
        self.where, self.ref, self.twin, self.land = where, ref, twin, land
        self.sends, self.recvs = sends, recvs
        self.done = 0

    def hop(self, i, arriving=False):
        step = SLAB_HOPS[i]
        core = self.where[4]
        if step == TWIN:
            src, dst = self.ref.at[:, :, 1 - core], self.twin
        else:
            base = NEAR if 4 <= i < 7 else HERE
            src = self.ref.at[:, spot(self.where, both(base, step)), core]
            dst = self.land.at[i]
        return remote(src, dst, self.sends, self.recvs, i, device(self.where, step))

    def add(self, at, lands):
        core = self.where[4]
        rows = self.ref.shape[0]

        @pl.loop(0, rows)
        def _(n):
            total = self.ref[n, at, core].astype(F32)
            for i in lands:
                total = total + self.land[i, n].astype(F32)
            self.ref[n, at, core] = total.astype(BF)

    def turn(self, stage):
        assert stage == self.done
        self.done += 1
        if stage == 0:
            self.hop(7).start()
        elif stage == 1:
            core = self.where[4]
            self.hop(7, True).wait_recv()
            rows = self.ref.shape[0]

            @pl.loop(0, rows)
            def _(n):
                total = self.ref[n, :, core].astype(F32) + self.twin[n].astype(F32)
                self.ref[n, :, core] = total.astype(BF)

            for i in range(1, 7):
                self.hop(i).start()
        else:
            for i in range(4, 7):
                self.hop(i, True).wait_recv()
            self.add(spot(self.where, NEAR), (4, 5, 6))
            self.hop(0).start()

    def close(self):
        for i in range(4):
            self.hop(i, True).wait_recv()
        self.add(spot(self.where), (0, 1, 2, 3))

    def finish(self):
        for i in range(len(SLAB_HOPS)):
            self.hop(i).wait_send()

    def total(self):
        return self.ref.at[:, spot(self.where), self.where[4]]


def scatter_scratch(n, cols):
    return [pltpu.VMEM((n, 8, SLAB, cols), BF), pltpu.VMEM((7, n, SLAB, cols), BF)]


def spread_scratch(cuts):
    return [DMA((cuts,)), DMA((7, cuts)), DMA((7, cuts)), DMA((SLAB_COUNT,)), DMA((SLAB_COUNT,))]


def qkv_cuts(w_ref, rep):
    rows = pl.ds(pl.multiple_of(rep * SLAB, SLAB), SLAB)

    def cuts(shard):
        return [
            (
                w_ref.at[rows, pl.ds(pl.multiple_of(j * WIDTH + shard * LOCAL, LOCAL), LOCAL)],
                (j * LOCAL, LOCAL),
            )
            for j in range(3)
        ]

    return cuts


def hidden_start(shard):
    return (shard // 2) * (2 * LOCAL_FF) + lax.rem(shard, 2) * (5 * 128)


def gate_up_cuts(gate_ref, up_ref, rep):
    rows = pl.ds(pl.multiple_of(rep * SLAB, SLAB), SLAB)

    def cuts(shard):
        cols = pl.ds(pl.multiple_of(hidden_start(shard), 128), HID)
        return [(gate_ref.at[rows, cols], (0, HID)), (up_ref.at[rows, cols], (HID, HID))]

    return cuts


def standardize(values):
    center = values - jnp.mean(values, -1, keepdims=True)
    inverse = lax.rsqrt(jnp.mean(center * center, -1, keepdims=True) + EPS)
    return (center * inverse, inverse)


def normalize(values, gain, shift_):
    scaled, inverse = standardize(values)
    return (scaled * gain + shift_, scaled, inverse)


def normalize_back(grad, gain, scaled, inverse):
    weighted = grad * gain
    return inverse * (
        weighted
        - jnp.mean(weighted, -1, keepdims=True)
        - scaled * jnp.mean(weighted * scaled, -1, keepdims=True)
    )


def small_row(small_ref, row):
    return jnp.concatenate([small_ref[s, row : row + 1, :] for s in range(GROUP)], axis=1)


def rotary_tables():
    positions = np.arange(TOTAL, dtype=np.float32)
    freqs = np.float32(BASE) ** (-np.arange(0, ROT, 2).astype(np.float32) / np.float32(ROT))
    angles = positions[:, None] * freqs[None, :].astype(np.float32)
    cosine, sine = np.cos(angles).astype(np.float32), np.sin(angles).astype(np.float32)
    half = ROT // 2
    one = np.ones((TOTAL, HEAD_DIM), np.float32)
    low, high = np.zeros((TOTAL, HEAD_DIM), np.float32), np.zeros((TOTAL, HEAD_DIM), np.float32)
    one[:, :half], one[:, half:ROT] = cosine, cosine
    low[:, :half] = -sine
    high[:, half:ROT] = sine
    return np.stack([np.concatenate([t, t], 1) for t in (one, low, high)])


def turned(values, table_ref, rows, sign):
    parts = []
    for side in range(2):
        part = values[:, side * 128 : (side + 1) * 128]
        swing = pltpu.roll(part, 128 - ROT // 2, 1) * table_ref[1, rows, :] + (
            pltpu.roll(part, ROT // 2, 1) * table_ref[2, rows, :]
        )
        straight = part * table_ref[0, rows, :]
        parts.append(straight + swing if sign > 0 else straight - swing)
    return jnp.concatenate(parts, axis=1)


def chunk_rows(i):
    return pl.ds(pl.multiple_of(i * CHUNK, CHUNK), CHUNK)


def token_chunk(ref, i):
    return ref[pl.ds(i * 2, 2)].reshape(CHUNK, WIDTH)


def bias_row(small_ref, shard, j):
    block = j * GROUP + shard
    return small_ref[block // 3, pl.ds(4 + lax.rem(block, 3), 1), :]


def project(shard, tokens_ref, w_ref, small_ref, table_ref, q_ref, k_ref, v_ref, first, last):
    @pl.loop(first, last, unroll=2)
    def _(i):
        rows = chunk_rows(i)
        tokens = token_chunk(tokens_ref, i)
        for j, ref in enumerate((q_ref, k_ref, v_ref)):
            w = w_ref[:, :, :, :, j * LOCAL : (j + 1) * LOCAL].reshape(WIDTH, LOCAL)
            value = dot(tokens, w) + bias_row(small_ref, shard, j)
            if j < 2:
                value = turned(value, table_ref, rows, 1)
            if j == 0:
                value = value * HEAD_DIM ** (-0.5)
            ref[rows, :] = value.astype(BF)


def head_lanes(h):
    return lax.broadcasted_iota(jnp.int32, (CHUNK, LOCAL), 1) // HEAD_DIM == h


def key_parts(i):
    last = (CHUNK * i, CHUNK * (i + 1), True)
    return ((0, CHUNK * i, False), last) if i else (last,)


def hide_later(values, hidden):
    shape = values.shape
    keys = lax.broadcasted_iota(jnp.int32, shape, 0)
    return jnp.where(keys <= lax.broadcasted_iota(jnp.int32, shape, 1), values, hidden)


def attend(q_ref, k_ref, v_ref, vt_ref, mixed_ref, att_ref, lse_ref, poll):
    vt_ref[...] = v_ref[...].astype(F32).T.astype(BF)
    for i in range(CHUNKS):
        cols = slice(CHUNK * i, CHUNK * (i + 1))

        @pl.loop(0, LOCAL_HEADS, unroll=LOCAL_HEADS)
        def _(h):
            query = jnp.where(head_lanes(h), q_ref[cols, :], jnp.zeros((), BF))
            lanes = pl.ds(pl.multiple_of(h * HEAD_DIM, HEAD_DIM), HEAD_DIM)
            scores = []
            for first, last, diagonal in key_parts(i):
                part = dot_nt(k_ref[first:last, :], query)
                scores.append(hide_later(part, -1e30) if diagonal else part)
            top = functools.reduce(jnp.maximum, [jnp.max(s, 0, keepdims=True) for s in scores])
            expo = [jnp.exp(s - top) for s in scores]
            denom = sum(jnp.sum(e, 0, keepdims=True) for e in expo)
            share = 1.0 / denom
            mixed_ref[lanes, cols] = sum(
                dot(vt_ref[lanes, first:last], (e * share).astype(BF))
                for e, (first, last, _) in zip(expo, key_parts(i))
            )
            lse_ref[pl.ds(h, 1), cols] = top + jnp.log(denom)

        att_ref[cols, :] = mixed_ref[:, cols].T.astype(BF)
        poll(i)


def attend_back(q_ref, k_ref, v_ref, da_ref, lse_ref, kt_ref, dqt_ref, dk_ref, dv_ref, poll):
    kt_ref[...] = k_ref[...].astype(F32).T.astype(BF)
    dk_ref[...] = jnp.zeros_like(dk_ref)
    dv_ref[...] = jnp.zeros_like(dv_ref)
    for i in range(CHUNKS):
        cols = slice(CHUNK * i, CHUNK * (i + 1))

        @pl.loop(0, LOCAL_HEADS, unroll=LOCAL_HEADS)
        def _(h):
            query = jnp.where(head_lanes(h), q_ref[cols, :], jnp.zeros((), BF))
            grad = jnp.where(head_lanes(h), da_ref[cols, :], jnp.zeros((), BF))
            lanes = pl.ds(pl.multiple_of(h * HEAD_DIM, HEAD_DIM), HEAD_DIM)
            top = lse_ref[pl.ds(h, 1), cols]
            probs, grad_probs = [], []
            for first, last, diagonal in key_parts(i):
                part = jnp.exp(dot_nt(k_ref[first:last, :], query) - top)
                probs.append(hide_later(part, 0.0) if diagonal else part)
                grad_probs.append(dot_nt(v_ref[first:last, :], grad))
            total = sum(jnp.sum(g * p, 0, keepdims=True) for g, p in zip(grad_probs, probs))
            pieces = []
            for p, g, (first, last, _) in zip(probs, grad_probs, key_parts(i)):
                grad_scores = (p * (g - total)).astype(BF)
                dv_ref[first:last, :] += dot(p.astype(BF), grad)
                dk_ref[first:last, :] += dot(grad_scores, query)
                pieces.append(dot(kt_ref[lanes, first:last], grad_scores))
            dqt_ref[lanes, cols] = sum(pieces)

        poll(i)


def times(left_ref, w_ref, out_ref, first=0, last=CHUNKS):
    @pl.loop(first, last, unroll=2)
    def _(i):
        left = left_ref[chunk_rows(i), :]
        for j in range(WIDTH // 512):
            cols = slice(j * 512, (j + 1) * 512)
            out_ref[pl.ds(i * 2, 2), :, cols] = (
                dot(left, w_ref[:, cols]).astype(BF).reshape(2, ROWS, 512)
            )


def times_back(left_ref, w_ref, out_ref):
    depth = left_ref.shape[1]

    @pl.loop(0, CHUNKS, unroll=2)
    def _(i):
        left = left_ref[chunk_rows(i), :]
        for j in range(GROUP):
            w = w_ref[j].reshape(LOCAL, depth)
            out_ref[pl.ds(i * 2, 2), :, j * LOCAL : (j + 1) * LOCAL] = (
                dot_nt(left, w).astype(BF).reshape(2, ROWS, LOCAL)
            )


def feed_forward(shard, tokens_ref, grads_ref, w_ref, down_ref, hid_ref, dgu_ref, j):
    odd = lax.rem(shard, 2)
    cols = slice(j * CHUNK, (j + 1) * CHUNK)
    late = slice(HID + j * CHUNK, HID + (j + 1) * CHUNK)

    @pl.loop(0, CHUNKS, unroll=2)
    def _(i):
        rows = chunk_rows(i)
        tokens, grads = token_chunk(tokens_ref, i), token_chunk(grads_ref, i)
        gate = dot(tokens, w_ref[:, :, :, :, cols].reshape(WIDTH, CHUNK))
        up = dot(tokens, w_ref[:, :, :, :, late].reshape(WIDTH, CHUNK))
        grad = dot_nt(grads, down_ref[cols, :])
        unit = lax.broadcasted_iota(jnp.int32, (CHUNK, CHUNK), 1) + (j * CHUNK - 64 * odd)
        mine = jnp.logical_and(unit >= 0, unit < LOCAL_FF)
        sigma = 1.0 / (1.0 + jnp.exp(-gate))
        silu = gate * sigma
        hid_ref[rows, cols] = jnp.where(mine, silu * up, 0.0).astype(BF)
        grad_gate = grad * up * (sigma * (1.0 + gate * (1.0 - sigma)))
        dgu_ref[rows, cols] = jnp.where(mine, grad_gate, 0.0).astype(BF)
        dgu_ref[rows, late] = jnp.where(mine, grad * silu, 0.0).astype(BF)


def outer(left_ref, right_ref, out_ref, first=0, last=None):
    depth = out_ref.shape[-1]
    size = 512 if depth % 512 == 0 else depth if depth < 512 else 256
    last = left_ref.shape[-1] // LOCAL if last is None else last

    @pl.loop(first, last, unroll=2)
    def _(m):
        cols = pl.ds(pl.multiple_of(m * LOCAL, LOCAL), LOCAL)
        if len(left_ref.shape) == 3:
            left = left_ref[:, :, cols].reshape(TOTAL, LOCAL)
        else:
            left = left_ref[:, cols]
        left = left.astype(F32).T.astype(BF)
        for j in range(depth // size):
            part = slice(j * size, (j + 1) * size)
            if len(right_ref.shape) == 3:
                right = right_ref[:, :, part].reshape(TOTAL, size)
            else:
                right = right_ref[:, part]
            out_ref[m, :, :, :, part] = dot(left, right).astype(BF).reshape(8, 2, SLAB, size)


class Return:
    def __init__(self, where, part, out, kind, own_sem, first_sends, first_recvs, sends, recvs):
        self.where, self.part, self.out, self.own_sem = where, part, out, own_sem
        self.first_sends, self.first_recvs = first_sends, first_recvs
        self.slabs = kind(where, out, sends, recvs)

    def first(self, n, offset, arriving=False):
        me = shard_at(self.where)
        source = shard_at(self.where, negative(offset)) if arriving else me
        return remote(
            self.part(shard_at(self.where, offset)),
            self.out.at[source, spot(self.where), self.where[4]],
            self.first_sends,
            self.first_recvs,
            n,
            device(self.where, offset),
        )

    def begin(self):
        for n, offset in enumerate(PEERS):
            self.first(n, offset).start()
        self.own().start()

    def own(self):
        me = shard_at(self.where)
        return pltpu.make_async_copy(
            self.part(me), self.out.at[me, spot(self.where), self.where[4]], self.own_sem
        )

    def middle(self):
        self.own().wait()
        for n, offset in enumerate(PEERS):
            self.first(n, offset, True).wait_recv()

    def turn(self, i):
        self.slabs.turn(i)

    def finish(self):
        self.slabs.finish()
        for n, offset in enumerate(PEERS):
            self.first(n, offset).wait_send()


class Vectors:
    ROUNDS = ((TWIN,), (NEAR,), ALONG)

    def __init__(self, where, msg, land, mine, round_land, first_sends, first_recvs, sends, recvs):
        self.where, self.msg, self.land, self.mine, self.round_land = where, msg, land, mine, round_land
        self.first_sends, self.first_recvs = first_sends, first_recvs
        self.sends, self.recvs = sends, recvs

    def first(self, n, offset, arriving=False):
        me = shard_at(self.where)
        source = shard_at(self.where, negative(offset)) if arriving else me
        return remote(
            self.msg.at[shard_at(self.where, offset)],
            self.land.at[source],
            self.first_sends,
            self.first_recvs,
            n,
            device(self.where, offset),
        )

    def begin(self):
        me = shard_at(self.where)
        for n, offset in enumerate(PEERS):
            self.first(n, offset).start()
        self.land[me] = self.msg[me]

    def middle(self):
        me = shard_at(self.where)
        for n, offset in enumerate(PEERS):
            self.first(n, offset, True).wait_recv()
        total = self.land[0]
        for source in range(1, GROUP):
            total = total + self.land[source]
        self.mine[0] = total
        for p in range(3):
            block = 3 * me + p
            self.mine[0, 4 + p : 5 + p, :] = self.land[lax.rem(block, GROUP), pl.ds(4 + block // GROUP, 1), :]

    def hop(self, n, i, step):
        return remote(self.mine.at[n], self.round_land.at[i], self.sends, self.recvs, i, device(self.where, step))

    def round(self, n):
        base = sum(len(r) for r in self.ROUNDS[:n])
        for i, step in enumerate(self.ROUNDS[n]):
            self.hop(n, base + i, step).start()
        total = self.mine[n]
        for i, step in enumerate(self.ROUNDS[n]):
            self.hop(n, base + i, step).wait_recv()
            total = total + self.round_land[base + i]
        self.mine[n + 1] = total

    def finish(self):
        for n, offset in enumerate(PEERS):
            self.first(n, offset).wait_send()
        for n, steps in enumerate(self.ROUNDS):
            base = sum(len(r) for r in self.ROUNDS[:n])
            for i, step in enumerate(steps):
                self.hop(n, base + i, step).wait_send()


VECTOR_SCRATCH = [
    pltpu.VMEM((GROUP, 8, LOCAL), F32),
    pltpu.VMEM((GROUP, 8, LOCAL), F32),
    pltpu.VMEM((4, 8, LOCAL), F32),
    pltpu.VMEM((5, 8, LOCAL), F32),
    DMA((7,)),
    DMA((7,)),
    DMA((5,)),
    DMA((5,)),
]


def params(cid=None, mib=56):
    if cid is None:
        return pltpu.CompilerParams(vmem_limit_bytes=mib * 2**20)
    return pltpu.CompilerParams(
        collective_id=cid, has_side_effects=True, vmem_limit_bytes=mib * 2**20
    )


class Copies:
    def __init__(self, sems):
        self.sems, self.flying = sems, {}

    def start(self, name, src, dst):
        copy = pltpu.make_async_copy(src, dst, self.sems.at[len(self.flying)])
        copy.start()
        self.flying[name] = [copy, False]

    def wait(self, *names):
        for name in names:
            entry = self.flying[name]
            if not entry[1]:
                entry[0].wait()
                entry[1] = True

    def finish(self):
        self.wait(*self.flying)


def front_kernel(
    x_ref, small_ref, table_ref, ow_ref, qkv_ref, gate_ref, up_ref, gy_ref,
    all_small, mid_ref, a1_out, a2_out, gy_out, wqkv_out, wgu_out, q_out, k_out, v_out, att_out, lse_out,
    a1, w_qkv, own_two, q, k, v, att, lse, vt, mixed, buf, land, local_sems, *sems,
):
    where = place()
    greet(where, PEERS + REP_NEIGHBOURS)
    me, rep = shard_at(where), rep_at(where)
    local = Copies(local_sems)

    def small(n, offset, arriving=False):
        owner = shard_at(where, negative(offset)) if arriving else me
        return remote(small_ref, all_small.at[owner], sems[0], sems[1], n, device(where, offset))

    for n, offset in enumerate(PEERS):
        small(n, offset).start()
    all_small[me] = small_ref[...]
    spread_qkv = Spread(where, qkv_cuts(qkv_ref, rep), w_qkv, *sems[2:7])
    spread_gu = Spread(where, gate_up_cuts(gate_ref, up_ref, rep), wgu_out, *sems[7:12])
    one = Gather(where, a1, *sems[12:14])
    two = Gather(where, a2_out, *sems[14:16], own=own_two)
    grads = Gather(where, gy_out, *sems[16:18], own=gy_ref)
    scatter = Scatter(where, buf, land, *sems[18:20])
    spread_qkv.begin()
    scaled, _ = standardize(x_ref[...].astype(F32))
    for n, offset in enumerate(PEERS):
        small(n, offset, True).wait_recv()
    a1[me] = (scaled * small_row(all_small, 0) + small_row(all_small, 1)).astype(BF)
    plan = Agenda()
    plan.add(agenda(one, TOKEN_TURNS, 0, 5))
    plan.until(1.0)
    spread_gu.begin()
    local.start("gy", gy_ref.at[0], gy_out.at[me])
    spread_qkv.middle()
    plan.add(slab_agenda(spread_qkv, 4, 4))
    plan.until(19)
    spread_gu.middle()
    plan.add(slab_agenda(spread_gu, 22, 8))
    plan.until(25)
    one.take_all()
    plan.add(agenda(grads, TOKEN_TURNS, 26, 5))
    plan.until(37)
    spread_qkv.slabs.take_all()
    local.start("a1", a1, a1_out)
    local.start("w_qkv", w_qkv, wqkv_out)
    for half in range(2):
        project(me, a1, w_qkv, all_small, table_ref, q, k, v, 2 * half, 2 * half + 2)
        plan.until(40 + 3 * half)
    attend(q, k, v, vt, mixed, att, lse, lambda i: plan.until(44 + 2 * i))
    for name, src, dst in (("q", q, q_out), ("k", k, k_out), ("v", v, v_out), ("att", att, att_out), ("lse", lse, lse_out)):
        local.start(name, src, dst)
    times(att, ow_ref, buf)
    plan.until(52)
    plan.add(agenda(scatter, TOKEN_TURNS, 53, 5, True))
    plan.until(80)
    scatter.take_all()
    mid = x_ref[...].astype(F32) + buf[me].astype(F32)
    mid_ref[...] = mid
    normed, _, _ = normalize(mid, small_row(all_small, 2), small_row(all_small, 3))
    own_two[0] = normed.astype(BF)
    plan.add(agenda(two, TOKEN_TURNS, 80, 5))
    plan.until(81)
    local.start("own_two", own_two.at[0], a2_out.at[me])
    plan.until(1000)
    spread_qkv.finish(True)
    for mover in (one, two, grads, scatter, spread_gu):
        mover.finish()
    for n, offset in enumerate(PEERS):
        small(n, offset).wait_send()
    local.finish()


def front(x, small, table, out_weight, qkv_weight, gate_weight, up_weight, gy):
    sds = jax.ShapeDtypeStruct
    tokens = sds((GROUP, ROWS, WIDTH), BF)
    head = sds((TOTAL, LOCAL), BF)
    token_sems = [DMA((COUNT,))] * 2
    return pl.pallas_call(
        front_kernel,
        out_shape=(
            sds((GROUP, 8, LOCAL), F32),
            sds((ROWS, WIDTH), F32),
            tokens,
            tokens,
            tokens,
            sds((GROUP, 8, 2, SLAB, 3 * LOCAL), BF),
            sds((GROUP, 8, 2, SLAB, 2 * HID), BF),
            head,
            head,
            head,
            head,
            sds((8, TOTAL), F32),
        ),
        in_specs=[VM] * 4 + [ANY] * 3 + [VM],
        out_specs=(VM, VM) + (ANY,) * 10,
        scratch_shapes=[
            pltpu.VMEM((GROUP, ROWS, WIDTH), BF),
            pltpu.VMEM((GROUP, 8, 2, SLAB, 3 * LOCAL), BF),
            pltpu.VMEM((1, ROWS, WIDTH), BF),
            *[pltpu.VMEM((TOTAL, LOCAL), BF)] * 4,
            pltpu.VMEM((8, TOTAL), F32),
            pltpu.VMEM((LOCAL, TOTAL), BF),
            pltpu.VMEM((LOCAL, TOTAL), F32),
            pltpu.VMEM((GROUP, ROWS, WIDTH), BF),
            pltpu.VMEM((LANDINGS, ROWS, FAR_COLS), BF),
            DMA((9,)),
            DMA((7,)),
            DMA((7,)),
        ]
        + spread_scratch(3)
        + spread_scratch(2)
        + token_sems * 4,
        compiler_params=params(0),
        name="front",
    )(x, small, table, out_weight, qkv_weight, gate_weight, up_weight, gy)


def middle_kernel(
    mid_ref, gy_own, small_ref, a2_in, gy_in, wgu_in, down_in,
    dmid_ref, sums_ref, dy_out, sgu_out, sdown_out, part_out,
    a2, gy, w, down, hid, dgu, buf, land, own, part, ggu, gdown, gu_0, gu_1, down_0, down_1, load_sems, local_sems, *sems,
):
    where = place()
    me, rep = shard_at(where), rep_at(where)
    odd = lax.rem(me, 2)
    loads = Copies(load_sems)

    def tile(j):
        for side in range(2):
            cols = pl.ds(side * HID + j * CHUNK, CHUNK)
            loads.start(("w", j, side), wgu_in.at[:, :, :, :, cols], w.at[:, :, :, :, cols])

    loads.start("a2", a2_in, a2)
    tile(0)
    loads.start("down", down_in, down.at[pl.ds(pl.multiple_of(64 * odd, 64), LOCAL_FF)])
    loads.start("gy", gy_in, gy)
    tile(1)
    tile(2)
    greet(where, NEIGHBOURS + REP_NEIGHBOURS)
    down[pl.ds(pl.multiple_of(LOCAL_FF * (1 - odd), 64), 64), :] = jnp.zeros((64, WIDTH), BF)
    loads.wait("a2", ("w", 0, 0), ("w", 0, 1), "down", "gy")
    for j in range(HID // CHUNK):
        if j:
            loads.wait(("w", j, 0), ("w", j, 1))
        feed_forward(me, a2, gy, w, down, hid, dgu, j)
    times_back(dgu, w, buf)
    scatter = Scatter(where, buf, land, *sems[0:2])
    gather = Gather(where, dy_out, *sems[2:4], own=own)
    local = Copies(local_sems)
    sum_gu = SlabScatter(where, ggu, gu_0, gu_1, *sems[4:6])
    sum_down = SlabScatter(where, gdown, down_0, down_1, *sems[6:8])
    plan = Agenda()
    plan.add(agenda(scatter, TOKEN_TURNS, 0, 5.5, True))
    plan.until(0.9)
    time = 0
    for m in range(GROUP):
        outer(a2, dgu, ggu, m, m + 1)
        time += 1.5
        plan.until(time)
    sum_gu.turn(0)
    for m in range(3):
        outer(hid, gy, gdown, m, m + 1)
        time += 2
        plan.until(time)
    sum_down.turn(0)
    plan.until(20)
    sum_gu.turn(1)
    plan.until(30)
    scatter.take_all()
    gain = small_row(small_ref, 2)
    _, scaled, inverse = normalize(mid_ref[...], gain, small_row(small_ref, 3))
    grad = buf[me].astype(F32)
    dmid = gy_own[0].astype(F32) + normalize_back(grad, gain, scaled, inverse)
    own[0] = dmid.astype(BF)
    plan.add(agenda(gather, TOKEN_TURNS, 32, 5.5))
    plan.until(34)
    local.start("own", own.at[0], dy_out.at[me])
    dmid_ref[...] = dmid
    sums_ref[0:1, :] = jnp.sum(grad * scaled, 0, keepdims=True)
    sums_ref[1:2, :] = jnp.sum(grad, 0, keepdims=True)
    sum_down.turn(1)
    plan.until(38)
    for n in range(CHUNKS):
        times(hid, down, part, n, n + 1)
        plan.until(40 + 2 * n)
    local.start("part", part, part_out)
    plan.until(54)
    sum_gu.turn(2)
    plan.until(56)
    sum_down.turn(2)
    plan.until(1000)
    gather.take_all()
    sum_gu.close()
    local.start("gu", sum_gu.total(), sgu_out)
    sum_down.close()
    local.start("down", sum_down.total(), sdown_out)
    for mover in (sum_gu, sum_down, gather, scatter, local):
        mover.finish()


def middle(mid, gy, small, a2, grads, w_gu, down_weight):
    sds = jax.ShapeDtypeStruct
    tokens = (GROUP, ROWS, WIDTH)
    return pl.pallas_call(
        middle_kernel,
        out_shape=(
            sds((ROWS, WIDTH), F32),
            sds((8, WIDTH), F32),
            sds(tokens, BF),
            sds((GROUP, SLAB, 2 * HID), BF),
            sds((3, SLAB, WIDTH), BF),
            sds(tokens, BF),
        ),
        in_specs=[VM] * 3 + [ANY] * 4,
        out_specs=(VM, VM) + (ANY,) * 4,
        scratch_shapes=[
            pltpu.VMEM(tokens, BF),
            pltpu.VMEM(tokens, BF),
            pltpu.VMEM((GROUP, 8, 2, SLAB, 2 * HID), BF),
            pltpu.VMEM((HID, WIDTH), BF),
            pltpu.VMEM((TOTAL, HID), BF),
            pltpu.VMEM((TOTAL, 2 * HID), BF),
            pltpu.VMEM(tokens, BF),
            pltpu.VMEM((LANDINGS, ROWS, FAR_COLS), BF),
            pltpu.VMEM((1, ROWS, WIDTH), BF),
            pltpu.VMEM(tokens, BF),
            pltpu.VMEM((GROUP, 8, 2, SLAB, 2 * HID), BF),
            pltpu.VMEM((3, 8, 2, SLAB, WIDTH), BF),
            *scatter_scratch(GROUP, 2 * HID),
            *scatter_scratch(3, WIDTH),
            DMA((9,)),
            DMA((4,)),
        ]
        + [DMA((COUNT,))] * 4
        + [DMA((SLAB_COUNT,))] * 4,
        compiler_params=params(1, 62),
        name="middle",
    )(mid, gy, small, a2, grads, w_gu, down_weight)


QKV_SPAN = (GROUP, 8, 2, SLAB, 3 * LOCAL)
HALF = 3 * LOCAL // 2
HALF_SPAN = (GROUP, 8, 2, SLAB, HALF)
GU_SPAN = (GROUP, 8, 2, SLAB, 2 * HID)
DOWN_SPAN = (3, 8, 2, SLAB, WIDTH)
OUT_SPAN = (4, 8, 2, SLAB, 512)


def back_kernel(
    x_ref, mid_ref, dmid_ref, small_ref, two_ref, table_ref, ow_ref,
    dy_in, a1_in, wqkv_in, q_in, k_in, v_in, att_in, lse_in, sgu_in, sdown_in, part_in,
    grad_ref, act_ref, vec_ref, gu_out, down_out, qkv_out, kv_out, out_out,
    toks, w, q, k, v, att, lse, da, kt, dqt, dk, dv, dqkv, buf, land,
    gqkv, gkv, gout, qkv_0, qkv_1, kv_0, kv_1, out_0, out_1, load_sems, own_sems, credit, *sems,
):
    where = place()
    me, rep = shard_at(where), rep_at(where)
    loads = Copies(load_sems)
    for name, src, dst in (
        ("part", part_in, buf), ("toks", dy_in, toks), ("q", q_in, q), ("k", k_in, k),
        ("v", v_in, v), ("lse", lse_in, lse), ("att", att_in, att), ("w", wqkv_in, w),
        ("down", sdown_in, down_out.at[:, spot(where), where[4]]),
    ):
        loads.start(name, src, dst)
    greet(where, PEERS + REP_NEIGHBOURS)
    down = Scatter(where, buf, land, *sems[0:2])
    one = Scatter(where, buf, land, *sems[2:4])
    sum_qkv = [
        SlabScatter(where, gqkv, qkv_0, qkv_1, *sems[4:6]),
        SlabScatter(where, gkv, kv_0, kv_1, *sems[28:30]),
    ]
    sum_out = SlabScatter(where, gout, out_0, out_1, *sems[6:8])
    back_gu = Return(where, lambda s: sgu_in.at[s], gu_out, RingGather, own_sems.at[0], *sems[8:12])
    back_qkv = [
        Return(
            where, lambda s: gqkv.at[s, spot(where), where[4]], qkv_out, SlabGather, own_sems.at[1], *sems[12:16]
        ),
        Return(
            where, lambda s: gkv.at[s, spot(where), where[4]], kv_out, SlabGather, own_sems.at[3], *sems[30:34]
        ),
    ]
    back_down = RingGather(where, down_out, *sems[16:18])
    back_out = RingGather(where, out_out, *sems[18:20])
    vectors = Vectors(where, *sems[20:28])
    plan = Agenda()
    back_gu.begin()
    loads.wait("part")
    plan.add(agenda(down, TOKEN_TURNS, 0, 6, True))
    plan.until(0.9)
    loads.wait("down")
    plan.add(slab_agenda(back_down, 1, 5))
    plan.until(1.5)
    loads.wait("toks")

    @pl.loop(0, CHUNKS, unroll=2)
    def _(i):
        da[chunk_rows(i), :] = dot_nt(token_chunk(toks, i), ow_ref[...]).astype(BF)

    back_gu.middle()
    plan.add(slab_agenda(back_gu, 5, 9))
    plan.until(5)
    loads.wait("q", "k", "v", "lse", "att")
    left = att[...].astype(F32).T.astype(BF)
    for n in range(4):
        right = toks[:, :, n * 512 : (n + 1) * 512].reshape(TOTAL, 512)
        gout[n] = dot(left, right).astype(BF).reshape(8, 2, SLAB, 512)
    loads.start("a1", a1_in, toks)
    plan.add([(7, sum_out, 0), (12, sum_out, 1), (30, sum_out, 2)])
    plan.until(7.5)
    attend_back(q, k, v, da, lse, kt, dqt, dk, dv, lambda i: plan.until(8.5 + 3 * i))
    plan.until(23)
    vectors.msg[...] = jnp.zeros_like(vectors.msg)
    for i in range(CHUNKS):
        rows = slice(i * CHUNK, (i + 1) * CHUNK)
        grad_q = dqt[:, rows].T * HEAD_DIM ** (-0.5)
        for j, value in enumerate((grad_q, dk[rows, :], dv[rows, :])):
            if j < 2:
                value = turned(value, table_ref, rows, -1)
            low = value.astype(BF)
            dqkv[rows, j * LOCAL : (j + 1) * LOCAL] = low
            vectors.msg[0, 4 + j : 5 + j, :] += jnp.sum(low.astype(F32), 0, keepdims=True)
    plan.until(25)
    loads.wait("a1", "w")
    outer(toks, dqkv.at[:, pl.ds(0, HALF)], gqkv)
    sum_qkv[0].turn(0)
    plan.until(29)
    outer(toks, dqkv.at[:, pl.ds(HALF, HALF)], gkv)
    sum_qkv[1].turn(0)
    plan.until(32)
    sum_qkv[0].turn(1)
    down.finish()
    for step in NEIGHBOURS:
        pl.semaphore_signal(credit, inc=1, device_id=device(where, step), device_id_type=MESH)
    act_ref[...] = (mid_ref[...] + buf[me].astype(F32)).astype(BF)
    times_back(dqkv, w, buf)
    sum_qkv[1].turn(1)
    pl.semaphore_wait(credit, len(NEIGHBOURS))
    plan.add(agenda(one, TOKEN_TURNS, 38, 5.5, True))
    plan.until(40)
    sum_out.close()
    out_own = pltpu.make_async_copy(
        sum_out.total(), out_out.at[:, spot(where), where[4]], own_sems.at[2]
    )
    out_own.start()
    plan.until(44)
    sum_qkv[0].turn(2)
    out_own.wait()
    plan.add(slab_agenda(back_out, 44, 4))
    plan.until(50)
    sum_qkv[0].close()
    back_qkv[0].begin()
    sum_qkv[1].turn(2)
    plan.until(53)
    back_qkv[0].middle()
    back_qkv[0].turn(0)
    plan.until(55)
    sum_qkv[1].close()
    back_qkv[1].begin()
    back_qkv[0].turn(1)
    plan.until(58)
    back_qkv[1].middle()
    back_qkv[1].turn(0)
    plan.until(62)
    one.take_all()
    gain = small_row(small_ref, 0)
    _, scaled, inverse = normalize(x_ref[...].astype(F32), gain, small_row(small_ref, 1))
    grad = buf[me].astype(F32)
    first, second = jnp.sum(grad * scaled, 0, keepdims=True), jnp.sum(grad, 0, keepdims=True)
    for d in range(GROUP):
        cols = slice(d * LOCAL, (d + 1) * LOCAL)
        vectors.msg[d, 0:1, :] = first[:, cols]
        vectors.msg[d, 1:2, :] = second[:, cols]
        vectors.msg[d, 2:4, :] = two_ref[0:2, cols]
        if d:
            vectors.msg[d, 4:7, :] = vectors.msg[0, 4:7, :]
    vectors.begin()
    back_qkv[1].turn(1)
    back_qkv[0].turn(2)
    grad_ref[...] = dmid_ref[...] + normalize_back(grad, gain, scaled, inverse)
    vectors.middle()
    vectors.round(0)
    vectors.round(1)
    vectors.round(2)
    vec_ref[...] = vectors.mine[3]
    plan.until(1000)
    back_qkv[1].turn(2)
    for mover in (one, *sum_qkv, sum_out, back_gu, back_down, back_out, *back_qkv, vectors):
        mover.finish()
    loads.finish()


def back(x, mid, dmid, small, sums_two, table, out_weight, dy, a1, w_qkv, q, k, v, att, lse, s_gu, s_down, part_down):
    sds = jax.ShapeDtypeStruct
    tokens = (GROUP, ROWS, WIDTH)
    slab_sems = [DMA((SLAB_COUNT,))] * 2
    return pl.pallas_call(
        back_kernel,
        out_shape=(
            sds((ROWS, WIDTH), F32),
            sds((ROWS, WIDTH), BF),
            sds((8, LOCAL), F32),
            *[sds(s, BF) for s in (GU_SPAN, DOWN_SPAN, HALF_SPAN, HALF_SPAN, OUT_SPAN)],
        ),
        in_specs=[VM] * 7 + [ANY] * 11,
        out_specs=(VM,) * 3 + (ANY,) * 5,
        scratch_shapes=[
            pltpu.VMEM(tokens, BF),
            pltpu.VMEM(QKV_SPAN, BF),
            *[pltpu.VMEM((TOTAL, LOCAL), BF)] * 4,
            pltpu.VMEM((8, TOTAL), F32),
            pltpu.VMEM((TOTAL, LOCAL), BF),
            pltpu.VMEM((LOCAL, TOTAL), BF),
            pltpu.VMEM((LOCAL, TOTAL), F32),
            pltpu.VMEM((TOTAL, LOCAL), F32),
            pltpu.VMEM((TOTAL, LOCAL), F32),
            pltpu.VMEM((TOTAL, 3 * LOCAL), BF),
            pltpu.VMEM(tokens, BF),
            pltpu.VMEM((LANDINGS, ROWS, FAR_COLS), BF),
            pltpu.VMEM(HALF_SPAN, BF),
            pltpu.VMEM(HALF_SPAN, BF),
            pltpu.VMEM(OUT_SPAN, BF),
            *scatter_scratch(GROUP, HALF),
            *scatter_scratch(GROUP, HALF),
            *scatter_scratch(4, 512),
            DMA((10,)),
            DMA((4,)),
            pltpu.SemaphoreType.REGULAR,
        ]
        + [DMA((COUNT,))] * 4
        + slab_sems * 2
        + ([DMA((7,))] * 2 + slab_sems) * 2
        + slab_sems * 2
        + VECTOR_SCRATCH
        + slab_sems
        + [DMA((7,))] * 2
        + slab_sems,
        compiler_params=params(2, 60),
        name="back",
    )(x, mid, dmid, small, sums_two, table, out_weight, dy, a1, w_qkv, q, k, v, att, lse, s_gu, s_down, part_down)


def unpack_kernel(odd_ref, gu_ref, qkv_ref, kv_ref, out_ref, down_ref, gate_out, up_out, qkv_out, out_out, down_out):
    for side, ref in enumerate((gate_out, up_out)):
        cols = slice(side * HID, (side + 1) * HID)
        for t in range(GROUP // 2):
            left, right = gu_ref[2 * t, :, cols].astype(F32), gu_ref[2 * t + 1, :, cols].astype(F32)
            ref[:, t * 2 * LOCAL_FF : (t + 1) * 2 * LOCAL_FF] = jnp.concatenate(
                [left[:, :640], left[:, 640:] + right[:, :128], right[:, 128:]], axis=1
            )
    for s in range(GROUP):
        for j in range(3):
            for part in range(2):
                cols = j * LOCAL + part * 128
                ref, at = (qkv_ref, cols) if cols < HALF else (kv_ref, cols - HALF)
                first = j * WIDTH + s * LOCAL + part * 128
                qkv_out[:, first : first + 128] = ref[s, :, at : at + 128].astype(F32)
    for n in range(4):
        out_out[:, n * 512 : (n + 1) * 512] = out_ref[n].astype(F32)
    rows = LOCAL_FF // 4
    first = pl.multiple_of(64 * odd_ref[0] + rows * pl.program_id(0), SLAB)
    down_out[...] = down_ref[pl.ds(first, rows), :].astype(F32)


def unpack(odd, g_gu, g_qkv, g_kv, g_out, g_down):
    sds = jax.ShapeDtypeStruct
    rows = LOCAL // 4
    return pl.pallas_call(
        unpack_kernel,
        grid_spec=pltpu.PrefetchScalarGridSpec(
            num_scalar_prefetch=1,
            grid=(4,),
            in_specs=[
                pl.BlockSpec((GROUP, rows, 2 * HID), lambda r, _: (0, r, 0)),
                *[pl.BlockSpec((GROUP, rows, HALF), lambda r, _: (0, r, 0))] * 2,
                pl.BlockSpec((4, rows, 512), lambda r, _: (0, r, 0)),
                pl.BlockSpec((HID, WIDTH), lambda r, _: (0, 0)),
            ],
            out_specs=[
                pl.BlockSpec((rows, FF), lambda r, _: (r, 0)),
                pl.BlockSpec((rows, FF), lambda r, _: (r, 0)),
                pl.BlockSpec((rows, 3 * WIDTH), lambda r, _: (r, 0)),
                pl.BlockSpec((rows, WIDTH), lambda r, _: (r, 0)),
                pl.BlockSpec((LOCAL_FF // 4, WIDTH), lambda r, _: (r, 0)),
            ],
        ),
        out_shape=(
            sds((LOCAL, FF), F32),
            sds((LOCAL, FF), F32),
            sds((LOCAL, 3 * WIDTH), F32),
            sds((LOCAL, WIDTH), F32),
            sds((LOCAL_FF, WIDTH), F32),
        ),
        compiler_params=params(),
        name="unpack",
    )(odd.reshape(1), g_gu, g_qkv, g_kv, g_out, g_down)


def shards(
    inputs,
    cotangent,
    ln1_gain,
    ln1_bias,
    qkv_weight,
    qkv_bias,
    out_weight,
    ln2_gain,
    ln2_bias,
    gate_weight,
    up_weight,
    down_weight,
):
    batch, length, width = inputs.shape
    odd = lax.rem(lax.axis_index("shard"), 2)
    table = jnp.asarray(rotary_tables())
    x = inputs.reshape(length, width)
    small, at = jnp.zeros((8 * LOCAL,), F32), 0
    for vector in (ln1_gain, ln1_bias, ln2_gain, ln2_bias, qkv_bias):
        small += jnp.pad(vector.astype(F32), (at, 8 * LOCAL - at - vector.shape[0]))
        at += vector.shape[0]
    small = small.reshape(8, LOCAL)
    all_small, mid, a1, a2, grads, w_qkv, w_gu, q, k, v, att, lse = front(
        x, small, table, out_weight, qkv_weight, gate_weight, up_weight, cotangent
    )
    dmid, sums_two, dy, s_gu, s_down, part_down = middle(
        mid, cotangent, all_small, a2, grads, w_gu, down_weight
    )
    input_grad, activations, vectors, g_gu, g_down, g_qkv, g_kv, g_out = back(
        x, mid, dmid, all_small, sums_two, table, out_weight, dy, a1, w_qkv, q, k, v, att, lse, s_gu, s_down, part_down
    )
    g_gate, g_up, g_qkv, g_out, g_down = unpack(
        odd,
        g_gu.reshape(GROUP, LOCAL, 2 * HID),
        g_qkv.reshape(GROUP, LOCAL, HALF),
        g_kv.reshape(GROUP, LOCAL, HALF),
        g_out.reshape(4, LOCAL, 512),
        g_down.reshape(HID, width),
    )
    return (
        activations.reshape(batch, length, width),
        input_grad.reshape(batch, length, width),
        vectors[0],
        vectors[1],
        g_qkv,
        vectors[4:7].reshape(3 * LOCAL),
        g_out,
        vectors[2],
        vectors[3],
        g_gate,
        g_up,
        g_down,
    )


def solution(mesh):
    tokens, vector, matrix = P("rep", "shard", None), P("shard"), P("shard", None)
    return jax.shard_map(
        shards,
        mesh=mesh,
        in_specs=(tokens, tokens, vector, vector, matrix, vector, matrix, vector, vector, matrix, matrix, matrix),
        out_specs=(tokens, tokens, vector, vector, matrix, vector, matrix, vector, vector, matrix, matrix, matrix),
        check_vma=False,
    )
```

```python
import functools

import jax
import jax.numpy as jnp
import numpy as np
from jax import lax
from jax.experimental import pallas as pl
from jax.experimental.pallas import tpu as pltpu
from jax.sharding import PartitionSpec as P

HEADS = 32
HEAD_DIM = 64
ROT = 16
WIDTH = 2048
GROUP = 8
REPS = 16
ROWS = 128
TOTAL = GROUP * ROWS
LOCAL = WIDTH // GROUP
LOCAL_HEADS = HEADS // GROUP
FF = 5632
LOCAL_FF = FF // GROUP
HID = 768
SLAB = LOCAL // REPS
NEAR_COLS, FAR_COLS = 768, 1280
CHUNK = 256
CHUNKS = TOTAL // CHUNK
EPS = 1e-05
BASE = 10000.0
BF = jnp.bfloat16
F32 = jnp.float32
MESH = pl.DeviceIdType.MESH
VM = pl.BlockSpec(memory_space=pltpu.VMEM)
ANY = pl.BlockSpec(memory_space=pl.ANY)
DMA = pltpu.SemaphoreType.DMA


def dot(left, right):
    return jnp.dot(left, right, preferred_element_type=F32)


def dot_nt(left, right):
    return lax.dot_general(left, right, (((1,), (1,)), ((), ())), preferred_element_type=F32)


FAR, UP, DOWN = (1, 0, 0, 0, 0), (0, 1, 0, 0, 0), (0, -1, 0, 0, 0)
NEAR, NORTH, SOUTH, TWIN = (0, 0, 1, 0, 0), (0, 0, 0, 1, 0), (0, 0, 0, -1, 0), (0, 0, 0, 0, 1)
HERE = (0, 0, 0, 0, 0)
SIZES = (2, 4, 2, 4, 2)
PEERS = tuple((f, z, 0, 0, 0) for f in range(2) for z in range(4) if (f, z) != (0, 0))


def place():
    shard, rep = lax.axis_index("shard"), lax.axis_index("rep")
    return (shard // 4, lax.rem(shard, 4), rep // 8, lax.rem(rep // 2, 4), lax.rem(rep, 2))


def shift(where, offset):
    return tuple(
        lax.rem(a + (o + 2 * n) % n, n) if o % n else a for a, o, n in zip(where, offset, SIZES)
    )


def shard_at(where, offset=HERE):
    far, level = shift(where, offset)[:2]
    return far * 4 + level


def rep_at(where, offset=HERE):
    near, north, core = shift(where, offset)[2:]
    return near * 8 + north * 2 + core


def device(where, offset):
    return (shard_at(where, offset), rep_at(where, offset))


def less(a, b):
    return tuple((p - q) % n for p, q, n in zip(a, b, SIZES))


def negative(a):
    return tuple(-p for p in a)


def greet(where, offsets):
    barrier = pltpu.get_barrier_semaphore()
    for offset in offsets:
        pl.semaphore_signal(
            barrier, inc=1, device_id=device(where, negative(offset)), device_id_type=MESH
        )
    pl.semaphore_wait(barrier, len(offsets))


def remote(src, dst, sends, recvs, i, to):
    return pltpu.make_async_remote_copy(
        src_ref=src,
        dst_ref=dst,
        send_sem=sends.at[i],
        recv_sem=recvs.at[i],
        device_id=to,
        device_id_type=MESH,
    )


def token_moves():
    moves = []

    def add(owner, part, step, first, turn, back):
        moves.append((owner, part, step, first, turn, back))
        return len(moves) - 1

    near, far = (0, NEAR_COLS), (NEAR_COLS, FAR_COLS)
    whole, top, low = (0, ROWS), (0, ROWS // 2), (ROWS // 2, ROWS // 2)
    up2 = (0, 2, 0, 0, 0)
    up = add(HERE, (whole, near), UP, None, 0, 15.5)
    down = add(HERE, (whole, near), DOWN, None, 0, 15.5)
    add(HERE, (whole, near), FAR, None, 0.2, 0.3)
    a = add(DOWN, (top, near), UP, up, 5.5, 7)
    b = add(UP, (low, near), DOWN, down, 5.5, 7)
    add(DOWN, (whole, near), FAR, up, 5.6, 0.2)
    add(UP, (whole, near), FAR, down, 5.6, 0.2)
    add(up2, (top, near), FAR, a, 10, 0)
    add(up2, (low, near), FAR, b, 10, 0)
    over = add(HERE, (whole, far), FAR, None, 0.1, 15)
    up = add(HERE, (whole, far), UP, None, 0.3, 9)
    down = add(HERE, (whole, far), DOWN, None, 0.3, 9)
    add(DOWN, (top, far), UP, up, 13, 0.1)
    add(UP, (low, far), DOWN, down, 13, 0.1)
    up = add(FAR, (whole, far), UP, over, 11.5, 6)
    down = add(FAR, (whole, far), DOWN, over, 11.5, 6)
    add(tuple(p + q for p, q in zip(FAR, DOWN)), (top, far), UP, up, 19.5, 0)
    add(tuple(p + q for p, q in zip(FAR, UP)), (low, far), DOWN, down, 19.5, 0)
    return tuple(moves)


MOVES = token_moves()
COUNT = len(MOVES)
TURNS = tuple(sorted(range(COUNT), key=lambda i: MOVES[i][4]))
BACK_TURNS = tuple(sorted(range(COUNT), key=lambda i: MOVES[i][5]))
FED = tuple(tuple(j for j in range(COUNT) if MOVES[j][3] == i) for i in range(COUNT))
NEIGHBOURS = (FAR, UP, DOWN)
LANDS = {}
for _i in range(COUNT):
    pair = MOVES[_i][1][0][0] > 0
    LANDS[_i] = LANDS[_i - 1] if pair else len(set(LANDS.values()))
LANDINGS = len(set(LANDS.values()))


def token_part(ref, block, part):
    (row, rows), (col, cols) = part
    return ref.at[block, pl.ds(row, rows), pl.ds(col, cols)]


class Gather:
    def __init__(self, where, ref, sends, recvs, own=None):
        self.where, self.ref, self.sends, self.recvs, self.own = where, ref, sends, recvs, own
        self.got = set()

    def move(self, i, arriving=False):
        owner, part, step = MOVES[i][:3]
        block = shard_at(self.where, less(owner, step) if arriving else owner)
        ref = token_part(self.ref, block, part)
        src = ref
        if owner == HERE and self.own is not None and not arriving:
            src = token_part(self.own, 0, part)
        return remote(src, ref, self.sends, self.recvs, i, device(self.where, step))

    def take(self, i):
        if i not in self.got:
            self.got.add(i)
            self.move(i, True).wait_recv()

    def turn(self, i):
        if MOVES[i][3] is not None:
            self.take(MOVES[i][3])
        self.move(i).start()

    def take_all(self):
        for i in TURNS:
            self.take(i)

    def settle(self):
        for i in TURNS:
            self.move(i).wait_send()

    def finish(self):
        self.take_all()
        self.settle()

    def run(self):
        for i in TURNS:
            self.turn(i)
        self.finish()


def agenda(mover, start):
    column = 5 if isinstance(mover, Scatter) else 4
    return [(start + MOVES[i][column], mover, i) for i in range(COUNT)]


def slab_agenda(mover, start, unit):
    turns = mover.slabs.TURNS if hasattr(mover, "slabs") else mover.TURNS
    return [(start + unit * t, mover, i) for i, t in enumerate(turns)]


class Agenda:
    def __init__(self):
        self.items = []

    def add(self, items):
        self.items = sorted(self.items + items, key=lambda e: e[0])

    def until(self, time):
        while self.items and self.items[0][0] <= time:
            _, mover, i = self.items.pop(0)
            mover.turn(i)


class Scatter:
    def __init__(self, where, buf, land, sends, recvs):
        self.where, self.buf, self.land, self.sends, self.recvs = where, buf, land, sends, recvs
        self.got = set()

    def move(self, i, arriving=False):
        owner, part, step = MOVES[i][:3]
        block = shard_at(self.where, owner if arriving else less(owner, step))
        (row, rows), (col, cols) = part
        return remote(
            token_part(self.buf, block, part),
            self.land.at[LANDS[i], pl.ds(row, rows), pl.ds(0, cols)],
            self.sends,
            self.recvs,
            i,
            device(self.where, negative(step)),
        )

    def take(self, i):
        if i in self.got:
            return
        self.got.add(i)
        owner, ((row, rows), (col, cols)) = MOVES[i][:2]
        self.move(i, True).wait_recv()
        at = (shard_at(self.where, owner), pl.ds(row, rows), pl.ds(col, cols))
        total = self.buf[at].astype(F32) + self.land[LANDS[i], pl.ds(row, rows), pl.ds(0, cols)].astype(F32)
        self.buf[at] = total.astype(BF)

    def turn(self, i):
        for j in FED[i]:
            self.take(j)
        self.move(i).start()

    def take_all(self):
        for i in BACK_TURNS:
            self.take(i)

    def settle(self):
        for i in BACK_TURNS:
            self.move(i).wait_send()

    def finish(self):
        self.take_all()
        self.settle()

    def run(self):
        for i in BACK_TURNS:
            self.turn(i)
        self.finish()


ALONG = ((0, 0, 0, 1, 0), (0, 0, 0, 3, 0), (0, 0, 0, 2, 0))
SLAB_HOPS = (NEAR,) + ALONG + ALONG + (TWIN,)
SLAB_COUNT = 10
REP_NEIGHBOURS = (NEAR, TWIN) + ALONG


def spot(where, offset=HERE):
    near, north = shift(where, offset)[2:4]
    return near * 4 + north


def both(a, b):
    return tuple(p + q for p, q in zip(a, b))


class Spread:
    def __init__(self, where, cuts, ref, own_sem, first_sends, first_recvs, sends, recvs):
        self.where, self.cuts, self.ref, self.own_sem = where, cuts, ref, own_sem
        self.first_sends, self.first_recvs = first_sends, first_recvs
        self.slabs = RingGather(where, ref, sends, recvs)

    def first(self, n, offset, arriving=False):
        me = shard_at(self.where)
        owner = shard_at(self.where, negative(offset)) if arriving else me
        copies = []
        for j, (src, (col, cols)) in enumerate(self.cuts(shard_at(self.where, offset))):
            copies.append(
                remote(
                    src,
                    self.ref.at[owner, spot(self.where), self.where[4], :, pl.ds(col, cols)],
                    self.first_sends,
                    self.first_recvs,
                    (n, j),
                    device(self.where, offset),
                )
            )
        return copies

    def own(self):
        me = shard_at(self.where)
        return [
            pltpu.make_async_copy(
                src,
                self.ref.at[me, spot(self.where), self.where[4], :, pl.ds(col, cols)],
                self.own_sem.at[j],
            )
            for j, (src, (col, cols)) in enumerate(self.cuts(me))
        ]

    def begin(self):
        for n, offset in enumerate(PEERS):
            for copy in self.first(n, offset):
                copy.start()
        for copy in self.own():
            copy.start()

    def middle(self):
        for copy in self.own():
            copy.wait()
        for n, offset in enumerate(PEERS):
            for copy in self.first(n, offset, True):
                copy.wait_recv()

    def finish(self, taken=False):
        self.slabs.finish(taken)
        for n, offset in enumerate(PEERS):
            for copy in self.first(n, offset):
                copy.wait_send()

    def turn(self, i):
        self.slabs.turn(i)


def slab_span(ref, first, count):
    size = ref.shape[0]
    start, stop = first * size // GROUP, (first + count) * size // GROUP
    return pl.ds(start, stop - start)


class SlabGather:
    TURNS = (0, 0.6, 4.2)

    def __init__(self, where, ref, sends, recvs):
        self.where, self.ref, self.sends, self.recvs = where, ref, sends, recvs
        self.done = 0

    def hop(self, i, arriving=False):
        step = SLAB_HOPS[i]
        core = self.where[4]
        if step == TWIN:
            part = self.ref.at[:, :, (1 - core) if arriving else core]
        else:
            base = NEAR if 4 <= i < 7 else HERE
            owner = both(base, negative(step)) if arriving else base
            part = self.ref.at[:, spot(self.where, owner), core]
        return remote(part, part, self.sends, self.recvs, i, device(self.where, step))

    def turn(self, stage):
        assert stage == self.done
        self.done += 1
        if stage == 0:
            for i in range(4):
                self.hop(i).start()
        elif stage == 1:
            self.hop(0, True).wait_recv()
            for i in range(4, 7):
                self.hop(i).start()
        else:
            for i in range(1, 7):
                self.hop(i, True).wait_recv()
            self.hop(7).start()

    def take_all(self):
        self.hop(7, True).wait_recv()

    def finish(self, taken=False):
        if not taken:
            self.take_all()
        for i in range(len(SLAB_HOPS)):
            self.hop(i).wait_send()


class RingGather:
    TURNS = (0, 0.6, 1.2, 2.3, 3.4)
    NORTH, SOUTH = ALONG[:2]
    HOPS = (
        (NEAR, HERE, 0),
        (NORTH, HERE, 0),
        (SOUTH, HERE, 0),
        (NORTH, NEAR, 0),
        (SOUTH, NEAR, 0),
        (NORTH, HERE, 1),
        (SOUTH, HERE, 1),
        (NORTH, NEAR, 1),
        (SOUTH, NEAR, 1),
        (TWIN, HERE, 2),
    )

    def __init__(self, where, ref, sends, recvs):
        self.where, self.ref, self.sends, self.recvs = where, ref, sends, recvs
        self.done = 0
        self.cut = ref.shape[0] - ref.shape[0] // 2

    def hop(self, i, arriving=False):
        (step, base, kind), core = self.HOPS[i], self.where[4]
        if kind == 2:
            part = self.ref.at[:, :, (1 - core) if arriving else core]
        else:
            owner = both(base, negative(step)) if kind else base
            if arriving:
                owner = both(owner, negative(step))
            blocks = slice(None)
            if kind:
                blocks = (
                    pl.ds(0, self.cut)
                    if step == self.NORTH
                    else pl.ds(self.cut, self.ref.shape[0] - self.cut)
                )
            part = self.ref.at[blocks, spot(self.where, owner), core]
        return remote(part, part, self.sends, self.recvs, i, device(self.where, step))

    def turn(self, stage):
        assert stage == self.done
        self.done += 1
        waits, starts = (
            ((), (0, 1, 2)),
            ((0,), (3, 4)),
            ((1, 2), (5, 6)),
            ((3, 4), (7, 8)),
            ((5, 6, 7, 8), (9,)),
        )[stage]
        for i in waits:
            self.hop(i, True).wait_recv()
        for i in starts:
            self.hop(i).start()

    def take_all(self):
        self.hop(9, True).wait_recv()

    def finish(self, taken=False):
        if not taken:
            self.take_all()
        for i in range(10):
            self.hop(i).wait_send()


class SlabScatter:
    TURNS = (0, 1.0, 5.5)

    def __init__(self, where, ref, twin, land, sends, recvs):
        self.where, self.ref, self.twin, self.land = where, ref, twin, land
        self.sends, self.recvs = sends, recvs
        self.done = 0

    def hop(self, i, arriving=False):
        step = SLAB_HOPS[i]
        core = self.where[4]
        if step == TWIN:
            src, dst = self.ref.at[:, :, 1 - core], self.twin
        else:
            base = NEAR if 4 <= i < 7 else HERE
            src = self.ref.at[:, spot(self.where, both(base, step)), core]
            dst = self.land.at[i]
        return remote(src, dst, self.sends, self.recvs, i, device(self.where, step))

    def add(self, at, lands):
        core = self.where[4]
        rows = self.ref.shape[0]

        @pl.loop(0, rows)
        def _(n):
            total = self.ref[n, at, core].astype(F32)
            for i in lands:
                total = total + self.land[i, n].astype(F32)
            self.ref[n, at, core] = total.astype(BF)

    def turn(self, stage):
        assert stage == self.done
        self.done += 1
        if stage == 0:
            self.hop(7).start()
        elif stage == 1:
            core = self.where[4]
            self.hop(7, True).wait_recv()
            rows = self.ref.shape[0]

            @pl.loop(0, rows)
            def _(n):
                total = self.ref[n, :, core].astype(F32) + self.twin[n].astype(F32)
                self.ref[n, :, core] = total.astype(BF)

            for i in range(1, 7):
                self.hop(i).start()
        else:
            for i in range(4, 7):
                self.hop(i, True).wait_recv()
            self.add(spot(self.where, NEAR), (4, 5, 6))
            self.hop(0).start()

    def close(self):
        for i in range(4):
            self.hop(i, True).wait_recv()
        self.add(spot(self.where), (0, 1, 2, 3))

    def finish(self):
        for i in range(len(SLAB_HOPS)):
            self.hop(i).wait_send()

    def total(self):
        return self.ref.at[:, spot(self.where), self.where[4]]


class RingScatter:
    NORTH, SOUTH, ACROSS = ALONG
    HOPS = (
        (TWIN, HERE, 2),
        (NORTH, NEAR, 1),
        (SOUTH, NEAR, 1),
        (NORTH, HERE, 1),
        (SOUTH, HERE, 1),
        (NORTH, NEAR, 0),
        (SOUTH, NEAR, 0),
        (NORTH, HERE, 0),
        (SOUTH, HERE, 0),
        (NEAR, HERE, 0),
    )

    def __init__(self, where, ref, twin, land, sends, recvs):
        self.where, self.ref, self.twin, self.land = where, ref, twin, land
        self.sends, self.recvs = sends, recvs
        self.done = 0
        self.cut = ref.shape[0] - ref.shape[0] // 2

    def blocks(self, i):
        step, _, kind = self.HOPS[i]
        size = self.ref.shape[0]
        if kind != 1:
            return 0, size
        return (0, self.cut) if step == self.NORTH else (self.cut, size)

    def hop(self, i, arriving=False):
        (step, base, kind), core = self.HOPS[i], self.where[4]
        if kind == 2:
            src, dst = self.ref.at[:, :, 1 - core], self.twin
        else:
            owner = both(base, self.ACROSS if kind else step)
            first, last = self.blocks(i)
            span = pl.ds(first, last - first)
            src, dst = self.ref.at[span, spot(self.where, owner), core], self.land.at[i - 1, span]
        return remote(src, dst, self.sends, self.recvs, i, device(self.where, step))

    def add(self, i, base):
        step, _, kind = self.HOPS[i]
        core = self.where[4]
        self.hop(i, True).wait_recv()
        at = spot(self.where, both(base, step) if kind else base)
        first, last = self.blocks(i)

        @pl.loop(first, last)
        def _(n):
            total = self.ref[n, at, core].astype(F32) + self.land[i - 1, n].astype(F32)
            self.ref[n, at, core] = total.astype(BF)

    def turn(self, stage):
        assert stage == self.done
        self.done += 1
        core = self.where[4]
        if stage == 0:
            starts = (0,)
        elif stage == 1:
            self.hop(0, True).wait_recv()

            @pl.loop(0, self.ref.shape[0])
            def _(n):
                total = self.ref[n, :, core].astype(F32) + self.twin[n].astype(F32)
                self.ref[n, :, core] = total.astype(BF)

            starts = (1, 2, 3, 4)
        elif stage == 2:
            self.add(1, NEAR)
            self.add(2, NEAR)
            starts = (5, 6)
        elif stage == 3:
            self.add(3, HERE)
            self.add(4, HERE)
            starts = (7, 8)
        else:
            self.add(5, NEAR)
            self.add(6, NEAR)
            starts = (9,)
        for i in starts:
            self.hop(i).start()

    def close(self):
        for i in (7, 8, 9):
            self.add(i, HERE)

    def finish(self):
        for i in range(10):
            self.hop(i).wait_send()

    def total(self):
        return self.ref.at[:, spot(self.where), self.where[4]]


def ring_scratch(n, cols):
    return [pltpu.VMEM((n, 8, SLAB, cols), BF), pltpu.VMEM((9, n, SLAB, cols), BF)]


def scatter_scratch(n, cols):
    return [pltpu.VMEM((n, 8, SLAB, cols), BF), pltpu.VMEM((7, n, SLAB, cols), BF)]


def spread_scratch(cuts):
    return [DMA((cuts,)), DMA((7, cuts)), DMA((7, cuts)), DMA((SLAB_COUNT,)), DMA((SLAB_COUNT,))]


def qkv_cuts(w_ref, rep):
    rows = pl.ds(pl.multiple_of(rep * SLAB, SLAB), SLAB)

    def cuts(shard):
        return [
            (
                w_ref.at[rows, pl.ds(pl.multiple_of(j * WIDTH + shard * LOCAL, LOCAL), LOCAL)],
                (j * LOCAL, LOCAL),
            )
            for j in range(3)
        ]

    return cuts


def hidden_start(shard):
    return (shard // 2) * (2 * LOCAL_FF) + lax.rem(shard, 2) * (5 * 128)


def gate_up_cuts(gate_ref, up_ref, rep):
    rows = pl.ds(pl.multiple_of(rep * SLAB, SLAB), SLAB)

    def cuts(shard):
        cols = pl.ds(pl.multiple_of(hidden_start(shard), 128), HID)
        return [(gate_ref.at[rows, cols], (0, HID)), (up_ref.at[rows, cols], (HID, HID))]

    return cuts


def standardize(values):
    center = values - jnp.mean(values, -1, keepdims=True)
    inverse = lax.rsqrt(jnp.mean(center * center, -1, keepdims=True) + EPS)
    return (center * inverse, inverse)


def normalize(values, gain, shift_):
    scaled, inverse = standardize(values)
    return (scaled * gain + shift_, scaled, inverse)


def normalize_back(grad, gain, scaled, inverse):
    weighted = grad * gain
    return inverse * (
        weighted
        - jnp.mean(weighted, -1, keepdims=True)
        - scaled * jnp.mean(weighted * scaled, -1, keepdims=True)
    )


def small_row(small_ref, row):
    return jnp.concatenate([small_ref[s, row : row + 1, :] for s in range(GROUP)], axis=1)


def rotary_tables():
    positions = np.arange(TOTAL, dtype=np.float32)
    freqs = np.float32(BASE) ** (-np.arange(0, ROT, 2).astype(np.float32) / np.float32(ROT))
    angles = positions[:, None] * freqs[None, :].astype(np.float32)
    cosine, sine = np.cos(angles).astype(np.float32), np.sin(angles).astype(np.float32)
    half = ROT // 2
    one = np.ones((TOTAL, HEAD_DIM), np.float32)
    low, high = np.zeros((TOTAL, HEAD_DIM), np.float32), np.zeros((TOTAL, HEAD_DIM), np.float32)
    one[:, :half], one[:, half:ROT] = cosine, cosine
    low[:, :half] = -sine
    high[:, half:ROT] = sine
    return np.stack([np.concatenate([t, t], 1) for t in (one, low, high)])


def turned(values, table_ref, rows, sign):
    parts = []
    for side in range(2):
        part = values[:, side * 128 : (side + 1) * 128]
        swing = pltpu.roll(part, 128 - ROT // 2, 1) * table_ref[1, rows, :] + (
            pltpu.roll(part, ROT // 2, 1) * table_ref[2, rows, :]
        )
        straight = part * table_ref[0, rows, :]
        parts.append(straight + swing if sign > 0 else straight - swing)
    return jnp.concatenate(parts, axis=1)


def chunk_rows(i):
    return pl.ds(pl.multiple_of(i * CHUNK, CHUNK), CHUNK)


def token_chunk(ref, i):
    return ref[pl.ds(i * 2, 2)].reshape(CHUNK, WIDTH)


def bias_row(small_ref, shard, j):
    block = j * GROUP + shard
    return small_ref[block // 3, pl.ds(4 + lax.rem(block, 3), 1), :]


def project(shard, tokens_ref, w_ref, small_ref, table_ref, q_ref, k_ref, v_ref, first, last):
    @pl.loop(first, last, unroll=2)
    def _(i):
        rows = chunk_rows(i)
        tokens = token_chunk(tokens_ref, i)
        for j, ref in enumerate((q_ref, k_ref, v_ref)):
            w = w_ref[:, :, :, :, j * LOCAL : (j + 1) * LOCAL].reshape(WIDTH, LOCAL)
            value = dot(tokens, w) + bias_row(small_ref, shard, j)
            if j < 2:
                value = turned(value, table_ref, rows, 1)
            if j == 0:
                value = value * HEAD_DIM ** (-0.5)
            ref[rows, :] = value.astype(BF)


def head_lanes(h):
    return lax.broadcasted_iota(jnp.int32, (CHUNK, LOCAL), 1) // HEAD_DIM == h


def key_parts(i):
    last = (CHUNK * i, CHUNK * (i + 1), True)
    return ((0, CHUNK * i, False), last) if i else (last,)


def hide_later(values, hidden):
    shape = values.shape
    keys = lax.broadcasted_iota(jnp.int32, shape, 0)
    return jnp.where(keys <= lax.broadcasted_iota(jnp.int32, shape, 1), values, hidden)


def attend(q_ref, k_ref, v_ref, vt_ref, mixed_ref, att_ref, lse_ref, poll):
    vt_ref[...] = v_ref[...].astype(F32).T.astype(BF)
    for i in range(CHUNKS):
        cols = slice(CHUNK * i, CHUNK * (i + 1))

        @pl.loop(0, LOCAL_HEADS, unroll=LOCAL_HEADS)
        def _(h):
            query = jnp.where(head_lanes(h), q_ref[cols, :], jnp.zeros((), BF))
            lanes = pl.ds(pl.multiple_of(h * HEAD_DIM, HEAD_DIM), HEAD_DIM)
            scores = []
            for first, last, diagonal in key_parts(i):
                part = dot_nt(k_ref[first:last, :], query)
                scores.append(hide_later(part, -1e30) if diagonal else part)
            top = functools.reduce(jnp.maximum, [jnp.max(s, 0, keepdims=True) for s in scores])
            expo = [jnp.exp(s - top) for s in scores]
            denom = sum(jnp.sum(e, 0, keepdims=True) for e in expo)
            share = 1.0 / denom
            mixed_ref[lanes, cols] = sum(
                dot(vt_ref[lanes, first:last], (e * share).astype(BF))
                for e, (first, last, _) in zip(expo, key_parts(i))
            )
            lse_ref[pl.ds(h, 1), cols] = top + jnp.log(denom)

        att_ref[cols, :] = mixed_ref[:, cols].T.astype(BF)
        poll(i)


def attend_back(q_ref, k_ref, v_ref, da_ref, lse_ref, kt_ref, dqt_ref, dk_ref, dv_ref, poll):
    kt_ref[...] = k_ref[...].astype(F32).T.astype(BF)
    dk_ref[...] = jnp.zeros_like(dk_ref)
    dv_ref[...] = jnp.zeros_like(dv_ref)
    for i in range(CHUNKS):
        cols = slice(CHUNK * i, CHUNK * (i + 1))

        @pl.loop(0, LOCAL_HEADS, unroll=LOCAL_HEADS)
        def _(h):
            query = jnp.where(head_lanes(h), q_ref[cols, :], jnp.zeros((), BF))
            grad = jnp.where(head_lanes(h), da_ref[cols, :], jnp.zeros((), BF))
            lanes = pl.ds(pl.multiple_of(h * HEAD_DIM, HEAD_DIM), HEAD_DIM)
            top = lse_ref[pl.ds(h, 1), cols]
            probs, grad_probs = [], []
            for first, last, diagonal in key_parts(i):
                part = jnp.exp(dot_nt(k_ref[first:last, :], query) - top)
                probs.append(hide_later(part, 0.0) if diagonal else part)
                grad_probs.append(dot_nt(v_ref[first:last, :], grad))
            total = sum(jnp.sum(g * p, 0, keepdims=True) for g, p in zip(grad_probs, probs))
            pieces = []
            for p, g, (first, last, _) in zip(probs, grad_probs, key_parts(i)):
                grad_scores = (p * (g - total)).astype(BF)
                dv_ref[first:last, :] += dot(p.astype(BF), grad)
                dk_ref[first:last, :] += dot(grad_scores, query)
                pieces.append(dot(kt_ref[lanes, first:last], grad_scores))
            dqt_ref[lanes, cols] = sum(pieces)

        poll(i)


def times(left_ref, w_ref, out_ref, first=0, last=CHUNKS):
    @pl.loop(first, last, unroll=2)
    def _(i):
        left = left_ref[chunk_rows(i), :]
        for j in range(WIDTH // 512):
            cols = slice(j * 512, (j + 1) * 512)
            out_ref[pl.ds(i * 2, 2), :, cols] = (
                dot(left, w_ref[:, cols]).astype(BF).reshape(2, ROWS, 512)
            )


def times_back(left_ref, w_ref, out_ref):
    depth = left_ref.shape[1]

    @pl.loop(0, CHUNKS, unroll=2)
    def _(i):
        left = left_ref[chunk_rows(i), :]
        for j in range(GROUP):
            w = w_ref[j].reshape(LOCAL, depth)
            out_ref[pl.ds(i * 2, 2), :, j * LOCAL : (j + 1) * LOCAL] = (
                dot_nt(left, w).astype(BF).reshape(2, ROWS, LOCAL)
            )


def feed_forward(shard, tokens_ref, grads_ref, w_ref, down_ref, hid_ref, dgu_ref, j):
    odd = lax.rem(shard, 2)
    cols = slice(j * CHUNK, (j + 1) * CHUNK)
    late = slice(HID + j * CHUNK, HID + (j + 1) * CHUNK)

    @pl.loop(0, CHUNKS, unroll=2)
    def _(i):
        rows = chunk_rows(i)
        tokens, grads = token_chunk(tokens_ref, i), token_chunk(grads_ref, i)
        gate = dot(tokens, w_ref[:, :, :, :, cols].reshape(WIDTH, CHUNK))
        up = dot(tokens, w_ref[:, :, :, :, late].reshape(WIDTH, CHUNK))
        grad = dot_nt(grads, down_ref[cols, :])
        unit = lax.broadcasted_iota(jnp.int32, (CHUNK, CHUNK), 1) + (j * CHUNK - 64 * odd)
        mine = jnp.logical_and(unit >= 0, unit < LOCAL_FF)
        sigma = 1.0 / (1.0 + jnp.exp(-gate))
        silu = gate * sigma
        hid_ref[rows, cols] = jnp.where(mine, silu * up, 0.0).astype(BF)
        grad_gate = grad * up * (sigma * (1.0 + gate * (1.0 - sigma)))
        dgu_ref[rows, cols] = jnp.where(mine, grad_gate, 0.0).astype(BF)
        dgu_ref[rows, late] = jnp.where(mine, grad * silu, 0.0).astype(BF)


def outer(left_ref, right_ref, out_ref, first=0, last=None):
    depth = out_ref.shape[-1]
    size = 512 if depth % 512 == 0 else depth if depth < 512 else 256
    last = left_ref.shape[-1] // LOCAL if last is None else last

    @pl.loop(first, last, unroll=2)
    def _(m):
        cols = pl.ds(pl.multiple_of(m * LOCAL, LOCAL), LOCAL)
        if len(left_ref.shape) == 3:
            left = left_ref[:, :, cols].reshape(TOTAL, LOCAL)
        else:
            left = left_ref[:, cols]
        left = left.astype(F32).T.astype(BF)
        for j in range(depth // size):
            part = slice(j * size, (j + 1) * size)
            if len(right_ref.shape) == 3:
                right = right_ref[:, :, part].reshape(TOTAL, size)
            else:
                right = right_ref[:, part]
            out_ref[m, :, :, :, part] = dot(left, right).astype(BF).reshape(8, 2, SLAB, size)


class Return:
    def __init__(self, where, part, out, kind, own_sem, first_sends, first_recvs, sends, recvs):
        self.where, self.part, self.out, self.own_sem = where, part, out, own_sem
        self.first_sends, self.first_recvs = first_sends, first_recvs
        self.slabs = kind(where, out, sends, recvs)

    def first(self, n, offset, arriving=False):
        me = shard_at(self.where)
        source = shard_at(self.where, negative(offset)) if arriving else me
        return remote(
            self.part(shard_at(self.where, offset)),
            self.out.at[source, spot(self.where), self.where[4]],
            self.first_sends,
            self.first_recvs,
            n,
            device(self.where, offset),
        )

    def begin(self):
        for n, offset in enumerate(PEERS):
            self.first(n, offset).start()
        self.own().start()

    def own(self):
        me = shard_at(self.where)
        return pltpu.make_async_copy(
            self.part(me), self.out.at[me, spot(self.where), self.where[4]], self.own_sem
        )

    def middle(self):
        self.own().wait()
        for n, offset in enumerate(PEERS):
            self.first(n, offset, True).wait_recv()

    def turn(self, i):
        self.slabs.turn(i)

    def finish(self):
        self.slabs.finish()
        for n, offset in enumerate(PEERS):
            self.first(n, offset).wait_send()


class Vectors:
    ROUNDS = ((TWIN,), (NEAR,), ALONG)

    def __init__(self, where, msg, land, mine, round_land, first_sends, first_recvs, sends, recvs):
        self.where, self.msg, self.land, self.mine, self.round_land = where, msg, land, mine, round_land
        self.first_sends, self.first_recvs = first_sends, first_recvs
        self.sends, self.recvs = sends, recvs

    def first(self, n, offset, arriving=False):
        me = shard_at(self.where)
        source = shard_at(self.where, negative(offset)) if arriving else me
        return remote(
            self.msg.at[shard_at(self.where, offset)],
            self.land.at[source],
            self.first_sends,
            self.first_recvs,
            n,
            device(self.where, offset),
        )

    def begin(self):
        me = shard_at(self.where)
        for n, offset in enumerate(PEERS):
            self.first(n, offset).start()
        self.land[me] = self.msg[me]

    def middle(self):
        me = shard_at(self.where)
        for n, offset in enumerate(PEERS):
            self.first(n, offset, True).wait_recv()
        total = self.land[0]
        for source in range(1, GROUP):
            total = total + self.land[source]
        self.mine[0] = total
        for p in range(3):
            block = 3 * me + p
            self.mine[0, 4 + p : 5 + p, :] = self.land[lax.rem(block, GROUP), pl.ds(4 + block // GROUP, 1), :]

    def hop(self, n, i, step):
        return remote(self.mine.at[n], self.round_land.at[i], self.sends, self.recvs, i, device(self.where, step))

    def round(self, n):
        base = sum(len(r) for r in self.ROUNDS[:n])
        for i, step in enumerate(self.ROUNDS[n]):
            self.hop(n, base + i, step).start()
        total = self.mine[n]
        for i, step in enumerate(self.ROUNDS[n]):
            self.hop(n, base + i, step).wait_recv()
            total = total + self.round_land[base + i]
        self.mine[n + 1] = total

    def finish(self):
        for n, offset in enumerate(PEERS):
            self.first(n, offset).wait_send()
        for n, steps in enumerate(self.ROUNDS):
            base = sum(len(r) for r in self.ROUNDS[:n])
            for i, step in enumerate(steps):
                self.hop(n, base + i, step).wait_send()


VECTOR_SCRATCH = [
    pltpu.VMEM((GROUP, 8, LOCAL), F32),
    pltpu.VMEM((GROUP, 8, LOCAL), F32),
    pltpu.VMEM((4, 8, LOCAL), F32),
    pltpu.VMEM((5, 8, LOCAL), F32),
    DMA((7,)),
    DMA((7,)),
    DMA((5,)),
    DMA((5,)),
]


def params(cid=None, mib=56):
    if cid is None:
        return pltpu.CompilerParams(vmem_limit_bytes=mib * 2**20)
    return pltpu.CompilerParams(
        collective_id=cid, has_side_effects=True, vmem_limit_bytes=mib * 2**20
    )


class Copies:
    def __init__(self, sems):
        self.sems, self.flying = sems, {}

    def start(self, name, src, dst):
        copy = pltpu.make_async_copy(src, dst, self.sems.at[len(self.flying)])
        copy.start()
        self.flying[name] = [copy, False]

    def wait(self, *names):
        for name in names:
            entry = self.flying[name]
            if not entry[1]:
                entry[0].wait()
                entry[1] = True

    def finish(self):
        self.wait(*self.flying)


def front_kernel(
    x_ref, small_ref, table_ref, ow_ref, qkv_ref, gate_ref, up_ref, gy_ref,
    all_small, mid_ref, a1_out, a2_out, gy_out, wqkv_out, wgu_out, q_out, k_out, v_out, att_out, lse_out,
    a1, w_qkv, own_two, q, k, v, att, lse, vt, mixed, buf, land, local_sems, *sems,
):
    where = place()
    greet(where, PEERS + REP_NEIGHBOURS)
    me, rep = shard_at(where), rep_at(where)
    local = Copies(local_sems)

    def small(n, offset, arriving=False):
        owner = shard_at(where, negative(offset)) if arriving else me
        return remote(small_ref, all_small.at[owner], sems[0], sems[1], n, device(where, offset))

    for n, offset in enumerate(PEERS):
        small(n, offset).start()
    all_small[me] = small_ref[...]
    spread_qkv = Spread(where, qkv_cuts(qkv_ref, rep), w_qkv, *sems[2:7])
    spread_gu = Spread(where, gate_up_cuts(gate_ref, up_ref, rep), wgu_out, *sems[7:12])
    one = Gather(where, a1, *sems[12:14])
    two = Gather(where, a2_out, *sems[14:16], own=own_two)
    grads = Gather(where, gy_out, *sems[16:18], own=gy_ref)
    scatter = Scatter(where, buf, land, *sems[18:20])
    spread_qkv.begin()
    scaled, _ = standardize(x_ref[...].astype(F32))
    for n, offset in enumerate(PEERS):
        small(n, offset, True).wait_recv()
    a1[me] = (scaled * small_row(all_small, 0) + small_row(all_small, 1)).astype(BF)
    plan = Agenda()
    plan.add(agenda(one, 0))
    plan.until(1.0)
    spread_gu.begin()
    local.start("gy", gy_ref.at[0], gy_out.at[me])
    spread_qkv.middle()
    plan.add(slab_agenda(spread_qkv, 4, 4))
    plan.until(19)
    spread_gu.middle()
    plan.add(slab_agenda(spread_gu, 22, 8))
    plan.until(25)
    one.take_all()
    plan.add(agenda(grads, 26))
    plan.until(37)
    spread_qkv.slabs.take_all()
    local.start("a1", a1, a1_out)
    local.start("w_qkv", w_qkv, wqkv_out)
    for half in range(2):
        project(me, a1, w_qkv, all_small, table_ref, q, k, v, 2 * half, 2 * half + 2)
        plan.until(40 + 3 * half)
    attend(q, k, v, vt, mixed, att, lse, lambda i: plan.until(44 + 2 * i))
    for name, src, dst in (("q", q, q_out), ("k", k, k_out), ("v", v, v_out), ("att", att, att_out), ("lse", lse, lse_out)):
        local.start(name, src, dst)
    times(att, ow_ref, buf)
    plan.until(52)
    plan.add(agenda(scatter, 53))
    plan.until(80)
    scatter.take_all()
    mid = x_ref[...].astype(F32) + buf[me].astype(F32)
    mid_ref[...] = mid
    normed, _, _ = normalize(mid, small_row(all_small, 2), small_row(all_small, 3))
    own_two[0] = normed.astype(BF)
    plan.add(agenda(two, 80))
    plan.until(81)
    local.start("own_two", own_two.at[0], a2_out.at[me])
    plan.until(1000)
    spread_qkv.finish(True)
    for mover in (one, two, grads, scatter, spread_gu):
        mover.finish()
    for n, offset in enumerate(PEERS):
        small(n, offset).wait_send()
    local.finish()


def front(x, small, table, out_weight, qkv_weight, gate_weight, up_weight, gy):
    sds = jax.ShapeDtypeStruct
    tokens = sds((GROUP, ROWS, WIDTH), BF)
    head = sds((TOTAL, LOCAL), BF)
    token_sems = [DMA((COUNT,))] * 2
    return pl.pallas_call(
        front_kernel,
        out_shape=(
            sds((GROUP, 8, LOCAL), F32),
            sds((ROWS, WIDTH), F32),
            tokens,
            tokens,
            tokens,
            sds((GROUP, 8, 2, SLAB, 3 * LOCAL), BF),
            sds((GROUP, 8, 2, SLAB, 2 * HID), BF),
            head,
            head,
            head,
            head,
            sds((8, TOTAL), F32),
        ),
        in_specs=[VM] * 4 + [ANY] * 3 + [VM],
        out_specs=(VM, VM) + (ANY,) * 10,
        scratch_shapes=[
            pltpu.VMEM((GROUP, ROWS, WIDTH), BF),
            pltpu.VMEM((GROUP, 8, 2, SLAB, 3 * LOCAL), BF),
            pltpu.VMEM((1, ROWS, WIDTH), BF),
            *[pltpu.VMEM((TOTAL, LOCAL), BF)] * 4,
            pltpu.VMEM((8, TOTAL), F32),
            pltpu.VMEM((LOCAL, TOTAL), BF),
            pltpu.VMEM((LOCAL, TOTAL), F32),
            pltpu.VMEM((GROUP, ROWS, WIDTH), BF),
            pltpu.VMEM((LANDINGS, ROWS, FAR_COLS), BF),
            DMA((9,)),
            DMA((7,)),
            DMA((7,)),
        ]
        + spread_scratch(3)
        + spread_scratch(2)
        + token_sems * 4,
        compiler_params=params(0),
        name="front",
    )(x, small, table, out_weight, qkv_weight, gate_weight, up_weight, gy)


def middle_kernel(
    mid_ref, gy_own, small_ref, a2_in, gy_in, wgu_in, down_in,
    dmid_ref, sums_ref, dy_out, sgu_out, sdown_out, part_out,
    a2, gy, w, down, hid, dgu, buf, land, own, part, ggu, gdown, one_0, one_1, two_0, two_1, down_0, down_1, load_sems, local_sems, *sems,
):
    where = place()
    me, rep = shard_at(where), rep_at(where)
    odd = lax.rem(me, 2)
    loads = Copies(load_sems)

    def tile(j):
        for side in range(2):
            cols = pl.ds(side * HID + j * CHUNK, CHUNK)
            loads.start(("w", j, side), wgu_in.at[:, :, :, :, cols], w.at[:, :, :, :, cols])

    loads.start("a2", a2_in, a2)
    tile(0)
    loads.start("down", down_in, down.at[pl.ds(pl.multiple_of(64 * odd, 64), LOCAL_FF)])
    loads.start("gy", gy_in, gy)
    tile(1)
    tile(2)
    greet(where, NEIGHBOURS + REP_NEIGHBOURS)
    down[pl.ds(pl.multiple_of(LOCAL_FF * (1 - odd), 64), 64), :] = jnp.zeros((64, WIDTH), BF)
    loads.wait("a2", ("w", 0, 0), ("w", 0, 1), "down", "gy")
    for j in range(HID // CHUNK):
        if j:
            loads.wait(("w", j, 0), ("w", j, 1))
        feed_forward(me, a2, gy, w, down, hid, dgu, j)
    times_back(dgu, w, buf)
    scatter = Scatter(where, buf, land, *sems[0:2])
    gather = Gather(where, dy_out, *sems[2:4], own=own)
    local = Copies(local_sems)
    half = GROUP // 2
    sum_gu = [
        RingScatter(where, ggu.at[pl.ds(0, half)], one_0, one_1, *sems[4:6]),
        RingScatter(where, ggu.at[pl.ds(half, half)], two_0, two_1, *sems[8:10]),
    ]
    sum_down = RingScatter(where, gdown, down_0, down_1, *sems[6:8])
    plan = Agenda()
    plan.add(agenda(scatter, 0))
    plan.until(0.9)
    time = 0
    for m in range(GROUP):
        outer(a2, dgu, ggu, m, m + 1)
        time += 1.4
        plan.until(time)
        if m == half - 1:
            plan.add([(6, sum_gu[0], 0), (10.5, sum_gu[0], 1), (15, sum_gu[0], 2), (20, sum_gu[0], 3), (25, sum_gu[0], 4)])
    plan.add([(11.3, sum_gu[1], 0), (15.5, sum_gu[1], 1), (23, sum_gu[1], 2), (29, sum_gu[1], 3), (36, sum_gu[1], 4)])
    plan.until(time)
    for m in range(3):
        outer(hid, gy, gdown, m, m + 1)
        time += 2
        plan.until(time)
    plan.add([(17.5, sum_down, 0), (22, sum_down, 1), (33.5, sum_down, 2), (37, sum_down, 3), (42, sum_down, 4)])
    plan.until(30)
    scatter.take_all()
    gain = small_row(small_ref, 2)
    _, scaled, inverse = normalize(mid_ref[...], gain, small_row(small_ref, 3))
    grad = buf[me].astype(F32)
    dmid = gy_own[0].astype(F32) + normalize_back(grad, gain, scaled, inverse)
    own[0] = dmid.astype(BF)
    plan.add(agenda(gather, 32))
    plan.until(33)
    local.start("own", own.at[0], dy_out.at[me])
    dmid_ref[...] = dmid
    sums_ref[0:1, :] = jnp.sum(grad * scaled, 0, keepdims=True)
    sums_ref[1:2, :] = jnp.sum(grad, 0, keepdims=True)
    plan.until(37)
    for n in range(CHUNKS):
        times(hid, down, part, n, n + 1)
        plan.until(39 + 2 * n)
    local.start("part", part, part_out)
    plan.until(50)
    for n in range(2):
        sum_gu[n].close()
        local.start(("gu", n), sum_gu[n].total(), sgu_out.at[pl.ds(half * n, half)])
    plan.until(1000)
    sum_down.close()
    local.start("down", sum_down.total(), sdown_out)
    gather.take_all()
    for mover in (*sum_gu, sum_down, gather, scatter, local):
        mover.finish()


def middle(mid, gy, small, a2, grads, w_gu, down_weight):
    sds = jax.ShapeDtypeStruct
    tokens = (GROUP, ROWS, WIDTH)
    return pl.pallas_call(
        middle_kernel,
        out_shape=(
            sds((ROWS, WIDTH), F32),
            sds((8, WIDTH), F32),
            sds(tokens, BF),
            sds((GROUP, SLAB, 2 * HID), BF),
            sds((3, SLAB, WIDTH), BF),
            sds(tokens, BF),
        ),
        in_specs=[VM] * 3 + [ANY] * 4,
        out_specs=(VM, VM) + (ANY,) * 4,
        scratch_shapes=[
            pltpu.VMEM(tokens, BF),
            pltpu.VMEM(tokens, BF),
            pltpu.VMEM((GROUP, 8, 2, SLAB, 2 * HID), BF),
            pltpu.VMEM((HID, WIDTH), BF),
            pltpu.VMEM((TOTAL, HID), BF),
            pltpu.VMEM((TOTAL, 2 * HID), BF),
            pltpu.VMEM(tokens, BF),
            pltpu.VMEM((LANDINGS, ROWS, FAR_COLS), BF),
            pltpu.VMEM((1, ROWS, WIDTH), BF),
            pltpu.VMEM(tokens, BF),
            pltpu.VMEM((GROUP, 8, 2, SLAB, 2 * HID), BF),
            pltpu.VMEM((3, 8, 2, SLAB, WIDTH), BF),
            *ring_scratch(GROUP // 2, 2 * HID),
            *ring_scratch(GROUP // 2, 2 * HID),
            *ring_scratch(3, WIDTH),
            DMA((9,)),
            DMA((5,)),
        ]
        + [DMA((COUNT,))] * 4
        + [DMA((SLAB_COUNT,))] * 6,
        compiler_params=params(1, 62),
        name="middle",
    )(mid, gy, small, a2, grads, w_gu, down_weight)


QKV_SPAN = (GROUP, 8, 2, SLAB, 3 * LOCAL)
HALF = 3 * LOCAL // 2
HALF_SPAN = (GROUP, 8, 2, SLAB, HALF)
GU_SPAN = (GROUP, 8, 2, SLAB, 2 * HID)
DOWN_SPAN = (3, 8, 2, SLAB, WIDTH)
OUT_SPAN = (4, 8, 2, SLAB, 512)


def back_kernel(
    x_ref, mid_ref, dmid_ref, small_ref, two_ref, table_ref, ow_ref,
    dy_in, a1_in, wqkv_in, q_in, k_in, v_in, att_in, lse_in, sgu_in, sdown_in, part_in,
    grad_ref, act_ref, vec_ref, gu_out, down_out, qkv_out, kv_out, out_out,
    toks, a1, w, q, k, v, att, lse, da, kt, dqt, dk, dv, dqkv, buf, land, buf_down, land_down,
    gqkv, gkv, gout, qkv_0, qkv_1, kv_0, kv_1, out_0, out_1, load_sems, own_sems, *sems,
):
    where = place()
    me, rep = shard_at(where), rep_at(where)
    loads = Copies(load_sems)
    for name, src, dst in (
        ("toks", dy_in, toks), ("q", q_in, q), ("k", k_in, k),
        ("v", v_in, v), ("lse", lse_in, lse), ("att", att_in, att), ("w", wqkv_in, w),
        ("down", sdown_in, down_out.at[:, spot(where), where[4]]), ("a1", a1_in, a1),
        ("part", part_in, buf_down),
    ):
        loads.start(name, src, dst)
    greet(where, PEERS + REP_NEIGHBOURS)
    down = Scatter(where, buf_down, land_down, *sems[0:2])
    one = Scatter(where, buf, land, *sems[2:4])
    sum_qkv = [
        SlabScatter(where, gqkv, qkv_0, qkv_1, *sems[4:6]),
        SlabScatter(where, gkv, kv_0, kv_1, *sems[28:30]),
    ]
    sum_out = SlabScatter(where, gout, out_0, out_1, *sems[6:8])
    back_gu = Return(where, lambda s: sgu_in.at[s], gu_out, RingGather, own_sems.at[0], *sems[8:12])
    back_qkv = [
        Return(
            where, lambda s: gqkv.at[s, spot(where), where[4]], qkv_out, SlabGather, own_sems.at[1], *sems[12:16]
        ),
        Return(
            where, lambda s: gkv.at[s, spot(where), where[4]], kv_out, SlabGather, own_sems.at[3], *sems[30:34]
        ),
    ]
    back_down = RingGather(where, down_out, *sems[16:18])
    back_out = SlabGather(where, out_out, *sems[18:20])
    vectors = Vectors(where, *sems[20:28])
    plan = Agenda()
    back_gu.begin()
    loads.wait("down")
    plan.add(slab_agenda(back_down, 1.5, 5))
    plan.until(1.5)
    loads.wait("toks")

    @pl.loop(0, CHUNKS, unroll=2)
    def _(i):
        da[chunk_rows(i), :] = dot_nt(token_chunk(toks, i), ow_ref[...]).astype(BF)

    loads.wait("q", "k", "v", "lse")

    def poll(i):
        if i == 0:
            back_gu.middle()
            plan.add(slab_agenda(back_gu, 6, 9))
        plan.until((6.5, 9, 12.5, 17)[i])

    attend_back(q, k, v, da, lse, kt, dqt, dk, dv, poll)
    vectors.msg[...] = jnp.zeros_like(vectors.msg)
    for i in range(CHUNKS):
        rows = slice(i * CHUNK, (i + 1) * CHUNK)
        grad_q = dqt[:, rows].T * HEAD_DIM ** (-0.5)
        for j, value in enumerate((grad_q, dk[rows, :], dv[rows, :])):
            if j < 2:
                value = turned(value, table_ref, rows, -1)
            low = value.astype(BF)
            dqkv[rows, j * LOCAL : (j + 1) * LOCAL] = low
            vectors.msg[0, 4 + j : 5 + j, :] += jnp.sum(low.astype(F32), 0, keepdims=True)
    loads.wait("w")
    times_back(dqkv, w, buf)
    plan.add(agenda(one, 20))
    plan.until(20.9)
    loads.wait("a1")
    for m in range(4):
        outer(a1, dqkv.at[:, pl.ds(0, HALF)], gqkv, 2 * m, 2 * m + 2)
        plan.until(22 + 1.3 * m)
    sum_qkv[0].turn(0)
    for m in range(4):
        outer(a1, dqkv.at[:, pl.ds(HALF, HALF)], gkv, 2 * m, 2 * m + 2)
        plan.until(27.3 + 1.3 * m)
    sum_qkv[1].turn(0)
    sum_qkv[0].turn(1)
    plan.until(33)
    loads.wait("att")
    left = att[...].astype(F32).T.astype(BF)
    for n in range(4):
        right = toks[:, :, n * 512 : (n + 1) * 512].reshape(TOTAL, 512)
        gout[n] = dot(left, right).astype(BF).reshape(8, 2, SLAB, 512)
    sum_out.turn(0)
    sum_qkv[1].turn(1)
    plan.until(36)
    sum_out.turn(1)
    back_down.finish()
    plan.until(40)
    sum_qkv[0].turn(2)
    back_gu.finish()
    sum_qkv[0].close()
    back_qkv[0].begin()
    sum_qkv[1].turn(2)
    plan.until(1000)
    one.take_all()
    loads.wait("part")
    plan.add(agenda(down, 50))
    plan.until(50.9)
    gain = small_row(small_ref, 0)
    _, scaled, inverse = normalize(x_ref[...].astype(F32), gain, small_row(small_ref, 1))
    grad = buf[me].astype(F32)
    first, second = jnp.sum(grad * scaled, 0, keepdims=True), jnp.sum(grad, 0, keepdims=True)
    for d in range(GROUP):
        cols = slice(d * LOCAL, (d + 1) * LOCAL)
        vectors.msg[d, 0:1, :] = first[:, cols]
        vectors.msg[d, 1:2, :] = second[:, cols]
        vectors.msg[d, 2:4, :] = two_ref[0:2, cols]
        if d:
            vectors.msg[d, 4:7, :] = vectors.msg[0, 4:7, :]
    vectors.begin()
    grad_ref[...] = dmid_ref[...] + normalize_back(grad, gain, scaled, inverse)
    sum_qkv[1].close()
    back_qkv[1].begin()
    back_qkv[0].middle()
    back_qkv[0].turn(0)
    plan.until(56)
    vectors.middle()
    back_qkv[0].turn(1)
    plan.until(57)
    back_qkv[1].middle()
    back_qkv[1].turn(0)
    vectors.round(0)
    plan.until(59)
    sum_out.turn(2)
    back_qkv[1].turn(1)
    vectors.round(1)
    one.settle()
    sum_qkv[0].finish()
    sum_out.close()
    out_own = pltpu.make_async_copy(
        sum_out.total(), out_out.at[:, spot(where), where[4]], own_sems.at[2]
    )
    out_own.start()
    vectors.round(2)
    vec_ref[...] = vectors.mine[3]
    plan.until(65)
    out_own.wait()
    back_out.turn(0)
    sum_qkv[1].finish()
    plan.until(1000)
    back_qkv[0].turn(2)
    back_out.turn(1)
    sum_out.finish()
    vectors.finish()
    loads.finish()
    back_qkv[1].turn(2)
    down.take_all()
    act_ref[...] = (mid_ref[...] + buf_down[me].astype(F32)).astype(BF)
    back_out.turn(2)
    for mover in (down, *back_qkv, back_out):
        mover.finish()


def back(x, mid, dmid, small, sums_two, table, out_weight, dy, a1, w_qkv, q, k, v, att, lse, s_gu, s_down, part_down):
    sds = jax.ShapeDtypeStruct
    tokens = (GROUP, ROWS, WIDTH)
    slab_sems = [DMA((SLAB_COUNT,))] * 2
    return pl.pallas_call(
        back_kernel,
        out_shape=(
            sds((ROWS, WIDTH), F32),
            sds((ROWS, WIDTH), BF),
            sds((8, LOCAL), F32),
            *[sds(s, BF) for s in (GU_SPAN, DOWN_SPAN, HALF_SPAN, HALF_SPAN, OUT_SPAN)],
        ),
        in_specs=[VM] * 7 + [ANY] * 11,
        out_specs=(VM,) * 3 + (ANY,) * 5,
        scratch_shapes=[
            pltpu.VMEM(tokens, BF),
            pltpu.VMEM(tokens, BF),
            pltpu.VMEM(QKV_SPAN, BF),
            *[pltpu.VMEM((TOTAL, LOCAL), BF)] * 4,
            pltpu.VMEM((8, TOTAL), F32),
            pltpu.VMEM((TOTAL, LOCAL), BF),
            pltpu.VMEM((LOCAL, TOTAL), BF),
            pltpu.VMEM((LOCAL, TOTAL), F32),
            pltpu.VMEM((TOTAL, LOCAL), F32),
            pltpu.VMEM((TOTAL, LOCAL), F32),
            pltpu.VMEM((TOTAL, 3 * LOCAL), BF),
            pltpu.VMEM(tokens, BF),
            pltpu.VMEM((LANDINGS, ROWS, FAR_COLS), BF),
            pltpu.VMEM(tokens, BF),
            pltpu.VMEM((LANDINGS, ROWS, FAR_COLS), BF),
            pltpu.VMEM(HALF_SPAN, BF),
            pltpu.VMEM(HALF_SPAN, BF),
            pltpu.VMEM(OUT_SPAN, BF),
            *scatter_scratch(GROUP, HALF),
            *scatter_scratch(GROUP, HALF),
            *scatter_scratch(4, 512),
            DMA((10,)),
            DMA((4,)),
        ]
        + [DMA((COUNT,))] * 4
        + slab_sems * 2
        + ([DMA((7,))] * 2 + slab_sems) * 2
        + slab_sems * 2
        + VECTOR_SCRATCH
        + slab_sems
        + [DMA((7,))] * 2
        + slab_sems,
        compiler_params=params(2, 60),
        name="back",
    )(x, mid, dmid, small, sums_two, table, out_weight, dy, a1, w_qkv, q, k, v, att, lse, s_gu, s_down, part_down)


def unpack_kernel(odd_ref, gu_ref, qkv_ref, kv_ref, out_ref, down_ref, gate_out, up_out, qkv_out, out_out, down_out):
    for side, ref in enumerate((gate_out, up_out)):
        cols = slice(side * HID, (side + 1) * HID)
        for t in range(GROUP // 2):
            left, right = gu_ref[2 * t, :, cols].astype(F32), gu_ref[2 * t + 1, :, cols].astype(F32)
            ref[:, t * 2 * LOCAL_FF : (t + 1) * 2 * LOCAL_FF] = jnp.concatenate(
                [left[:, :640], left[:, 640:] + right[:, :128], right[:, 128:]], axis=1
            )
    for s in range(GROUP):
        for j in range(3):
            for part in range(2):
                cols = j * LOCAL + part * 128
                ref, at = (qkv_ref, cols) if cols < HALF else (kv_ref, cols - HALF)
                first = j * WIDTH + s * LOCAL + part * 128
                qkv_out[:, first : first + 128] = ref[s, :, at : at + 128].astype(F32)
    for n in range(4):
        out_out[:, n * 512 : (n + 1) * 512] = out_ref[n].astype(F32)
    rows = LOCAL_FF // 4
    first = pl.multiple_of(64 * odd_ref[0] + rows * pl.program_id(0), SLAB)
    down_out[...] = down_ref[pl.ds(first, rows), :].astype(F32)


def unpack(odd, g_gu, g_qkv, g_kv, g_out, g_down):
    sds = jax.ShapeDtypeStruct
    rows = LOCAL // 4
    return pl.pallas_call(
        unpack_kernel,
        grid_spec=pltpu.PrefetchScalarGridSpec(
            num_scalar_prefetch=1,
            grid=(4,),
            in_specs=[
                pl.BlockSpec((GROUP, rows, 2 * HID), lambda r, _: (0, r, 0)),
                *[pl.BlockSpec((GROUP, rows, HALF), lambda r, _: (0, r, 0))] * 2,
                pl.BlockSpec((4, rows, 512), lambda r, _: (0, r, 0)),
                pl.BlockSpec((HID, WIDTH), lambda r, _: (0, 0)),
            ],
            out_specs=[
                pl.BlockSpec((rows, FF), lambda r, _: (r, 0)),
                pl.BlockSpec((rows, FF), lambda r, _: (r, 0)),
                pl.BlockSpec((rows, 3 * WIDTH), lambda r, _: (r, 0)),
                pl.BlockSpec((rows, WIDTH), lambda r, _: (r, 0)),
                pl.BlockSpec((LOCAL_FF // 4, WIDTH), lambda r, _: (r, 0)),
            ],
        ),
        out_shape=(
            sds((LOCAL, FF), F32),
            sds((LOCAL, FF), F32),
            sds((LOCAL, 3 * WIDTH), F32),
            sds((LOCAL, WIDTH), F32),
            sds((LOCAL_FF, WIDTH), F32),
        ),
        compiler_params=params(),
        name="unpack",
    )(odd.reshape(1), g_gu, g_qkv, g_kv, g_out, g_down)


def shards(
    inputs,
    cotangent,
    ln1_gain,
    ln1_bias,
    qkv_weight,
    qkv_bias,
    out_weight,
    ln2_gain,
    ln2_bias,
    gate_weight,
    up_weight,
    down_weight,
):
    batch, length, width = inputs.shape
    odd = lax.rem(lax.axis_index("shard"), 2)
    table = jnp.asarray(rotary_tables())
    x = inputs.reshape(length, width)
    small, at = jnp.zeros((8 * LOCAL,), F32), 0
    for vector in (ln1_gain, ln1_bias, ln2_gain, ln2_bias, qkv_bias):
        small += jnp.pad(vector.astype(F32), (at, 8 * LOCAL - at - vector.shape[0]))
        at += vector.shape[0]
    small = small.reshape(8, LOCAL)
    all_small, mid, a1, a2, grads, w_qkv, w_gu, q, k, v, att, lse = front(
        x, small, table, out_weight, qkv_weight, gate_weight, up_weight, cotangent
    )
    dmid, sums_two, dy, s_gu, s_down, part_down = middle(
        mid, cotangent, all_small, a2, grads, w_gu, down_weight
    )
    input_grad, activations, vectors, g_gu, g_down, g_qkv, g_kv, g_out = back(
        x, mid, dmid, all_small, sums_two, table, out_weight, dy, a1, w_qkv, q, k, v, att, lse, s_gu, s_down, part_down
    )
    g_gate, g_up, g_qkv, g_out, g_down = unpack(
        odd,
        g_gu.reshape(GROUP, LOCAL, 2 * HID),
        g_qkv.reshape(GROUP, LOCAL, HALF),
        g_kv.reshape(GROUP, LOCAL, HALF),
        g_out.reshape(4, LOCAL, 512),
        g_down.reshape(HID, width),
    )
    return (
        activations.reshape(batch, length, width),
        input_grad.reshape(batch, length, width),
        vectors[0],
        vectors[1],
        g_qkv,
        vectors[4:7].reshape(3 * LOCAL),
        g_out,
        vectors[2],
        vectors[3],
        g_gate,
        g_up,
        g_down,
    )


def solution(mesh):
    tokens, vector, matrix = P("rep", "shard", None), P("shard"), P("shard", None)
    return jax.shard_map(
        shards,
        mesh=mesh,
        in_specs=(tokens, tokens, vector, vector, matrix, vector, matrix, vector, vector, matrix, matrix, matrix),
        out_specs=(tokens, tokens, vector, vector, matrix, vector, matrix, vector, vector, matrix, matrix, matrix),
        check_vma=False,
    )
```

```python
import functools

import jax
import jax.numpy as jnp
import numpy as np
from jax import lax
from jax.experimental import pallas as pl
from jax.experimental.pallas import tpu as pltpu
from jax.sharding import PartitionSpec as P

HEADS = 32
HEAD_DIM = 64
ROT = 16
WIDTH = 2048
GROUP = 8
REPS = 16
ROWS = 128
TOTAL = GROUP * ROWS
LOCAL = WIDTH // GROUP
LOCAL_HEADS = HEADS // GROUP
FF = 5632
LOCAL_FF = FF // GROUP
HID = 768
SLAB = LOCAL // REPS
NEAR_COLS, FAR_COLS = 768, 1280
CHUNK = 256
CHUNKS = TOTAL // CHUNK
EPS = 1e-05
BASE = 10000.0
BF = jnp.bfloat16
F32 = jnp.float32
MESH = pl.DeviceIdType.MESH
VM = pl.BlockSpec(memory_space=pltpu.VMEM)
ANY = pl.BlockSpec(memory_space=pl.ANY)
DMA = pltpu.SemaphoreType.DMA


def dot(left, right):
    return jnp.dot(left, right, preferred_element_type=F32)


def dot_nt(left, right):
    return lax.dot_general(left, right, (((1,), (1,)), ((), ())), preferred_element_type=F32)


FAR, UP, DOWN = (1, 0, 0, 0, 0), (0, 1, 0, 0, 0), (0, -1, 0, 0, 0)
NEAR, NORTH, SOUTH, TWIN = (0, 0, 1, 0, 0), (0, 0, 0, 1, 0), (0, 0, 0, -1, 0), (0, 0, 0, 0, 1)
HERE = (0, 0, 0, 0, 0)
SIZES = (2, 4, 2, 4, 2)
PEERS = tuple((f, z, 0, 0, 0) for f in range(2) for z in range(4) if (f, z) != (0, 0))


def place():
    shard, rep = lax.axis_index("shard"), lax.axis_index("rep")
    return (shard // 4, lax.rem(shard, 4), rep // 8, lax.rem(rep // 2, 4), lax.rem(rep, 2))


def shift(where, offset):
    return tuple(
        lax.rem(a + (o + 2 * n) % n, n) if o % n else a for a, o, n in zip(where, offset, SIZES)
    )


def shard_at(where, offset=HERE):
    far, level = shift(where, offset)[:2]
    return far * 4 + level


def rep_at(where, offset=HERE):
    near, north, core = shift(where, offset)[2:]
    return near * 8 + north * 2 + core


def device(where, offset):
    return (shard_at(where, offset), rep_at(where, offset))


def less(a, b):
    return tuple((p - q) % n for p, q, n in zip(a, b, SIZES))


def negative(a):
    return tuple(-p for p in a)


def greet(where, offsets):
    barrier = pltpu.get_barrier_semaphore()
    for offset in offsets:
        pl.semaphore_signal(
            barrier, inc=1, device_id=device(where, negative(offset)), device_id_type=MESH
        )
    pl.semaphore_wait(barrier, len(offsets))


def remote(src, dst, sends, recvs, i, to):
    return pltpu.make_async_remote_copy(
        src_ref=src,
        dst_ref=dst,
        send_sem=sends.at[i],
        recv_sem=recvs.at[i],
        device_id=to,
        device_id_type=MESH,
    )


def token_moves():
    moves = []

    def add(owner, part, step, first, turn, back):
        moves.append((owner, part, step, first, turn, back))
        return len(moves) - 1

    near, far = (0, NEAR_COLS), (NEAR_COLS, FAR_COLS)
    whole, top, low = (0, ROWS), (0, ROWS // 2), (ROWS // 2, ROWS // 2)
    up2 = (0, 2, 0, 0, 0)
    up = add(HERE, (whole, near), UP, None, 0, 15.5)
    down = add(HERE, (whole, near), DOWN, None, 0, 15.5)
    add(HERE, (whole, near), FAR, None, 0.2, 0.3)
    a = add(DOWN, (top, near), UP, up, 5.5, 7)
    b = add(UP, (low, near), DOWN, down, 5.5, 7)
    add(DOWN, (whole, near), FAR, up, 5.6, 0.2)
    add(UP, (whole, near), FAR, down, 5.6, 0.2)
    add(up2, (top, near), FAR, a, 10, 0)
    add(up2, (low, near), FAR, b, 10, 0)
    over = add(HERE, (whole, far), FAR, None, 0.1, 15)
    up = add(HERE, (whole, far), UP, None, 0.3, 9)
    down = add(HERE, (whole, far), DOWN, None, 0.3, 9)
    add(DOWN, (top, far), UP, up, 13, 0.1)
    add(UP, (low, far), DOWN, down, 13, 0.1)
    up = add(FAR, (whole, far), UP, over, 11.5, 6)
    down = add(FAR, (whole, far), DOWN, over, 11.5, 6)
    add(tuple(p + q for p, q in zip(FAR, DOWN)), (top, far), UP, up, 19.5, 0)
    add(tuple(p + q for p, q in zip(FAR, UP)), (low, far), DOWN, down, 19.5, 0)
    return tuple(moves)


MOVES = token_moves()
COUNT = len(MOVES)
TURNS = tuple(sorted(range(COUNT), key=lambda i: MOVES[i][4]))
BACK_TURNS = tuple(sorted(range(COUNT), key=lambda i: MOVES[i][5]))
FED = tuple(tuple(j for j in range(COUNT) if MOVES[j][3] == i) for i in range(COUNT))
NEIGHBOURS = (FAR, UP, DOWN)
LANDS = {}
for _i in range(COUNT):
    pair = MOVES[_i][1][0][0] > 0
    LANDS[_i] = LANDS[_i - 1] if pair else len(set(LANDS.values()))
LANDINGS = len(set(LANDS.values()))


def token_part(ref, block, part):
    (row, rows), (col, cols) = part
    return ref.at[block, pl.ds(row, rows), pl.ds(col, cols)]


class Gather:
    def __init__(self, where, ref, sends, recvs, own=None):
        self.where, self.ref, self.sends, self.recvs, self.own = where, ref, sends, recvs, own
        self.got = set()

    def move(self, i, arriving=False):
        owner, part, step = MOVES[i][:3]
        block = shard_at(self.where, less(owner, step) if arriving else owner)
        ref = token_part(self.ref, block, part)
        src = ref
        if owner == HERE and self.own is not None and not arriving:
            src = token_part(self.own, 0, part)
        return remote(src, ref, self.sends, self.recvs, i, device(self.where, step))

    def take(self, i):
        if i not in self.got:
            self.got.add(i)
            self.move(i, True).wait_recv()

    def turn(self, i):
        if MOVES[i][3] is not None:
            self.take(MOVES[i][3])
        self.move(i).start()

    def take_all(self):
        for i in TURNS:
            self.take(i)

    def settle(self):
        for i in TURNS:
            self.move(i).wait_send()

    def finish(self):
        self.take_all()
        self.settle()

    def run(self):
        for i in TURNS:
            self.turn(i)
        self.finish()


def agenda(mover, start):
    column = 5 if isinstance(mover, Scatter) else 4
    return [(start + MOVES[i][column], mover, i) for i in range(COUNT)]


def slab_agenda(mover, start, unit):
    turns = mover.slabs.TURNS if hasattr(mover, "slabs") else mover.TURNS
    return [(start + unit * t, mover, i) for i, t in enumerate(turns)]


class Agenda:
    def __init__(self):
        self.items = []

    def add(self, items):
        self.items = sorted(self.items + items, key=lambda e: e[0])

    def until(self, time):
        while self.items and self.items[0][0] <= time:
            _, mover, i = self.items.pop(0)
            mover.turn(i)


class Scatter:
    def __init__(self, where, buf, land, sends, recvs):
        self.where, self.buf, self.land, self.sends, self.recvs = where, buf, land, sends, recvs
        self.got = set()

    def move(self, i, arriving=False):
        owner, part, step = MOVES[i][:3]
        block = shard_at(self.where, owner if arriving else less(owner, step))
        (row, rows), (col, cols) = part
        return remote(
            token_part(self.buf, block, part),
            self.land.at[LANDS[i], pl.ds(row, rows), pl.ds(0, cols)],
            self.sends,
            self.recvs,
            i,
            device(self.where, negative(step)),
        )

    def take(self, i):
        if i in self.got:
            return
        self.got.add(i)
        owner, ((row, rows), (col, cols)) = MOVES[i][:2]
        self.move(i, True).wait_recv()
        at = (shard_at(self.where, owner), pl.ds(row, rows), pl.ds(col, cols))
        total = self.buf[at].astype(F32) + self.land[LANDS[i], pl.ds(row, rows), pl.ds(0, cols)].astype(F32)
        self.buf[at] = total.astype(BF)

    def turn(self, i):
        for j in FED[i]:
            self.take(j)
        self.move(i).start()

    def take_all(self):
        for i in BACK_TURNS:
            self.take(i)

    def settle(self):
        for i in BACK_TURNS:
            self.move(i).wait_send()

    def finish(self):
        self.take_all()
        self.settle()

    def run(self):
        for i in BACK_TURNS:
            self.turn(i)
        self.finish()


ALONG = ((0, 0, 0, 1, 0), (0, 0, 0, 3, 0), (0, 0, 0, 2, 0))
SLAB_HOPS = (NEAR,) + ALONG + ALONG + (TWIN,)
SLAB_COUNT = 10
REP_NEIGHBOURS = (NEAR, TWIN) + ALONG


def spot(where, offset=HERE):
    near, north = shift(where, offset)[2:4]
    return near * 4 + north


def both(a, b):
    return tuple(p + q for p, q in zip(a, b))


class Spread:
    def __init__(self, where, cuts, ref, own_sem, first_sends, first_recvs, sends, recvs):
        self.where, self.cuts, self.ref, self.own_sem = where, cuts, ref, own_sem
        self.first_sends, self.first_recvs = first_sends, first_recvs
        self.slabs = RingGather(where, ref, sends, recvs)

    def first(self, n, offset, arriving=False):
        me = shard_at(self.where)
        owner = shard_at(self.where, negative(offset)) if arriving else me
        copies = []
        for j, (src, (col, cols)) in enumerate(self.cuts(shard_at(self.where, offset))):
            copies.append(
                remote(
                    src,
                    self.ref.at[owner, spot(self.where), self.where[4], :, pl.ds(col, cols)],
                    self.first_sends,
                    self.first_recvs,
                    (n, j),
                    device(self.where, offset),
                )
            )
        return copies

    def own(self):
        me = shard_at(self.where)
        return [
            pltpu.make_async_copy(
                src,
                self.ref.at[me, spot(self.where), self.where[4], :, pl.ds(col, cols)],
                self.own_sem.at[j],
            )
            for j, (src, (col, cols)) in enumerate(self.cuts(me))
        ]

    def begin(self):
        for n, offset in enumerate(PEERS):
            for copy in self.first(n, offset):
                copy.start()
        for copy in self.own():
            copy.start()

    def middle(self):
        for copy in self.own():
            copy.wait()
        for n, offset in enumerate(PEERS):
            for copy in self.first(n, offset, True):
                copy.wait_recv()

    def finish(self, taken=False):
        self.slabs.finish(taken)
        for n, offset in enumerate(PEERS):
            for copy in self.first(n, offset):
                copy.wait_send()

    def turn(self, i):
        self.slabs.turn(i)


def slab_span(ref, first, count):
    size = ref.shape[0]
    start, stop = first * size // GROUP, (first + count) * size // GROUP
    return pl.ds(start, stop - start)


class SlabGather:
    TURNS = (0, 0.6, 4.2)

    def __init__(self, where, ref, sends, recvs):
        self.where, self.ref, self.sends, self.recvs = where, ref, sends, recvs
        self.done = 0

    def hop(self, i, arriving=False):
        step = SLAB_HOPS[i]
        core = self.where[4]
        if step == TWIN:
            part = self.ref.at[:, :, (1 - core) if arriving else core]
        else:
            base = NEAR if 4 <= i < 7 else HERE
            owner = both(base, negative(step)) if arriving else base
            part = self.ref.at[:, spot(self.where, owner), core]
        return remote(part, part, self.sends, self.recvs, i, device(self.where, step))

    def turn(self, stage):
        assert stage == self.done
        self.done += 1
        if stage == 0:
            for i in range(4):
                self.hop(i).start()
        elif stage == 1:
            self.hop(0, True).wait_recv()
            for i in range(4, 7):
                self.hop(i).start()
        else:
            for i in range(1, 7):
                self.hop(i, True).wait_recv()
            self.hop(7).start()

    def take_all(self):
        self.hop(7, True).wait_recv()

    def finish(self, taken=False):
        if not taken:
            self.take_all()
        for i in range(len(SLAB_HOPS)):
            self.hop(i).wait_send()


class RingGather:
    TURNS = (0, 0.6, 1.2, 2.3, 3.4)
    NORTH, SOUTH = ALONG[:2]
    HOPS = (
        (NEAR, HERE, 0),
        (NORTH, HERE, 0),
        (SOUTH, HERE, 0),
        (NORTH, NEAR, 0),
        (SOUTH, NEAR, 0),
        (NORTH, HERE, 1),
        (SOUTH, HERE, 1),
        (NORTH, NEAR, 1),
        (SOUTH, NEAR, 1),
        (TWIN, HERE, 2),
    )

    def __init__(self, where, ref, sends, recvs):
        self.where, self.ref, self.sends, self.recvs = where, ref, sends, recvs
        self.done = 0
        self.cut = ref.shape[0] - ref.shape[0] // 2

    def hop(self, i, arriving=False):
        (step, base, kind), core = self.HOPS[i], self.where[4]
        if kind == 2:
            part = self.ref.at[:, :, (1 - core) if arriving else core]
        else:
            owner = both(base, negative(step)) if kind else base
            if arriving:
                owner = both(owner, negative(step))
            blocks = slice(None)
            if kind:
                blocks = (
                    pl.ds(0, self.cut)
                    if step == self.NORTH
                    else pl.ds(self.cut, self.ref.shape[0] - self.cut)
                )
            part = self.ref.at[blocks, spot(self.where, owner), core]
        return remote(part, part, self.sends, self.recvs, i, device(self.where, step))

    def turn(self, stage):
        assert stage == self.done
        self.done += 1
        waits, starts = (
            ((), (0, 1, 2)),
            ((0,), (3, 4)),
            ((1, 2), (5, 6)),
            ((3, 4), (7, 8)),
            ((5, 6, 7, 8), (9,)),
        )[stage]
        for i in waits:
            self.hop(i, True).wait_recv()
        for i in starts:
            self.hop(i).start()

    def take_all(self):
        self.hop(9, True).wait_recv()

    def finish(self, taken=False):
        if not taken:
            self.take_all()
        for i in range(10):
            self.hop(i).wait_send()


class SlabScatter:
    TURNS = (0, 1.0, 5.5)

    def __init__(self, where, ref, twin, land, sends, recvs):
        self.where, self.ref, self.twin, self.land = where, ref, twin, land
        self.sends, self.recvs = sends, recvs
        self.done = 0

    def hop(self, i, arriving=False):
        step = SLAB_HOPS[i]
        core = self.where[4]
        if step == TWIN:
            src, dst = self.ref.at[:, :, 1 - core], self.twin
        else:
            base = NEAR if 4 <= i < 7 else HERE
            src = self.ref.at[:, spot(self.where, both(base, step)), core]
            dst = self.land.at[i]
        return remote(src, dst, self.sends, self.recvs, i, device(self.where, step))

    def add(self, at, lands):
        core = self.where[4]
        rows = self.ref.shape[0]

        @pl.loop(0, rows)
        def _(n):
            total = self.ref[n, at, core].astype(F32)
            for i in lands:
                total = total + self.land[i, n].astype(F32)
            self.ref[n, at, core] = total.astype(BF)

    def turn(self, stage):
        assert stage == self.done
        self.done += 1
        if stage == 0:
            self.hop(7).start()
        elif stage == 1:
            core = self.where[4]
            self.hop(7, True).wait_recv()
            rows = self.ref.shape[0]

            @pl.loop(0, rows)
            def _(n):
                total = self.ref[n, :, core].astype(F32) + self.twin[n].astype(F32)
                self.ref[n, :, core] = total.astype(BF)

            for i in range(1, 7):
                self.hop(i).start()
        else:
            for i in range(4, 7):
                self.hop(i, True).wait_recv()
            self.add(spot(self.where, NEAR), (4, 5, 6))
            self.hop(0).start()

    def close(self):
        for i in range(4):
            self.hop(i, True).wait_recv()
        self.add(spot(self.where), (0, 1, 2, 3))

    def finish(self):
        for i in range(len(SLAB_HOPS)):
            self.hop(i).wait_send()

    def total(self):
        return self.ref.at[:, spot(self.where), self.where[4]]


class RingScatter:
    NORTH, SOUTH, ACROSS = ALONG
    HOPS = (
        (TWIN, HERE, 2),
        (NORTH, NEAR, 1),
        (SOUTH, NEAR, 1),
        (NORTH, HERE, 1),
        (SOUTH, HERE, 1),
        (NORTH, NEAR, 0),
        (SOUTH, NEAR, 0),
        (NORTH, HERE, 0),
        (SOUTH, HERE, 0),
        (NEAR, HERE, 0),
    )

    def __init__(self, where, ref, twin, land, sends, recvs):
        self.where, self.ref, self.twin, self.land = where, ref, twin, land
        self.sends, self.recvs = sends, recvs
        self.done = 0
        self.cut = ref.shape[0] - ref.shape[0] // 2

    def blocks(self, i):
        step, _, kind = self.HOPS[i]
        size = self.ref.shape[0]
        if kind != 1:
            return 0, size
        return (0, self.cut) if step == self.NORTH else (self.cut, size)

    def hop(self, i, arriving=False):
        (step, base, kind), core = self.HOPS[i], self.where[4]
        if kind == 2:
            src, dst = self.ref.at[:, :, 1 - core], self.twin
        else:
            owner = both(base, self.ACROSS if kind else step)
            first, last = self.blocks(i)
            span = pl.ds(first, last - first)
            src, dst = self.ref.at[span, spot(self.where, owner), core], self.land.at[i - 1, span]
        return remote(src, dst, self.sends, self.recvs, i, device(self.where, step))

    def add(self, i, base):
        step, _, kind = self.HOPS[i]
        core = self.where[4]
        self.hop(i, True).wait_recv()
        at = spot(self.where, both(base, step) if kind else base)
        first, last = self.blocks(i)

        @pl.loop(first, last)
        def _(n):
            total = self.ref[n, at, core].astype(F32) + self.land[i - 1, n].astype(F32)
            self.ref[n, at, core] = total.astype(BF)

    def turn(self, stage):
        assert stage == self.done
        self.done += 1
        core = self.where[4]
        if stage == 0:
            starts = (0,)
        elif stage == 1:
            self.hop(0, True).wait_recv()

            @pl.loop(0, self.ref.shape[0])
            def _(n):
                total = self.ref[n, :, core].astype(F32) + self.twin[n].astype(F32)
                self.ref[n, :, core] = total.astype(BF)

            starts = (1, 2, 3, 4)
        elif stage == 2:
            self.add(1, NEAR)
            self.add(2, NEAR)
            starts = (5, 6)
        elif stage == 3:
            self.add(3, HERE)
            self.add(4, HERE)
            starts = (7, 8)
        else:
            self.add(5, NEAR)
            self.add(6, NEAR)
            starts = (9,)
        for i in starts:
            self.hop(i).start()

    def close(self):
        for i in (7, 8, 9):
            self.add(i, HERE)

    def finish(self):
        for i in range(10):
            self.hop(i).wait_send()

    def total(self):
        return self.ref.at[:, spot(self.where), self.where[4]]


def ring_scratch(n, cols):
    return [pltpu.VMEM((n, 8, SLAB, cols), BF), pltpu.VMEM((9, n, SLAB, cols), BF)]


def scatter_scratch(n, cols):
    return [pltpu.VMEM((n, 8, SLAB, cols), BF), pltpu.VMEM((7, n, SLAB, cols), BF)]


def spread_scratch(cuts):
    return [DMA((cuts,)), DMA((7, cuts)), DMA((7, cuts)), DMA((SLAB_COUNT,)), DMA((SLAB_COUNT,))]


def qkv_cuts(w_ref, rep):
    rows = pl.ds(pl.multiple_of(rep * SLAB, SLAB), SLAB)

    def cuts(shard):
        return [
            (
                w_ref.at[rows, pl.ds(pl.multiple_of(j * WIDTH + shard * LOCAL, LOCAL), LOCAL)],
                (j * LOCAL, LOCAL),
            )
            for j in range(3)
        ]

    return cuts


def hidden_start(shard):
    return (shard // 2) * (2 * LOCAL_FF) + lax.rem(shard, 2) * (5 * 128)


def gate_up_cuts(gate_ref, up_ref, rep):
    rows = pl.ds(pl.multiple_of(rep * SLAB, SLAB), SLAB)

    def cuts(shard):
        cols = pl.ds(pl.multiple_of(hidden_start(shard), 128), HID)
        return [(gate_ref.at[rows, cols], (0, HID)), (up_ref.at[rows, cols], (HID, HID))]

    return cuts


def standardize(values):
    center = values - jnp.mean(values, -1, keepdims=True)
    inverse = lax.rsqrt(jnp.mean(center * center, -1, keepdims=True) + EPS)
    return (center * inverse, inverse)


def normalize(values, gain, shift_):
    scaled, inverse = standardize(values)
    return (scaled * gain + shift_, scaled, inverse)


def normalize_back(grad, gain, scaled, inverse):
    weighted = grad * gain
    return inverse * (
        weighted
        - jnp.mean(weighted, -1, keepdims=True)
        - scaled * jnp.mean(weighted * scaled, -1, keepdims=True)
    )


def small_row(small_ref, row):
    return jnp.concatenate([small_ref[s, row : row + 1, :] for s in range(GROUP)], axis=1)


def rotary_tables():
    positions = np.arange(TOTAL, dtype=np.float32)
    freqs = np.float32(BASE) ** (-np.arange(0, ROT, 2).astype(np.float32) / np.float32(ROT))
    angles = positions[:, None] * freqs[None, :].astype(np.float32)
    cosine, sine = np.cos(angles).astype(np.float32), np.sin(angles).astype(np.float32)
    half = ROT // 2
    one = np.ones((TOTAL, HEAD_DIM), np.float32)
    low, high = np.zeros((TOTAL, HEAD_DIM), np.float32), np.zeros((TOTAL, HEAD_DIM), np.float32)
    one[:, :half], one[:, half:ROT] = cosine, cosine
    low[:, :half] = -sine
    high[:, half:ROT] = sine
    return np.stack([np.concatenate([t, t], 1) for t in (one, low, high)])


def turned(values, table_ref, rows, sign):
    parts = []
    for side in range(2):
        part = values[:, side * 128 : (side + 1) * 128]
        swing = pltpu.roll(part, 128 - ROT // 2, 1) * table_ref[1, rows, :] + (
            pltpu.roll(part, ROT // 2, 1) * table_ref[2, rows, :]
        )
        straight = part * table_ref[0, rows, :]
        parts.append(straight + swing if sign > 0 else straight - swing)
    return jnp.concatenate(parts, axis=1)


def chunk_rows(i):
    return pl.ds(pl.multiple_of(i * CHUNK, CHUNK), CHUNK)


def token_chunk(ref, i):
    return ref[pl.ds(i * 2, 2)].reshape(CHUNK, WIDTH)


def bias_row(small_ref, shard, j):
    block = j * GROUP + shard
    return small_ref[block // 3, pl.ds(4 + lax.rem(block, 3), 1), :]


def project(shard, tokens_ref, w_ref, small_ref, table_ref, q_ref, k_ref, v_ref, first, last):
    @pl.loop(first, last, unroll=2)
    def _(i):
        rows = chunk_rows(i)
        tokens = token_chunk(tokens_ref, i)
        for j, ref in enumerate((q_ref, k_ref, v_ref)):
            w = w_ref[:, :, :, :, j * LOCAL : (j + 1) * LOCAL].reshape(WIDTH, LOCAL)
            value = dot(tokens, w) + bias_row(small_ref, shard, j)
            if j < 2:
                value = turned(value, table_ref, rows, 1)
            if j == 0:
                value = value * HEAD_DIM ** (-0.5)
            ref[rows, :] = value.astype(BF)


def head_lanes(h):
    return lax.broadcasted_iota(jnp.int32, (CHUNK, LOCAL), 1) // HEAD_DIM == h


def key_parts(i):
    last = (CHUNK * i, CHUNK * (i + 1), True)
    return ((0, CHUNK * i, False), last) if i else (last,)


def hide_later(values, hidden):
    shape = values.shape
    keys = lax.broadcasted_iota(jnp.int32, shape, 0)
    return jnp.where(keys <= lax.broadcasted_iota(jnp.int32, shape, 1), values, hidden)


def attend(q_ref, k_ref, v_ref, vt_ref, mixed_ref, att_ref, lse_ref, poll):
    vt_ref[...] = v_ref[...].astype(F32).T.astype(BF)
    for i in range(CHUNKS):
        cols = slice(CHUNK * i, CHUNK * (i + 1))

        @pl.loop(0, LOCAL_HEADS, unroll=LOCAL_HEADS)
        def _(h):
            query = jnp.where(head_lanes(h), q_ref[cols, :], jnp.zeros((), BF))
            lanes = pl.ds(pl.multiple_of(h * HEAD_DIM, HEAD_DIM), HEAD_DIM)
            scores = []
            for first, last, diagonal in key_parts(i):
                part = dot_nt(k_ref[first:last, :], query)
                scores.append(hide_later(part, -1e30) if diagonal else part)
            top = functools.reduce(jnp.maximum, [jnp.max(s, 0, keepdims=True) for s in scores])
            expo = [jnp.exp(s - top) for s in scores]
            denom = sum(jnp.sum(e, 0, keepdims=True) for e in expo)
            share = 1.0 / denom
            mixed_ref[lanes, cols] = sum(
                dot(vt_ref[lanes, first:last], (e * share).astype(BF))
                for e, (first, last, _) in zip(expo, key_parts(i))
            )
            lse_ref[pl.ds(h, 1), cols] = top + jnp.log(denom)

        att_ref[cols, :] = mixed_ref[:, cols].T.astype(BF)
        poll(i)


def attend_back(q_ref, k_ref, v_ref, da_ref, lse_ref, kt_ref, dqt_ref, dk_ref, dv_ref, poll):
    kt_ref[...] = k_ref[...].astype(F32).T.astype(BF)
    dk_ref[...] = jnp.zeros_like(dk_ref)
    dv_ref[...] = jnp.zeros_like(dv_ref)
    for i in range(CHUNKS):
        cols = slice(CHUNK * i, CHUNK * (i + 1))

        @pl.loop(0, LOCAL_HEADS, unroll=LOCAL_HEADS)
        def _(h):
            query = jnp.where(head_lanes(h), q_ref[cols, :], jnp.zeros((), BF))
            grad = jnp.where(head_lanes(h), da_ref[cols, :], jnp.zeros((), BF))
            lanes = pl.ds(pl.multiple_of(h * HEAD_DIM, HEAD_DIM), HEAD_DIM)
            top = lse_ref[pl.ds(h, 1), cols]
            probs, grad_probs = [], []
            for first, last, diagonal in key_parts(i):
                part = jnp.exp(dot_nt(k_ref[first:last, :], query) - top)
                probs.append(hide_later(part, 0.0) if diagonal else part)
                grad_probs.append(dot_nt(v_ref[first:last, :], grad))
            total = sum(jnp.sum(g * p, 0, keepdims=True) for g, p in zip(grad_probs, probs))
            pieces = []
            for p, g, (first, last, _) in zip(probs, grad_probs, key_parts(i)):
                grad_scores = (p * (g - total)).astype(BF)
                dv_ref[first:last, :] += dot(p.astype(BF), grad)
                dk_ref[first:last, :] += dot(grad_scores, query)
                pieces.append(dot(kt_ref[lanes, first:last], grad_scores))
            dqt_ref[lanes, cols] = sum(pieces)

        poll(i)


def times(left_ref, w_ref, out_ref, first=0, last=CHUNKS):
    @pl.loop(first, last, unroll=2)
    def _(i):
        left = left_ref[chunk_rows(i), :]
        for j in range(WIDTH // 512):
            cols = slice(j * 512, (j + 1) * 512)
            out_ref[pl.ds(i * 2, 2), :, cols] = (
                dot(left, w_ref[:, cols]).astype(BF).reshape(2, ROWS, 512)
            )


def times_back(left_ref, w_ref, out_ref):
    depth = left_ref.shape[1]

    @pl.loop(0, CHUNKS, unroll=4)
    def _(i):
        left = left_ref[chunk_rows(i), :]
        for j in range(GROUP):
            w = w_ref[j].reshape(LOCAL, depth)
            out_ref[pl.ds(i * 2, 2), :, j * LOCAL : (j + 1) * LOCAL] = (
                dot_nt(left, w).astype(BF).reshape(2, ROWS, LOCAL)
            )


def feed_forward(shard, tokens_ref, grads_ref, w_ref, down_ref, hid_ref, dgu_ref, j):
    odd = lax.rem(shard, 2)
    cols = slice(j * CHUNK, (j + 1) * CHUNK)
    late = slice(HID + j * CHUNK, HID + (j + 1) * CHUNK)

    @pl.loop(0, CHUNKS, unroll=4)
    def _(i):
        rows = chunk_rows(i)
        tokens, grads = token_chunk(tokens_ref, i), token_chunk(grads_ref, i)
        gate = dot(tokens, w_ref[:, :, :, :, cols].reshape(WIDTH, CHUNK))
        up = dot(tokens, w_ref[:, :, :, :, late].reshape(WIDTH, CHUNK))
        grad = dot_nt(grads, down_ref[cols, :])
        unit = lax.broadcasted_iota(jnp.int32, (CHUNK, CHUNK), 1) + (j * CHUNK - 64 * odd)
        mine = jnp.logical_and(unit >= 0, unit < LOCAL_FF)
        sigma = 1.0 / (1.0 + jnp.exp(-gate))
        silu = gate * sigma
        hid_ref[rows, cols] = jnp.where(mine, silu * up, 0.0).astype(BF)
        grad_gate = grad * up * (sigma * (1.0 + gate * (1.0 - sigma)))
        dgu_ref[rows, cols] = jnp.where(mine, grad_gate, 0.0).astype(BF)
        dgu_ref[rows, late] = jnp.where(mine, grad * silu, 0.0).astype(BF)


def outer(left_ref, right_ref, out_ref, first=0, last=None):
    depth = out_ref.shape[-1]
    size = 512 if depth % 512 == 0 else depth if depth < 512 else 256
    last = left_ref.shape[-1] // LOCAL if last is None else last

    @pl.loop(first, last, unroll=2)
    def _(m):
        cols = pl.ds(pl.multiple_of(m * LOCAL, LOCAL), LOCAL)
        if len(left_ref.shape) == 3:
            left = left_ref[:, :, cols].reshape(TOTAL, LOCAL)
        else:
            left = left_ref[:, cols]
        left = left.astype(F32).T.astype(BF)
        for j in range(depth // size):
            part = slice(j * size, (j + 1) * size)
            if len(right_ref.shape) == 3:
                right = right_ref[:, :, part].reshape(TOTAL, size)
            else:
                right = right_ref[:, part]
            out_ref[m, :, :, :, part] = dot(left, right).astype(BF).reshape(8, 2, SLAB, size)


class Return:
    def __init__(self, where, part, out, kind, own_sem, first_sends, first_recvs, sends, recvs):
        self.where, self.part, self.out, self.own_sem = where, part, out, own_sem
        self.first_sends, self.first_recvs = first_sends, first_recvs
        self.slabs = kind(where, out, sends, recvs)

    def first(self, n, offset, arriving=False):
        me = shard_at(self.where)
        source = shard_at(self.where, negative(offset)) if arriving else me
        return remote(
            self.part(shard_at(self.where, offset)),
            self.out.at[source, spot(self.where), self.where[4]],
            self.first_sends,
            self.first_recvs,
            n,
            device(self.where, offset),
        )

    def begin(self):
        for n, offset in enumerate(PEERS):
            self.first(n, offset).start()
        self.own().start()

    def own(self):
        me = shard_at(self.where)
        return pltpu.make_async_copy(
            self.part(me), self.out.at[me, spot(self.where), self.where[4]], self.own_sem
        )

    def middle(self):
        self.own().wait()
        for n, offset in enumerate(PEERS):
            self.first(n, offset, True).wait_recv()

    def turn(self, i):
        self.slabs.turn(i)

    def finish(self):
        self.slabs.finish()
        for n, offset in enumerate(PEERS):
            self.first(n, offset).wait_send()


class Vectors:
    ROUNDS = ((TWIN,), (NEAR,), ALONG)

    def __init__(self, where, msg, land, mine, round_land, first_sends, first_recvs, sends, recvs):
        self.where, self.msg, self.land, self.mine, self.round_land = where, msg, land, mine, round_land
        self.first_sends, self.first_recvs = first_sends, first_recvs
        self.sends, self.recvs = sends, recvs

    def first(self, n, offset, arriving=False):
        me = shard_at(self.where)
        source = shard_at(self.where, negative(offset)) if arriving else me
        return remote(
            self.msg.at[shard_at(self.where, offset)],
            self.land.at[source],
            self.first_sends,
            self.first_recvs,
            n,
            device(self.where, offset),
        )

    def begin(self):
        me = shard_at(self.where)
        for n, offset in enumerate(PEERS):
            self.first(n, offset).start()
        self.land[me] = self.msg[me]

    def middle(self):
        me = shard_at(self.where)
        for n, offset in enumerate(PEERS):
            self.first(n, offset, True).wait_recv()
        total = self.land[0]
        for source in range(1, GROUP):
            total = total + self.land[source]
        self.mine[0] = total
        for p in range(3):
            block = 3 * me + p
            self.mine[0, 4 + p : 5 + p, :] = self.land[lax.rem(block, GROUP), pl.ds(4 + block // GROUP, 1), :]

    def hop(self, n, i, step):
        return remote(self.mine.at[n], self.round_land.at[i], self.sends, self.recvs, i, device(self.where, step))

    def round(self, n):
        base = sum(len(r) for r in self.ROUNDS[:n])
        for i, step in enumerate(self.ROUNDS[n]):
            self.hop(n, base + i, step).start()
        total = self.mine[n]
        for i, step in enumerate(self.ROUNDS[n]):
            self.hop(n, base + i, step).wait_recv()
            total = total + self.round_land[base + i]
        self.mine[n + 1] = total

    def finish(self):
        for n, offset in enumerate(PEERS):
            self.first(n, offset).wait_send()
        for n, steps in enumerate(self.ROUNDS):
            base = sum(len(r) for r in self.ROUNDS[:n])
            for i, step in enumerate(steps):
                self.hop(n, base + i, step).wait_send()


VECTOR_SCRATCH = [
    pltpu.VMEM((GROUP, 8, LOCAL), F32),
    pltpu.VMEM((GROUP, 8, LOCAL), F32),
    pltpu.VMEM((4, 8, LOCAL), F32),
    pltpu.VMEM((5, 8, LOCAL), F32),
    DMA((7,)),
    DMA((7,)),
    DMA((5,)),
    DMA((5,)),
]


def params(cid=None, mib=56):
    if cid is None:
        return pltpu.CompilerParams(vmem_limit_bytes=mib * 2**20)
    return pltpu.CompilerParams(
        collective_id=cid, has_side_effects=True, vmem_limit_bytes=mib * 2**20
    )


class Copies:
    def __init__(self, sems):
        self.sems, self.flying = sems, {}

    def start(self, name, src, dst):
        copy = pltpu.make_async_copy(src, dst, self.sems.at[len(self.flying)])
        copy.start()
        self.flying[name] = [copy, False]

    def wait(self, *names):
        for name in names:
            entry = self.flying[name]
            if not entry[1]:
                entry[0].wait()
                entry[1] = True

    def finish(self):
        self.wait(*self.flying)


def front_kernel(
    x_ref, small_ref, table_ref, ow_ref, qkv_ref, gate_ref, up_ref, gy_ref,
    all_small, mid_ref, a1_out, a2_out, gy_out, wqkv_out, wgu_out, q_out, k_out, v_out, att_out, lse_out,
    a1, w_qkv, own_two, q, k, v, att, lse, vt, mixed, buf, land, local_sems, *sems,
):
    where = place()
    greet(where, PEERS + REP_NEIGHBOURS)
    me, rep = shard_at(where), rep_at(where)
    local = Copies(local_sems)

    def small(n, offset, arriving=False):
        owner = shard_at(where, negative(offset)) if arriving else me
        return remote(small_ref, all_small.at[owner], sems[0], sems[1], n, device(where, offset))

    for n, offset in enumerate(PEERS):
        small(n, offset).start()
    all_small[me] = small_ref[...]
    spread_qkv = Spread(where, qkv_cuts(qkv_ref, rep), w_qkv, *sems[2:7])
    spread_gu = Spread(where, gate_up_cuts(gate_ref, up_ref, rep), wgu_out, *sems[7:12])
    one = Gather(where, a1, *sems[12:14])
    two = Gather(where, a2_out, *sems[14:16], own=own_two)
    grads = Gather(where, gy_out, *sems[16:18], own=gy_ref)
    scatter = Scatter(where, buf, land, *sems[18:20])
    spread_qkv.begin()
    scaled, _ = standardize(x_ref[...].astype(F32))
    for n, offset in enumerate(PEERS):
        small(n, offset, True).wait_recv()
    a1[me] = (scaled * small_row(all_small, 0) + small_row(all_small, 1)).astype(BF)
    plan = Agenda()
    plan.add(agenda(one, 0))
    plan.until(1.0)
    spread_gu.begin()
    local.start("gy", gy_ref.at[0], gy_out.at[me])
    spread_qkv.middle()
    plan.add(slab_agenda(spread_qkv, 4, 4))
    plan.until(19)
    spread_gu.middle()
    plan.add(slab_agenda(spread_gu, 22, 8))
    plan.until(25)
    one.take_all()
    plan.add(agenda(grads, 26))
    plan.until(37)
    spread_qkv.slabs.take_all()
    local.start("a1", a1, a1_out)
    local.start("w_qkv", w_qkv, wqkv_out)
    for half in range(2):
        project(me, a1, w_qkv, all_small, table_ref, q, k, v, 2 * half, 2 * half + 2)
        plan.until(40 + 3 * half)
    attend(q, k, v, vt, mixed, att, lse, lambda i: plan.until(44 + 2 * i))
    for name, src, dst in (("q", q, q_out), ("k", k, k_out), ("v", v, v_out), ("att", att, att_out), ("lse", lse, lse_out)):
        local.start(name, src, dst)
    times(att, ow_ref, buf)
    plan.until(52)
    plan.add(agenda(scatter, 53))
    plan.until(80)
    scatter.take_all()
    mid = x_ref[...].astype(F32) + buf[me].astype(F32)
    mid_ref[...] = mid
    normed, _, _ = normalize(mid, small_row(all_small, 2), small_row(all_small, 3))
    own_two[0] = normed.astype(BF)
    plan.add(agenda(two, 80))
    plan.until(81)
    local.start("own_two", own_two.at[0], a2_out.at[me])
    plan.until(1000)
    spread_qkv.finish(True)
    for mover in (one, two, grads, scatter, spread_gu):
        mover.finish()
    for n, offset in enumerate(PEERS):
        small(n, offset).wait_send()
    local.finish()


def front(x, small, table, out_weight, qkv_weight, gate_weight, up_weight, gy):
    sds = jax.ShapeDtypeStruct
    tokens = sds((GROUP, ROWS, WIDTH), BF)
    head = sds((TOTAL, LOCAL), BF)
    token_sems = [DMA((COUNT,))] * 2
    return pl.pallas_call(
        front_kernel,
        out_shape=(
            sds((GROUP, 8, LOCAL), F32),
            sds((ROWS, WIDTH), F32),
            tokens,
            tokens,
            tokens,
            sds((GROUP, 8, 2, SLAB, 3 * LOCAL), BF),
            sds((GROUP, 8, 2, SLAB, 2 * HID), BF),
            head,
            head,
            head,
            head,
            sds((8, TOTAL), F32),
        ),
        in_specs=[VM] * 4 + [ANY] * 3 + [VM],
        out_specs=(VM, VM) + (ANY,) * 10,
        scratch_shapes=[
            pltpu.VMEM((GROUP, ROWS, WIDTH), BF),
            pltpu.VMEM((GROUP, 8, 2, SLAB, 3 * LOCAL), BF),
            pltpu.VMEM((1, ROWS, WIDTH), BF),
            *[pltpu.VMEM((TOTAL, LOCAL), BF)] * 4,
            pltpu.VMEM((8, TOTAL), F32),
            pltpu.VMEM((LOCAL, TOTAL), BF),
            pltpu.VMEM((LOCAL, TOTAL), F32),
            pltpu.VMEM((GROUP, ROWS, WIDTH), BF),
            pltpu.VMEM((LANDINGS, ROWS, FAR_COLS), BF),
            DMA((9,)),
            DMA((7,)),
            DMA((7,)),
        ]
        + spread_scratch(3)
        + spread_scratch(2)
        + token_sems * 4,
        compiler_params=params(0),
        name="front",
    )(x, small, table, out_weight, qkv_weight, gate_weight, up_weight, gy)


def middle_kernel(
    mid_ref, gy_own, small_ref, a2_in, gy_in, wgu_in, down_in,
    dmid_ref, sums_ref, dy_out, sgu_out, sdown_out, part_out,
    a2, gy, w, down, hid, dgu, buf, land, own, part, ggu, gdown, one_0, one_1, two_0, two_1, down_0, down_1, load_sems, local_sems, *sems,
):
    where = place()
    me, rep = shard_at(where), rep_at(where)
    odd = lax.rem(me, 2)
    loads = Copies(load_sems)

    def tile(j):
        for side in range(2):
            cols = pl.ds(side * HID + j * CHUNK, CHUNK)
            loads.start(("w", j, side), wgu_in.at[:, :, :, :, cols], w.at[:, :, :, :, cols])

    loads.start("a2", a2_in, a2)
    tile(0)
    loads.start("down", down_in, down.at[pl.ds(pl.multiple_of(64 * odd, 64), LOCAL_FF)])
    loads.start("gy", gy_in, gy)
    tile(1)
    tile(2)
    greet(where, NEIGHBOURS + REP_NEIGHBOURS)
    down[pl.ds(pl.multiple_of(LOCAL_FF * (1 - odd), 64), 64), :] = jnp.zeros((64, WIDTH), BF)
    loads.wait("a2", ("w", 0, 0), ("w", 0, 1), "down", "gy")
    for j in range(HID // CHUNK):
        if j:
            loads.wait(("w", j, 0), ("w", j, 1))
        feed_forward(me, a2, gy, w, down, hid, dgu, j)
    times_back(dgu, w, buf)
    scatter = Scatter(where, buf, land, *sems[0:2])
    gather = Gather(where, dy_out, *sems[2:4], own=own)
    local = Copies(local_sems)
    half = GROUP // 2
    sum_gu = [
        RingScatter(where, ggu.at[pl.ds(0, half)], one_0, one_1, *sems[4:6]),
        RingScatter(where, ggu.at[pl.ds(half, half)], two_0, two_1, *sems[8:10]),
    ]
    sum_down = RingScatter(where, gdown, down_0, down_1, *sems[6:8])
    plan = Agenda()
    plan.add(agenda(scatter, 0))
    plan.until(0.9)
    time = 0
    for m in range(GROUP):
        outer(a2, dgu, ggu, m, m + 1)
        time += 1.4
        plan.until(time)
        if m == half - 1:
            plan.add([(6, sum_gu[0], 0), (10.5, sum_gu[0], 1), (15, sum_gu[0], 2), (20, sum_gu[0], 3), (25, sum_gu[0], 4)])
    plan.add([(11.3, sum_gu[1], 0), (15.5, sum_gu[1], 1), (23, sum_gu[1], 2), (29, sum_gu[1], 3), (36, sum_gu[1], 4)])
    plan.until(time)
    for m in range(3):
        outer(hid, gy, gdown, m, m + 1)
        time += 2
        plan.until(time)
    plan.add([(17.5, sum_down, 0), (22, sum_down, 1), (33.5, sum_down, 2), (37, sum_down, 3), (42, sum_down, 4)])
    plan.until(30)
    scatter.take_all()
    gain = small_row(small_ref, 2)
    _, scaled, inverse = normalize(mid_ref[...], gain, small_row(small_ref, 3))
    grad = buf[me].astype(F32)
    dmid = gy_own[0].astype(F32) + normalize_back(grad, gain, scaled, inverse)
    own[0] = dmid.astype(BF)
    plan.add(agenda(gather, 32))
    plan.until(33)
    local.start("own", own.at[0], dy_out.at[me])
    dmid_ref[...] = dmid
    sums_ref[0:1, :] = jnp.sum(grad * scaled, 0, keepdims=True)
    sums_ref[1:2, :] = jnp.sum(grad, 0, keepdims=True)
    plan.until(37)
    for n in range(CHUNKS):
        times(hid, down, part, n, n + 1)
        plan.until(39 + 2 * n)
    local.start("part", part, part_out)
    plan.until(50)
    for n in range(2):
        sum_gu[n].close()
        local.start(("gu", n), sum_gu[n].total(), sgu_out.at[pl.ds(half * n, half)])
    plan.until(1000)
    sum_down.close()
    local.start("down", sum_down.total(), sdown_out)
    gather.take_all()
    for mover in (*sum_gu, sum_down, gather, scatter, local):
        mover.finish()


def middle(mid, gy, small, a2, grads, w_gu, down_weight):
    sds = jax.ShapeDtypeStruct
    tokens = (GROUP, ROWS, WIDTH)
    return pl.pallas_call(
        middle_kernel,
        out_shape=(
            sds((ROWS, WIDTH), F32),
            sds((8, WIDTH), F32),
            sds(tokens, BF),
            sds((GROUP, SLAB, 2 * HID), BF),
            sds((3, SLAB, WIDTH), BF),
            sds(tokens, BF),
        ),
        in_specs=[VM] * 3 + [ANY] * 4,
        out_specs=(VM, VM) + (ANY,) * 4,
        scratch_shapes=[
            pltpu.VMEM(tokens, BF),
            pltpu.VMEM(tokens, BF),
            pltpu.VMEM((GROUP, 8, 2, SLAB, 2 * HID), BF),
            pltpu.VMEM((HID, WIDTH), BF),
            pltpu.VMEM((TOTAL, HID), BF),
            pltpu.VMEM((TOTAL, 2 * HID), BF),
            pltpu.VMEM(tokens, BF),
            pltpu.VMEM((LANDINGS, ROWS, FAR_COLS), BF),
            pltpu.VMEM((1, ROWS, WIDTH), BF),
            pltpu.VMEM(tokens, BF),
            pltpu.VMEM((GROUP, 8, 2, SLAB, 2 * HID), BF),
            pltpu.VMEM((3, 8, 2, SLAB, WIDTH), BF),
            *ring_scratch(GROUP // 2, 2 * HID),
            *ring_scratch(GROUP // 2, 2 * HID),
            *ring_scratch(3, WIDTH),
            DMA((9,)),
            DMA((5,)),
        ]
        + [DMA((COUNT,))] * 4
        + [DMA((SLAB_COUNT,))] * 6,
        compiler_params=params(1, 62),
        name="middle",
    )(mid, gy, small, a2, grads, w_gu, down_weight)


QKV_SPAN = (GROUP, 8, 2, SLAB, 3 * LOCAL)
HALF = 3 * LOCAL // 2
HALF_SPAN = (GROUP, 8, 2, SLAB, HALF)
GU_SPAN = (GROUP, 8, 2, SLAB, 2 * HID)
DOWN_SPAN = (3, 8, 2, SLAB, WIDTH)
OUT_SPAN = (4, 8, 2, SLAB, 512)


def back_kernel(
    x_ref, mid_ref, dmid_ref, small_ref, two_ref, table_ref, ow_ref,
    dy_in, a1_in, wqkv_in, q_in, k_in, v_in, att_in, lse_in, sgu_in, sdown_in, part_in,
    grad_ref, act_ref, vec_ref, gu_out, down_out, qkv_out, kv_out, out_out,
    toks, a1, w, q, k, v, att, lse, da, kt, dqt, dk, dv, dqkv, buf, land, buf_down, land_down,
    gqkv, gkv, gout, qkv_0, qkv_1, kv_0, kv_1, out_0, out_1, load_sems, own_sems, *sems,
):
    where = place()
    me, rep = shard_at(where), rep_at(where)
    loads = Copies(load_sems)
    for name, src, dst in (
        ("toks", dy_in, toks), ("q", q_in, q), ("k", k_in, k),
        ("v", v_in, v), ("lse", lse_in, lse), ("att", att_in, att), ("w", wqkv_in, w),
        ("down", sdown_in, down_out.at[:, spot(where), where[4]]), ("a1", a1_in, a1),
        ("part", part_in, buf_down),
    ):
        loads.start(name, src, dst)
    greet(where, PEERS + REP_NEIGHBOURS)
    down = Scatter(where, buf_down, land_down, *sems[0:2])
    one = Scatter(where, buf, land, *sems[2:4])
    sum_qkv = [
        SlabScatter(where, gqkv, qkv_0, qkv_1, *sems[4:6]),
        SlabScatter(where, gkv, kv_0, kv_1, *sems[28:30]),
    ]
    sum_out = SlabScatter(where, gout, out_0, out_1, *sems[6:8])
    back_gu = Return(where, lambda s: sgu_in.at[s], gu_out, RingGather, own_sems.at[0], *sems[8:12])
    back_qkv = [
        Return(
            where, lambda s: gqkv.at[s, spot(where), where[4]], qkv_out, SlabGather, own_sems.at[1], *sems[12:16]
        ),
        Return(
            where, lambda s: gkv.at[s, spot(where), where[4]], kv_out, SlabGather, own_sems.at[3], *sems[30:34]
        ),
    ]
    back_down = RingGather(where, down_out, *sems[16:18])
    back_out = SlabGather(where, out_out, *sems[18:20])
    vectors = Vectors(where, *sems[20:28])
    plan = Agenda()
    back_gu.begin()
    loads.wait("down")
    plan.add(slab_agenda(back_down, 1.5, 5))
    plan.until(1.5)
    loads.wait("toks")

    @pl.loop(0, CHUNKS, unroll=4)
    def _(i):
        da[chunk_rows(i), :] = dot_nt(token_chunk(toks, i), ow_ref[...]).astype(BF)

    loads.wait("q", "k", "v", "lse")

    def poll(i):
        if i == 0:
            back_gu.middle()
            plan.add(slab_agenda(back_gu, 6, 9))
        plan.until((6.5, 9, 12.5, 17)[i])

    attend_back(q, k, v, da, lse, kt, dqt, dk, dv, poll)
    vectors.msg[...] = jnp.zeros_like(vectors.msg)
    for i in range(CHUNKS):
        rows = slice(i * CHUNK, (i + 1) * CHUNK)
        grad_q = dqt[:, rows].T * HEAD_DIM ** (-0.5)
        for j, value in enumerate((grad_q, dk[rows, :], dv[rows, :])):
            if j < 2:
                value = turned(value, table_ref, rows, -1)
            low = value.astype(BF)
            dqkv[rows, j * LOCAL : (j + 1) * LOCAL] = low
            vectors.msg[0, 4 + j : 5 + j, :] += jnp.sum(low.astype(F32), 0, keepdims=True)
    loads.wait("w")
    times_back(dqkv, w, buf)
    plan.add(agenda(one, 20))
    plan.until(20.9)
    loads.wait("a1")
    for m in range(4):
        outer(a1, dqkv.at[:, pl.ds(0, HALF)], gqkv, 2 * m, 2 * m + 2)
        plan.until(22 + 1.3 * m)
    sum_qkv[0].turn(0)
    for m in range(4):
        outer(a1, dqkv.at[:, pl.ds(HALF, HALF)], gkv, 2 * m, 2 * m + 2)
        plan.until(27.3 + 1.3 * m)
    sum_qkv[1].turn(0)
    sum_qkv[0].turn(1)
    plan.until(33)
    loads.wait("att")
    left = att[...].astype(F32).T.astype(BF)
    for n in range(4):
        right = toks[:, :, n * 512 : (n + 1) * 512].reshape(TOTAL, 512)
        gout[n] = dot(left, right).astype(BF).reshape(8, 2, SLAB, 512)
    sum_out.turn(0)
    sum_qkv[1].turn(1)
    plan.until(36)
    sum_out.turn(1)
    back_down.finish()
    plan.until(40)
    sum_qkv[0].turn(2)
    back_gu.finish()
    sum_qkv[0].close()
    back_qkv[0].begin()
    sum_qkv[1].turn(2)
    plan.until(1000)
    one.take_all()
    loads.wait("part")
    plan.add(agenda(down, 50))
    plan.until(50.9)
    gain = small_row(small_ref, 0)
    _, scaled, inverse = normalize(x_ref[...].astype(F32), gain, small_row(small_ref, 1))
    grad = buf[me].astype(F32)
    first, second = jnp.sum(grad * scaled, 0, keepdims=True), jnp.sum(grad, 0, keepdims=True)
    for d in range(GROUP):
        cols = slice(d * LOCAL, (d + 1) * LOCAL)
        vectors.msg[d, 0:1, :] = first[:, cols]
        vectors.msg[d, 1:2, :] = second[:, cols]
        vectors.msg[d, 2:4, :] = two_ref[0:2, cols]
        if d:
            vectors.msg[d, 4:7, :] = vectors.msg[0, 4:7, :]
    vectors.begin()
    grad_ref[...] = dmid_ref[...] + normalize_back(grad, gain, scaled, inverse)
    sum_qkv[1].close()
    back_qkv[1].begin()
    back_qkv[0].middle()
    back_qkv[0].turn(0)
    plan.until(56)
    vectors.middle()
    back_qkv[0].turn(1)
    plan.until(57)
    back_qkv[1].middle()
    back_qkv[1].turn(0)
    vectors.round(0)
    plan.until(59)
    sum_out.turn(2)
    back_qkv[1].turn(1)
    vectors.round(1)
    one.settle()
    sum_qkv[0].finish()
    sum_out.close()
    out_own = pltpu.make_async_copy(
        sum_out.total(), out_out.at[:, spot(where), where[4]], own_sems.at[2]
    )
    out_own.start()
    vectors.round(2)
    vec_ref[...] = vectors.mine[3]
    plan.until(65)
    out_own.wait()
    back_out.turn(0)
    sum_qkv[1].finish()
    plan.until(1000)
    back_qkv[0].turn(2)
    back_out.turn(1)
    sum_out.finish()
    vectors.finish()
    loads.finish()
    back_qkv[1].turn(2)
    down.take_all()
    act_ref[...] = (mid_ref[...] + buf_down[me].astype(F32)).astype(BF)
    back_out.turn(2)
    for mover in (down, *back_qkv, back_out):
        mover.finish()


def back(x, mid, dmid, small, sums_two, table, out_weight, dy, a1, w_qkv, q, k, v, att, lse, s_gu, s_down, part_down):
    sds = jax.ShapeDtypeStruct
    tokens = (GROUP, ROWS, WIDTH)
    slab_sems = [DMA((SLAB_COUNT,))] * 2
    return pl.pallas_call(
        back_kernel,
        out_shape=(
            sds((ROWS, WIDTH), F32),
            sds((ROWS, WIDTH), BF),
            sds((8, LOCAL), F32),
            *[sds(s, BF) for s in (GU_SPAN, DOWN_SPAN, HALF_SPAN, HALF_SPAN, OUT_SPAN)],
        ),
        in_specs=[VM] * 7 + [ANY] * 11,
        out_specs=(VM,) * 3 + (ANY,) * 5,
        scratch_shapes=[
            pltpu.VMEM(tokens, BF),
            pltpu.VMEM(tokens, BF),
            pltpu.VMEM(QKV_SPAN, BF),
            *[pltpu.VMEM((TOTAL, LOCAL), BF)] * 4,
            pltpu.VMEM((8, TOTAL), F32),
            pltpu.VMEM((TOTAL, LOCAL), BF),
            pltpu.VMEM((LOCAL, TOTAL), BF),
            pltpu.VMEM((LOCAL, TOTAL), F32),
            pltpu.VMEM((TOTAL, LOCAL), F32),
            pltpu.VMEM((TOTAL, LOCAL), F32),
            pltpu.VMEM((TOTAL, 3 * LOCAL), BF),
            pltpu.VMEM(tokens, BF),
            pltpu.VMEM((LANDINGS, ROWS, FAR_COLS), BF),
            pltpu.VMEM(tokens, BF),
            pltpu.VMEM((LANDINGS, ROWS, FAR_COLS), BF),
            pltpu.VMEM(HALF_SPAN, BF),
            pltpu.VMEM(HALF_SPAN, BF),
            pltpu.VMEM(OUT_SPAN, BF),
            *scatter_scratch(GROUP, HALF),
            *scatter_scratch(GROUP, HALF),
            *scatter_scratch(4, 512),
            DMA((10,)),
            DMA((4,)),
        ]
        + [DMA((COUNT,))] * 4
        + slab_sems * 2
        + ([DMA((7,))] * 2 + slab_sems) * 2
        + slab_sems * 2
        + VECTOR_SCRATCH
        + slab_sems
        + [DMA((7,))] * 2
        + slab_sems,
        compiler_params=params(2, 60),
        name="back",
    )(x, mid, dmid, small, sums_two, table, out_weight, dy, a1, w_qkv, q, k, v, att, lse, s_gu, s_down, part_down)


def unpack_kernel(odd_ref, gu_ref, qkv_ref, kv_ref, out_ref, down_ref, gate_out, up_out, qkv_out, out_out, down_out):
    for side, ref in enumerate((gate_out, up_out)):
        cols = slice(side * HID, (side + 1) * HID)
        for t in range(GROUP // 2):
            left, right = gu_ref[2 * t, :, cols].astype(F32), gu_ref[2 * t + 1, :, cols].astype(F32)
            ref[:, t * 2 * LOCAL_FF : (t + 1) * 2 * LOCAL_FF] = jnp.concatenate(
                [left[:, :640], left[:, 640:] + right[:, :128], right[:, 128:]], axis=1
            )
    for s in range(GROUP):
        for j in range(3):
            for part in range(2):
                cols = j * LOCAL + part * 128
                ref, at = (qkv_ref, cols) if cols < HALF else (kv_ref, cols - HALF)
                first = j * WIDTH + s * LOCAL + part * 128
                qkv_out[:, first : first + 128] = ref[s, :, at : at + 128].astype(F32)
    for n in range(4):
        out_out[:, n * 512 : (n + 1) * 512] = out_ref[n].astype(F32)
    rows = LOCAL_FF // 4
    first = pl.multiple_of(64 * odd_ref[0] + rows * pl.program_id(0), SLAB)
    down_out[...] = down_ref[pl.ds(first, rows), :].astype(F32)


def unpack(odd, g_gu, g_qkv, g_kv, g_out, g_down):
    sds = jax.ShapeDtypeStruct
    rows = LOCAL // 4
    return pl.pallas_call(
        unpack_kernel,
        grid_spec=pltpu.PrefetchScalarGridSpec(
            num_scalar_prefetch=1,
            grid=(4,),
            in_specs=[
                pl.BlockSpec((GROUP, rows, 2 * HID), lambda r, _: (0, r, 0)),
                *[pl.BlockSpec((GROUP, rows, HALF), lambda r, _: (0, r, 0))] * 2,
                pl.BlockSpec((4, rows, 512), lambda r, _: (0, r, 0)),
                pl.BlockSpec((HID, WIDTH), lambda r, _: (0, 0)),
            ],
            out_specs=[
                pl.BlockSpec((rows, FF), lambda r, _: (r, 0)),
                pl.BlockSpec((rows, FF), lambda r, _: (r, 0)),
                pl.BlockSpec((rows, 3 * WIDTH), lambda r, _: (r, 0)),
                pl.BlockSpec((rows, WIDTH), lambda r, _: (r, 0)),
                pl.BlockSpec((LOCAL_FF // 4, WIDTH), lambda r, _: (r, 0)),
            ],
        ),
        out_shape=(
            sds((LOCAL, FF), F32),
            sds((LOCAL, FF), F32),
            sds((LOCAL, 3 * WIDTH), F32),
            sds((LOCAL, WIDTH), F32),
            sds((LOCAL_FF, WIDTH), F32),
        ),
        compiler_params=params(),
        name="unpack",
    )(odd.reshape(1), g_gu, g_qkv, g_kv, g_out, g_down)


def shards(
    inputs,
    cotangent,
    ln1_gain,
    ln1_bias,
    qkv_weight,
    qkv_bias,
    out_weight,
    ln2_gain,
    ln2_bias,
    gate_weight,
    up_weight,
    down_weight,
):
    batch, length, width = inputs.shape
    odd = lax.rem(lax.axis_index("shard"), 2)
    table = jnp.asarray(rotary_tables())
    x = inputs.reshape(length, width)
    small, at = jnp.zeros((8 * LOCAL,), F32), 0
    for vector in (ln1_gain, ln1_bias, ln2_gain, ln2_bias, qkv_bias):
        small += jnp.pad(vector.astype(F32), (at, 8 * LOCAL - at - vector.shape[0]))
        at += vector.shape[0]
    small = small.reshape(8, LOCAL)
    all_small, mid, a1, a2, grads, w_qkv, w_gu, q, k, v, att, lse = front(
        x, small, table, out_weight, qkv_weight, gate_weight, up_weight, cotangent
    )
    dmid, sums_two, dy, s_gu, s_down, part_down = middle(
        mid, cotangent, all_small, a2, grads, w_gu, down_weight
    )
    input_grad, activations, vectors, g_gu, g_down, g_qkv, g_kv, g_out = back(
        x, mid, dmid, all_small, sums_two, table, out_weight, dy, a1, w_qkv, q, k, v, att, lse, s_gu, s_down, part_down
    )
    g_gate, g_up, g_qkv, g_out, g_down = unpack(
        odd,
        g_gu.reshape(GROUP, LOCAL, 2 * HID),
        g_qkv.reshape(GROUP, LOCAL, HALF),
        g_kv.reshape(GROUP, LOCAL, HALF),
        g_out.reshape(4, LOCAL, 512),
        g_down.reshape(HID, width),
    )
    return (
        activations.reshape(batch, length, width),
        input_grad.reshape(batch, length, width),
        vectors[0],
        vectors[1],
        g_qkv,
        vectors[4:7].reshape(3 * LOCAL),
        g_out,
        vectors[2],
        vectors[3],
        g_gate,
        g_up,
        g_down,
    )


def solution(mesh):
    tokens, vector, matrix = P("rep", "shard", None), P("shard"), P("shard", None)
    return jax.shard_map(
        shards,
        mesh=mesh,
        in_specs=(tokens, tokens, vector, vector, matrix, vector, matrix, vector, vector, matrix, matrix, matrix),
        out_specs=(tokens, tokens, vector, vector, matrix, vector, matrix, vector, vector, matrix, matrix, matrix),
        check_vma=False,
    )
```
